32 devices in a mesh: dp: 8 (over y, x, core), tp: 4 (over z).
Axes of the slice: x: 2, y: 2, z: 4, core: 2. Of those that a mesh axis runs over, the one named last changes fastest.
Arguments:
- patches: bfloat16 [8192, 8192], P('dp', 'tp'), may hold values from -6 to 6
- keep_mask: int32 [8192], P(('dp', 'tp')), may hold values 0 or 1
- segments: int32 [8, 1024], P('dp'), may hold values from 0 to 3, as said below
- embed_weight: bfloat16 [8192, 1024], P('tp'), may hold values from -0.0625 to 0.0625
- first_gain: float32 [1024], replicated, may hold values from 0.1 to 1.9
- mamba_gate: bfloat16 [1024, 2048], P(None, 'tp'), may hold values from -0.1875 to 0.1875
- mamba_input: bfloat16 [1024, 2048], P(None, 'tp'), may hold values from -0.1875 to 0.1875
- state_in: bfloat16 [1024, 512], P(None, 'tp'), may hold values from -0.1875 to 0.1875
- state_out: bfloat16 [1024, 512], P(None, 'tp'), may hold values from -0.1875 to 0.1875
- step_weight: bfloat16 [1024, 32], P(None, 'tp'), may hold values from -0.1875 to 0.1875
- conv_input: float32 [4, 2048], P(None, 'tp'), may hold values from -3 to 3
- conv_statein: float32 [4, 512], P(None, 'tp'), may hold values from -3 to 3
- conv_stateout: float32 [4, 512], P(None, 'tp'), may hold values from -3 to 3
- step_bias: float32 [32], P('tp'), may hold values from -4 to -1
- rate_log: float32 [32], P('tp'), may hold values from -6 to 0
- skip_gain: float32 [32], P('tp'), may hold values from 0.5 to 1.5
- inner_gain: float32 [2048], P('tp'), may hold values from 0.1 to 1.9
- mamba_output: bfloat16 [2048, 1024], P('tp'), may hold values from -0.125 to 0.125
- query_weight: bfloat16 [1024, 1024], P(None, 'tp'), may hold values from -0.1875 to 0.1875
- key_weight: bfloat16 [1024, 1024], P(None, 'tp'), may hold values from -0.1875 to 0.1875
- value_weight: bfloat16 [1024, 1024], P(None, 'tp'), may hold values from -0.1875 to 0.1875
- attn_output: bfloat16 [1024, 1024], P('tp'), may hold values from -0.5 to 0.5
- second_gain: float32 [1024], replicated, may hold values from 0.1 to 1.9
- ffn_gate: bfloat16 [1024, 4096], P(None, 'tp'), may hold values from -0.1875 to 0.1875
- ffn_up: bfloat16 [1024, 4096], P(None, 'tp'), may hold values from -0.1875 to 0.1875
- ffn_down: bfloat16 [4096, 1024], P('tp'), may hold values from -0.09375 to 0.09375
- out_grad: bfloat16 [8192, 1024], P(('dp', 'tp')), may hold values from -6 to 6
Outputs:
- out: bfloat16 [8192, 1024], P(('dp', 'tp'))
- patches_grad: bfloat16 [8192, 8192], P('dp', 'tp')
- embed_weight_grad: float32 [8192, 1024], P('tp', 'dp')
- first_gain_grad: float32 [1024], P(('dp', 'tp'))
- mamba_gate_grad: float32 [1024, 2048], P('dp', 'tp')
- mamba_input_grad: float32 [1024, 2048], P('dp', 'tp')
- state_in_grad: float32 [1024, 512], P('dp', 'tp')
- state_out_grad: float32 [1024, 512], P('dp', 'tp')
- step_weight_grad: float32 [1024, 32], P('dp', 'tp')
- conv_input_grad: float32 [4, 2048], P(None, 'tp')
- conv_statein_grad: float32 [4, 512], P(None, 'tp')
- conv_stateout_grad: float32 [4, 512], P(None, 'tp')
- step_bias_grad: float32 [32], P('tp')
- rate_log_grad: float32 [32], P('tp')
- skip_gain_grad: float32 [32], P('tp')
- inner_gain_grad: float32 [2048], P('tp')
- mamba_output_grad: float32 [2048, 1024], P('tp', 'dp')
- query_weight_grad: float32 [1024, 1024], P('dp', 'tp')
- key_weight_grad: float32 [1024, 1024], P('dp', 'tp')
- value_weight_grad: float32 [1024, 1024], P('dp', 'tp')
- attn_output_grad: float32 [1024, 1024], P('tp', 'dp')
- second_gain_grad: float32 [1024], P(('dp', 'tp'))
- ffn_gate_grad: float32 [1024, 4096], P('dp', 'tp')
- ffn_up_grad: float32 [1024, 4096], P('dp', 'tp')
- ffn_down_grad: float32 [4096, 1024], P('tp', 'dp')
The draws below stay inside these ranges and needn't reach their ends.
Inputs may be any that keep to these rules, and one draw needn't show every extreme that they name: `segments`: along each row the document numbers never fall and rise by one at a time; each row holds documents 0 to 3.
All inputs are finite; a program needn't handle non-finite values. No bound on the sum of `keep_mask` on one device may be relied on, other than what follows from the above.
Results may differ from the reference program's by a relative error of at most 0.0208.
Values may be sent and summed in bfloat16 or wider, within the bound.
A program may use at most 256 MiB of HBM per device.

```python
import jax
import jax.numpy as jnp
from jax import lax

D = 1024
HEADS = 32
NST = 128
G = 4
KCONV = 4
AHDIM = 64
FF = 4096
PD = 8192
INNER = 2048
ATT = 1024
SEQ = 1024
SEQS = 8
TOKENS = 8192


def draw_segments(key, part):
    key = jax.random.fold_in(key, 11)
    subkeys = jax.random.split(key, 3)
    first_cut = jax.random.randint(subkeys[0], (SEQS, 1), 1, SEQ // 16 + 1)
    second_cut = jax.random.randint(subkeys[1], (SEQS, 1), SEQ // 16 + 1, SEQ // 8 + 1)
    third_cut = jax.random.randint(subkeys[2], (SEQS, 1), SEQ - SEQ // 8, SEQ)
    positions = jnp.arange(SEQ, dtype=jnp.int32)[None, :]
    return (positions >= first_cut).astype(jnp.int32) + (positions >= second_cut).astype(jnp.int32) + (positions >= third_cut).astype(jnp.int32)


def set_ends(entries, stream_key, least, high):
    longest = entries.shape.index(max(entries.shape))
    spots = []
    for shift in (0, 1):
        where = [jax.random.randint(jax.random.fold_in(stream_key, axis), (), 0, length) for axis, length in enumerate(entries.shape)]
        where[longest] = (where[longest] + shift) % entries.shape[longest]
        spots.append(tuple(where))
    return entries.at[spots[0]].set(least).at[spots[1]].set(high)


def with_spikes(array, stream_key, source, target, shards_of, factor):
    owner, partner = [(jnp.arange(array.shape[dim]) // (array.shape[dim] // shards_of)).reshape([-1 if axis == dim else 1 for axis in range(array.ndim)]) for dim in (source, target)]
    chosen = jax.random.permutation(stream_key, shards_of)[partner]
    strong = (owner == chosen) | (owner == (partner + shards_of // 2) % shards_of)
    return jnp.where(strong, factor * array, array)


def steps_of(own_key, dims, shards, low, largest):
    loudness, own = 1.0, jax.random.fold_in(own_key, 6)
    for dim, parts in shards:
        heights = jnp.exp(jax.random.uniform(jax.random.fold_in(own, dim), (parts,), jnp.float32, low / len(shards), largest / len(shards)))
        loudness = loudness * jnp.repeat(heights, dims[dim] // parts).reshape([-1 if axis == dim else 1 for axis in range(len(dims))])
    return loudness


def scatter_about(key, dims, deviation, limit, pieces=(), kind=jnp.bfloat16):
    values = deviation * jax.random.normal(key, dims, jnp.float32)
    if pieces:
        values = values * steps_of(key, dims, pieces, -0.22, 0.18)
    return jnp.clip(values, -limit, limit).astype(kind)


def heavy_noise(own_key, extent, scale, bound, cuts, heavy, kind=jnp.bfloat16):
    values = scale * jax.random.normal(own_key, extent, jnp.float32)
    if cuts:
        values = values * steps_of(own_key, extent, cuts, -0.22, 0.18)
    return jnp.clip(with_spikes(values, jax.random.fold_in(own_key, 3), *heavy), -bound, bound).astype(kind)


def setup_inputs(seed: int = 0) -> dict:
    key_list = jax.random.split(jax.random.key(seed), 28)
    return {
        "patches": scatter_about(key_list[0], (TOKENS, PD), 1.0, 6.0, ((0, 8), (1, 4))),
        "keep_mask": set_ends((jax.random.randint(key_list[1], (TOKENS,), 0, 8) < 7).astype(jnp.int32), jax.random.fold_in(key_list[1], 1), 0, 1),
        "segments": draw_segments(jax.random.fold_in(key_list[27], 71), 0),
        "embed_weight": scatter_about(key_list[3], (PD, D), PD ** -0.5, 0.0625, ((0, 4),)),
        "first_gain": jnp.clip(1.0 + 0.18 * jax.random.normal(key_list[4], (D,), jnp.float32), 0.1, 1.9),
        "mamba_gate": scatter_about(key_list[5], (D, INNER), D ** -0.5, 0.1875, ((1, 4),)),
        "mamba_input": scatter_about(key_list[6], (D, INNER), D ** -0.5, 0.1875, ((1, 4),)),
        "state_in": scatter_about(key_list[7], (D, G * NST), D ** -0.5, 0.1875, ((1, 4),)),
        "state_out": scatter_about(key_list[8], (D, G * NST), D ** -0.5, 0.1875, ((1, 4),)),
        "step_weight": scatter_about(key_list[9], (D, HEADS), D ** -0.5, 0.1875, ((1, 4),)),
        "conv_input": scatter_about(key_list[10], (KCONV, INNER), KCONV ** -0.5, 3.0, ((1, 4),), jnp.float32),
        "conv_statein": scatter_about(key_list[11], (KCONV, G * NST), KCONV ** -0.5, 3.0, ((1, 4),), jnp.float32),
        "conv_stateout": scatter_about(key_list[12], (KCONV, G * NST), KCONV ** -0.5, 3.0, ((1, 4),), jnp.float32),
        "step_bias": jnp.clip(-4.0 + 3.0 * jax.random.uniform(key_list[13], (HEADS,), jnp.float32) ** steps_of(key_list[13], (HEADS,), ((0, 4),), -0.2, 0.2), -4.0, -1.0),
        "rate_log": jnp.clip(-6.0 + 6.0 * jax.random.uniform(key_list[14], (HEADS,), jnp.float32) ** steps_of(key_list[14], (HEADS,), ((0, 4),), -0.2, 0.2), -6.0, 0.0),
        "skip_gain": jnp.clip(0.5 + 1.0 * jax.random.uniform(key_list[15], (HEADS,), jnp.float32) ** steps_of(key_list[15], (HEADS,), ((0, 4),), -0.2, 0.2), 0.5, 1.5),
        "inner_gain": jnp.clip(1.0 + 0.18 * jax.random.normal(key_list[16], (INNER,), jnp.float32), 0.1, 1.9),
        "mamba_output": scatter_about(key_list[17], (INNER, D), INNER ** -0.5, 0.125, ((0, 4),)),
        "query_weight": scatter_about(key_list[18], (D, ATT), D ** -0.5, 0.1875, ((1, 4),)),
        "key_weight": scatter_about(key_list[19], (D, ATT), D ** -0.5, 0.1875, ((1, 4),)),
        "value_weight": scatter_about(key_list[20], (D, ATT), D ** -0.5, 0.1875, ((1, 4),)),
        "attn_output": scatter_about(key_list[21], (ATT, D), (ATT // 8) ** -0.5, 0.5, ((0, 4),)),
        "second_gain": jnp.clip(1.0 + 0.18 * jax.random.normal(key_list[22], (D,), jnp.float32), 0.1, 1.9),
        "ffn_gate": scatter_about(key_list[23], (D, FF), D ** -0.5, 0.1875, ((1, 4),)),
        "ffn_up": scatter_about(key_list[24], (D, FF), D ** -0.5, 0.1875, ((1, 4),)),
        "ffn_down": scatter_about(key_list[25], (FF, D), FF ** -0.5, 0.09375, ((0, 4),)),
        "out_grad": heavy_noise(key_list[26], (TOKENS, D), 1.0, 6.0, ((0, 32),), (0, 1, 32, 2.75)),
    }


eps = 1e-05
exact_mode = lax.Precision.HIGHEST

@jax.custom_vjp
def low(v):
    return lax.optimization_barrier(v.astype(jnp.bfloat16)).astype(jnp.float32)

@jax.custom_vjp
def low_back(v):
    return v

def low_keep(v):
    return (low(v), None)

def low_pass(kept, grad):
    return (grad,)

def back_keep(v):
    return (v, None)

def back_low(kept, grad):
    return (low(grad),)
low.defvjp(low_keep, low_pass)
low_back.defvjp(back_keep, back_low)

def rms_scale(signal, gain):
    return signal * lax.rsqrt(lax.optimization_barrier(jnp.mean(signal * signal, axis=-1, keepdims=True)) + eps) * gain

def shifted_rows(signal, lag_rows, segment):
    length = signal.shape[0]
    shifted = jnp.concatenate([jnp.zeros((lag_rows, signal.shape[1]), signal.dtype), signal[:length - lag_rows]], axis=0)
    seg_shift = jnp.concatenate([jnp.full((lag_rows,), -1, jnp.int32), segment[:length - lag_rows]])
    return jnp.where((seg_shift == segment)[:, None], shifted, 0.0)

def causal_conv(signal, kernel, segment):
    output = signal * kernel[0]
    for lag_rows in range(1, kernel.shape[0]):
        output = output + shifted_rows(signal, lag_rows, segment) * kernel[lag_rows]
    return jax.nn.silu(output)

def visible(first_row, block_rows, segment):
    positions = jnp.arange(segment.shape[0], dtype=jnp.int32)
    row_pos = first_row + jnp.arange(block_rows, dtype=jnp.int32)
    row_seg = lax.dynamic_slice_in_dim(segment, first_row, block_rows, 0)
    return (row_pos[:, None] >= positions[None, :]) & (row_seg[:, None] == segment[None, :])

def mixer_core(gate_z, inner_x, state_b, state_c, step_raw, queries, key_rows, value_rows, conv_input, conv_statein, conv_stateout, step_bias, rate_log, skip_gain, inner_gain, segment):
    length = inner_x.shape[0]
    head_count = step_raw.shape[1]
    head_dim = inner_x.shape[1] // head_count
    groups = state_b.shape[1] // NST
    per_group = head_count // groups
    inner_width = inner_x.shape[1]
    block_rows = min(512, length)
    block_count = length // block_rows
    xconv = causal_conv(inner_x, conv_input, segment)
    bconv = causal_conv(state_b, conv_statein, segment)
    cconv = causal_conv(state_c, conv_stateout, segment)
    step_size = jax.nn.softplus(step_raw + step_bias)
    cum_log = jnp.cumsum(step_size * -jnp.exp(rate_log), axis=0)
    scaled_x = (xconv.reshape(length, head_count, head_dim) * step_size[:, :, None]).transpose(1, 0, 2)
    bgroup = bconv.reshape(length, groups, NST).transpose(1, 0, 2)
    cgroup = cconv.reshape(length, groups, NST).transpose(1, 0, 2)
    log_heads = cum_log.T

    def ssd_rows(block_index):
        first_row = block_index * block_rows
        rows_c = lax.dynamic_slice_in_dim(cgroup, first_row, block_rows, 1)
        inner_prod = jnp.einsum('gtn,gsn->gts', rows_c, bgroup, precision=exact_mode)
        inner_prod = jnp.repeat(inner_prod, per_group, axis=0)
        allowed = visible(first_row, block_rows, segment)[None]
        rows_log = lax.dynamic_slice_in_dim(log_heads, first_row, block_rows, 1)
        log_gap = rows_log[:, :, None] - log_heads[:, None, :]
        factor = jnp.where(allowed, jnp.exp(jnp.where(allowed, log_gap, 0.0)), 0.0)
        return jnp.einsum('hts,hsp->htp', inner_prod * factor, scaled_x, precision=exact_mode)
    blocks = jnp.arange(block_count, dtype=jnp.int32)
    ssd_out = lax.map(jax.checkpoint(ssd_rows), blocks)
    ssd_out = ssd_out.transpose(1, 0, 2, 3).reshape(head_count, length, head_dim).transpose(1, 0, 2)
    ssd_out = ssd_out + xconv.reshape(length, head_count, head_dim) * skip_gain[:, None]
    gated_out = ssd_out.reshape(length, inner_width) * jax.nn.silu(gate_z)
    grouped = gated_out.reshape(length, groups, inner_width // groups)
    grouped = grouped * lax.rsqrt(lax.optimization_barrier(jnp.mean(grouped * grouped, axis=-1, keepdims=True)) + eps)
    mamba_out = grouped.reshape(length, inner_width) * inner_gain
    att_heads = queries.shape[1] // AHDIM
    query_h = queries.reshape(length, att_heads, AHDIM).transpose(1, 0, 2)
    key_h = key_rows.reshape(length, att_heads, AHDIM).transpose(1, 0, 2)
    value_h = value_rows.reshape(length, att_heads, AHDIM).transpose(1, 0, 2)

    def attend_rows(block_index):
        first_row = block_index * block_rows
        rows_q = lax.dynamic_slice_in_dim(query_h, first_row, block_rows, 1)
        scores = jnp.einsum('hqd,hkd->hqk', rows_q, key_h, precision=exact_mode) * AHDIM ** (-0.5)
        allowed = visible(first_row, block_rows, segment)[None]
        scores = jnp.where(allowed, scores, -1e+30)
        peak = lax.optimization_barrier(jnp.max(scores, axis=-1, keepdims=True))
        weights = jnp.exp(scores - peak)
        weights = weights / lax.optimization_barrier(jnp.sum(weights, axis=-1, keepdims=True))
        return jnp.einsum('hqk,hkd->hqd', weights, value_h, precision=exact_mode)
    attn_out = lax.map(jax.checkpoint(attend_rows), blocks)
    attn_out = attn_out.transpose(1, 0, 2, 3).reshape(att_heads, length, AHDIM).transpose(1, 0, 2)
    return (mamba_out, attn_out.reshape(length, att_heads * AHDIM))

def sequence_forward(params, patch_rows, keep_rows, segment):
    embed_weight, first_gain, mamba_gate, mamba_input, state_in, state_out, step_weight, conv_input, conv_statein, conv_stateout, step_bias, rate_log, skip_gain, inner_gain, mamba_output, query_weight, key_weight, value_weight, attn_output, second_gain, ffn_gate, ffn_up, ffn_down = params
    embedded = low_back(jnp.dot(patch_rows, embed_weight, precision=exact_mode))
    resid_one = embedded * keep_rows[:, None]
    normed_one = low(rms_scale(resid_one, first_gain))
    projections = [low_back(jnp.dot(normed_one, weight_mat, precision=exact_mode)) for weight_mat in (mamba_gate, mamba_input, state_in, state_out, step_weight, query_weight, key_weight, value_weight)]
    mamba_out, attn_out = mixer_core(projections[0], projections[1], projections[2], projections[3], projections[4], projections[5], projections[6], projections[7], conv_input, conv_statein, conv_stateout, step_bias, rate_log, skip_gain, inner_gain, segment)
    mixer_sum = jnp.dot(low(mamba_out), mamba_output, precision=exact_mode) + jnp.dot(low(attn_out), attn_output, precision=exact_mode)
    resid_two = resid_one + low_back(mixer_sum)
    normed_two = low(rms_scale(resid_two, second_gain))
    gate_val = low_back(jnp.dot(normed_two, ffn_gate, precision=exact_mode))
    up_val = low_back(jnp.dot(normed_two, ffn_up, precision=exact_mode))
    hidden = low(jax.nn.silu(gate_val) * up_val)
    return resid_two + low_back(jnp.dot(hidden, ffn_down, precision=exact_mode))

def reference(patches, keep_mask, segments, embed_weight, first_gain, mamba_gate, mamba_input, state_in, state_out, step_weight, conv_input, conv_statein, conv_stateout, step_bias, rate_log, skip_gain, inner_gain, mamba_output, query_weight, key_weight, value_weight, attn_output, second_gain, ffn_gate, ffn_up, ffn_down, out_grad):
    params = (embed_weight, first_gain, mamba_gate, mamba_input, state_in, state_out, step_weight, conv_input, conv_statein, conv_stateout, step_bias, rate_log, skip_gain, inner_gain, mamba_output, query_weight, key_weight, value_weight, attn_output, second_gain, ffn_gate, ffn_up, ffn_down)
    floats = tuple((member.astype(jnp.float32) for member in params))
    patch_all = patches.astype(jnp.float32).reshape(SEQS, SEQ, PD)
    keep_all = keep_mask.astype(jnp.float32).reshape(SEQS, SEQ)

    def forward(param_tuple, patch_data):

        def single_sequence(sequence_items):
            return sequence_forward(param_tuple, sequence_items[0], sequence_items[1], sequence_items[2])
        return lax.map(jax.checkpoint(single_sequence), (patch_data, keep_all, segments))
    result, pullback = jax.vjp(forward, floats, patch_all)
    param_grads, patch_grad = pullback(out_grad.astype(jnp.float32).reshape(SEQS, SEQ, D))
    output = result.reshape(TOKENS, D).astype(jnp.bfloat16)
    patches_grad = patch_grad.reshape(TOKENS, PD).astype(jnp.bfloat16)
    return (output, patches_grad, param_grads[0], param_grads[1], param_grads[2], param_grads[3], param_grads[4], param_grads[5], param_grads[6], param_grads[7], param_grads[8], param_grads[9], param_grads[10], param_grads[11], param_grads[12], param_grads[13], param_grads[14], param_grads[15], param_grads[16], param_grads[17], param_grads[18], param_grads[19], param_grads[20], param_grads[21], param_grads[22])
```

```python
import functools

import jax
import jax.numpy as jnp
from jax import lax
from jax.experimental import pallas as pl
from jax.experimental.pallas import tpu as pltpu
from jax.sharding import PartitionSpec as P

f32 = jnp.float32
bf16 = jnp.bfloat16
eps = 1e-05
NST = 128
LOG2E = 1.4426950408889634
LOW = -1e30
NN = ((1,), (0,))
NT = ((1,), (1,))
TN = ((0,), (0,))
PROJ = 2048
STEPS = 8


def mm(a, b, dims=NN):
    return lax.dot_general(a, b, (dims, ((), ())), preferred_element_type=f32)


def mmx(a, b, dims=NN):
    return lax.dot_general(
        a, b, (dims, ((), ())), preferred_element_type=f32, precision=lax.Precision.HIGHEST
    )


def iota(shape, axis):
    return lax.broadcasted_iota(jnp.int32, shape, axis)


def expand(v):
    low_half = iota((1, 128), 1) < 64
    return jnp.concatenate(
        [
            jnp.where(low_half, v[:, h : h + 1], v[:, h + 1 : h + 2])
            for h in range(0, v.shape[1], 2)
        ],
        axis=1,
    )


def head_sum(v):
    owner = (iota((512, 8), 0) // 64 == iota((512, 8), 1)).astype(f32)
    return mmx(v, owner)


def softplus(v):
    return jnp.maximum(v, 0.0) + jnp.log1p(jnp.exp(-jnp.abs(v)))


def tile4(v):
    return jnp.concatenate([v, v, v, v], axis=1)


def fill_segments(seg_ref, segcol):
    length = seg_ref.shape[1]
    segcol[0:8, :] = jnp.full((8, 128), -1.0, f32)
    segcol[length + 8 : length + 16, :] = jnp.full((8, 128), -2.0, f32)
    for row in range(0, length, 128):
        piece = jnp.broadcast_to(seg_ref[0:1, row : row + 128], (128, 128))
        segcol[8 + row : 8 + row + 128, :] = piece.T


def taps_of(taps, tile):
    if tile < 4:
        return taps[0][:, tile * 128 : tile * 128 + 128]
    return taps[tile - 3][...]


def conv_masks(rows, segx):
    here = segx[8 : 8 + rows, :]
    return [(segx[8 - lag : 8 - lag + rows, :] == here).astype(f32) for lag in (1, 2, 3)]


def conv_pre(tile, rows, uext, masks, taps):
    lanes = slice(tile * 128, tile * 128 + 128)
    w = taps_of(taps, tile)
    lags = [uext[8 : 8 + rows, lanes]]
    for lag in (1, 2, 3):
        lags.append(uext[8 - lag : 8 - lag + rows, lanes] * masks[lag - 1])
    pre = lags[0] * w[0:1, :]
    for lag in (1, 2, 3):
        pre = pre + lags[lag] * w[lag : lag + 1, :]
    return pre, lags


def load_inputs(first, rows, proj, segcol, uext, segx):
    @pl.when(first == 0)
    def _():
        uext[0:8, :] = jnp.zeros((8, 768), f32)

    @pl.when(first > 0)
    def _():
        uext[0:8, :] = proj[pl.ds(pl.multiple_of(first - 16, 16), 16), 512:1280].astype(f32)[8:16]

    uext[8 : 8 + rows, :] = proj[pl.ds(first, rows), 512:1280].astype(f32)
    segx[...] = segcol[pl.ds(first, rows + 16), :]


def decays(first, rows, step, bias, rate):
    raw = step[pl.ds(first, rows), :] + bias[...]
    size = softplus(raw)
    logs = size * -jnp.exp(rate[...])
    scaled = logs * LOG2E
    lower = (iota((rows, rows), 0) >= iota((rows, rows), 1)).astype(f32)
    cum = mmx(lower, scaled)
    wide = jnp.concatenate([cum, jnp.zeros((rows, 120), f32)], axis=1)
    return raw, size, logs, cum, wide.T[0:8, :]


def half_masks():
    low_half = iota((1, 128), 1) < 64
    return low_half, jnp.logical_not(low_half)


def keep(mask, v):
    return jnp.where(mask, v, jnp.zeros_like(v))


def mixer_fwd_chunk(
    index, rows, proj, step, seg, segcol, taps, bias, rate, skip, gain, uext, segx, state,
    oacc, stats, mix_out, ssd_out, states_out, lse_out,
):
    first = pl.multiple_of(index * rows, rows)
    here = pl.ds(first, rows)
    halves = half_masks()
    load_inputs(first, rows, proj, segcol, uext, segx)
    masks = conv_masks(rows, segx)
    acts = []
    for tile in range(6):
        pre, _ = conv_pre(tile, rows, uext, masks, taps)
        acts.append(pre * jax.nn.sigmoid(pre))
    xc = jnp.concatenate(acts[0:4], axis=1)
    bc, cc = acts[4].astype(bf16), acts[5].astype(bf16)
    _, size, _, cum, cumr = decays(first, rows, step, bias, rate)
    segc = segx[8 : 8 + rows, :]
    before = segx[7:8, :]
    goes_on = (segc == before).astype(f32)
    segr = seg[0:1, here]
    wide_seg = jnp.concatenate([segc] * (rows // 128), axis=1)
    allowed = (iota((rows, rows), 0) >= iota((rows, rows), 1)) & (wide_seg == segr)
    away = jnp.where(allowed, 0.0, LOW)
    cb = mm(cc, bc, NT)
    xs = xc * expand(size)
    xsb = xs.astype(bf16)
    parts = []
    for pair in range(4):
        lhs = []
        for h in (2 * pair, 2 * pair + 1):
            gap = cum[:, h : h + 1] - cumr[h : h + 1, :] + away
            lhs.append((cb * jnp.exp2(gap)).astype(bf16))
        xp = xsb[:, pair * 128 : pair * 128 + 128]
        rhs = jnp.concatenate([keep(halves[0], xp), keep(halves[1], xp)], axis=0)
        parts.append(mm(jnp.concatenate(lhs, axis=1), rhs))
    ssd = jnp.concatenate(parts, axis=1) + xc * expand(skip[...])
    st = state[...]
    stb = st.astype(bf16)
    states_out[index] = stb
    ssd = ssd + mm(cc, stb) * expand(jnp.exp2(cum)) * tile4(goes_on)
    last = cum[rows - 1 : rows, :]
    fits = (segc == segc[rows - 1 : rows, :]).astype(f32)
    weight = expand(jnp.exp2(last - cum)) * tile4(fits)
    added = mm(bc, (xs * weight).astype(bf16), TN)
    passes = (segc[rows - 1 : rows, :] == before).astype(f32)
    state[...] = st * (expand(jnp.exp2(last)) * tile4(passes)) + added
    ssd_out[here, :] = ssd.astype(bf16)
    z = proj[here, 0:512].astype(f32)
    g = ssd * (z * jax.nn.sigmoid(z))
    r = lax.rsqrt(jnp.mean(g * g, axis=1, keepdims=True) + eps)
    mix_out[here, 0:512] = (g * r * gain[...]).astype(bf16)
    own_seg = seg[0:1, here]

    def keys(block, fresh):
        start = pl.multiple_of(block * rows, rows)
        away = attention_away(start, first, rows, own_seg, segcol)
        for pair in range(2):
            lanes = pair * 128
            q = proj[here, 1280 + lanes : 1408 + lanes] * jnp.asarray(0.125, bf16)
            k = proj[pl.ds(start, rows), 1536 + lanes : 1664 + lanes]
            v = proj[pl.ds(start, rows), 1792 + lanes : 1920 + lanes]
            for half in range(2):
                h = 2 * pair + half
                mine = slice(h * 64, h * 64 + 64)
                s = mm(k, keep(halves[half], q), NT) + away
                peak = jnp.max(s, axis=0, keepdims=True)
                if not fresh:
                    old = stats[h : h + 1, :]
                    peak = jnp.maximum(peak, old)
                    fade = jnp.exp(old - peak)
                p = jnp.exp(s - peak)
                total = jnp.sum(p, axis=0, keepdims=True)
                o = mm(v, p.astype(bf16), TN)[half * 64 : half * 64 + 64, :]
                if not fresh:
                    total = total + stats[h + 4 : h + 5, :] * fade
                    o = o + oacc[mine, :] * fade
                stats[h : h + 1, :] = peak
                stats[h + 4 : h + 5, :] = total
                oacc[mine, :] = o

    keys(index, True)

    def earlier(block, _):
        keys(block, False)
        return 0

    lax.fori_loop(0, index, earlier, 0)
    lse_out[0:4, here] = stats[0:4, :] + jnp.log(stats[4:8, :])
    for h in range(4):
        mine = slice(h * 64, h * 64 + 64)
        oacc[mine, :] = oacc[mine, :] * (1.0 / stats[h + 4 : h + 5, :])
    for pair in range(2):
        mine = slice(pair * 128, pair * 128 + 128)
        mix_out[here, 512 + pair * 128 : 640 + pair * 128] = oacc[mine, :].T.astype(bf16)


def attention_away(start, first, rows, own_seg, segcol):
    key_seg = segcol[pl.ds(start + 8, rows), :]
    wide = jnp.concatenate([key_seg] * (rows // 128), axis=1)
    allowed = (wide == own_seg) & (
        iota((rows, rows), 0) + start <= iota((rows, rows), 1) + first
    )
    return jnp.where(allowed, 0.0, LOW)


def mixer_bwd_chunk(
    index, rows, proj, step, seg, segcol, taps, bias, rate, skip, gain, uext, segx, dext,
    dstate, dkv, dqs, mix, ssd_in, states_in, lse_in, dmix, dproj, dstep, dtaps, dheads, dgain, dskip,
):
    first = pl.multiple_of(index * rows, rows)
    here = pl.ds(first, rows)
    halves = half_masks()
    load_inputs(first, rows, proj, segcol, uext, segx)
    masks = conv_masks(rows, segx)
    acts = []
    for tile in range(6):
        pre, _ = conv_pre(tile, rows, uext, masks, taps)
        acts.append(pre * jax.nn.sigmoid(pre))
    xc = jnp.concatenate(acts[0:4], axis=1)
    bc, cc = acts[4].astype(bf16), acts[5].astype(bf16)
    raw, size, logs, cum, cumr = decays(first, rows, step, bias, rate)
    z = proj[here, 0:512].astype(f32)
    ssd = ssd_in[here, :].astype(f32)
    dmo = dmix[here, 0:512].astype(f32)
    sig = jax.nn.sigmoid(z)
    act = z * sig
    g = ssd * act
    r = lax.rsqrt(jnp.mean(g * g, axis=1, keepdims=True) + eps)
    gain_part = jnp.sum(dmo * g * r, axis=0, keepdims=True)
    a = dmo * gain[...]
    dg = r * a - (r * r * r) * g * jnp.mean(a * g, axis=1, keepdims=True)
    dssd = dg * act
    dproj[here, 0:512] = (dg * ssd * (sig * (1.0 + z * (1.0 - sig)))).astype(bf16)
    skip_part = jnp.sum(dssd * xc, axis=0, keepdims=True)
    dxc = dssd * expand(skip[...])
    dyb = dssd.astype(bf16)
    wide_size = expand(size)
    xs = xc * wide_size
    xsb = xs.astype(bf16)
    segc = segx[8 : 8 + rows, :]
    before = segx[7:8, :]
    goes_on = (segc == before).astype(f32)
    segr = seg[0:1, here]
    wide_seg = jnp.concatenate([segc] * (rows // 128), axis=1)
    allowed = (iota((rows, rows), 0) <= iota((rows, rows), 1)) & (wide_seg == segr)
    away = jnp.where(allowed, 0.0, LOW)
    cbt = mm(bc, cc, NT)
    dcbt = jnp.zeros((rows, rows), f32)
    to_rows = []
    from_rows = jnp.zeros((rows, 8), f32)
    parts = []
    for pair in range(4):
        lanes = slice(pair * 128, pair * 128 + 128)
        lhs, rhs = [], []
        for half in range(2):
            h = 2 * pair + half
            lt = jnp.exp2(cumr[h : h + 1, :] - cum[:, h : h + 1] + away)
            mt = cbt * lt
            lhs.append(mt.astype(bf16))
            rhs.append(keep(halves[half], dyb[:, lanes]))
            dl = mm(keep(halves[half], xsb[:, lanes]), dyb[:, lanes], NT)
            dcbt = dcbt + dl * lt
            gt = dl * mt
            to_rows.append(jnp.sum(gt, axis=0, keepdims=True))
            from_rows = jnp.where(
                iota((1, 8), 1) == h, jnp.sum(gt, axis=1, keepdims=True), from_rows
            )
        parts.append(mm(jnp.concatenate(lhs, axis=1), jnp.concatenate(rhs, axis=0)))
    dxs = jnp.concatenate(parts, axis=1)
    dcb = dcbt.astype(bf16)
    db = mm(dcb, cc)
    dc = mm(dcb, bc, TN)
    upper = (iota((rows, rows), 0) <= iota((rows, rows), 1)).astype(f32)
    late = -from_rows
    reach = expand(jnp.exp2(cum)) * tile4(goes_on)
    stb = states_in[index]
    dye = dssd * reach
    dyeb = dye.astype(bf16)
    dc = dc + mm(dyeb, stb, NT)
    late = late + head_sum(dye * mm(cc, stb))
    into_state = mm(cc, dyeb, TN)
    last = cum[rows - 1 : rows, :]
    fits = (segc == segc[rows - 1 : rows, :]).astype(f32)
    weight = expand(jnp.exp2(last - cum)) * tile4(fits)
    dst = dstate[...]
    dsb = dst.astype(bf16)
    dxi = mm(bc, dsb) * weight
    dxs = dxs + dxi
    db = db + mm((xs * weight).astype(bf16), dsb, NT)
    strict = (iota((rows, rows), 0) > iota((rows, rows), 1)).astype(f32)
    dlog = mmx(strict, head_sum(xs * dxi))
    passes = (segc[rows - 1 : rows, :] == before).astype(f32)
    fade = expand(jnp.exp2(last)) * tile4(passes)
    through = jnp.sum(stb.astype(f32) * dst, axis=0, keepdims=True) * fade
    dlog = dlog + head_sum(jnp.broadcast_to(through, (8, 512)))[0:1, :]
    dstate[...] = dst * fade + into_state
    dlog = dlog + mmx(upper, late) + mmx(upper, jnp.concatenate(to_rows, axis=0), NT)
    dsize = head_sum(dxs * xc) - dlog * jnp.exp(rate[...])
    rate_part = jnp.sum(dlog * logs, axis=0, keepdims=True)
    draw = dsize * jax.nn.sigmoid(raw)
    bias_part = jnp.sum(draw, axis=0, keepdims=True)
    dstep[here, :] = draw.astype(dstep.dtype)
    dxc = dxc + dxs * wide_size
    dacts = [dxc[:, t * 128 : t * 128 + 128] for t in range(4)] + [db, dc]
    dext[rows : rows + 8, :] = dext[0:8, :]
    ahead = [(segx[8 + lag : 8 + lag + rows, :] == segc).astype(f32) for lag in (1, 2, 3)]
    for tile in range(6):
        lanes = slice(tile * 128, tile * 128 + 128)
        w = taps_of(taps, tile)
        pre, lags = conv_pre(tile, rows, uext, masks, taps)
        sig = jax.nn.sigmoid(pre)
        dpre = dacts[tile] * (sig * (1.0 + pre * (1.0 - sig)))
        dext[0:rows, lanes] = dpre
        du = dpre * w[0:1, :]
        for lag in (1, 2, 3):
            du = du + dext[lag : lag + rows, lanes] * ahead[lag - 1] * w[lag : lag + 1, :]
        dproj[here, 512 + tile * 128 : 640 + tile * 128] = du.astype(bf16)
        sums = jnp.concatenate(
            [jnp.sum(dpre * shifted, axis=0, keepdims=True) for shifted in lags], axis=0
        )
        dtaps[:, lanes] = dtaps[:, lanes] + sums
    head_parts = jnp.concatenate([bias_part, rate_part], axis=0)
    dheads[...] = dheads[...] + head_parts
    dgain[...] = dgain[...] + gain_part
    dskip[...] = dskip[...] + skip_part
    own_seg = seg[0:1, here]
    dos = [dmix[here, 512 + pair * 128 : 640 + pair * 128] for pair in range(2)]
    owner = (iota((8, 256), 1) // 64 == iota((8, 256), 0)).astype(f32)
    delta = mmx(
        owner,
        jnp.concatenate(dos, axis=1).astype(f32) * mix[here, 512:768].astype(f32),
        NT,
    )
    dqs[...] = jnp.zeros_like(dqs)

    def keys(block, _):
        start = pl.multiple_of(block * rows, rows)
        there = pl.ds(start, rows)
        away = attention_away(start, first, rows, own_seg, segcol)
        for pair in range(2):
            lanes = pair * 128
            q = proj[here, 1280 + lanes : 1408 + lanes] * jnp.asarray(0.125, bf16)
            k = proj[there, 1536 + lanes : 1664 + lanes]
            v = proj[there, 1792 + lanes : 1920 + lanes]
            ps, dss, qms, doms = [], [], [], []
            for half in range(2):
                h = 2 * pair + half
                mine = slice(h * 64, h * 64 + 64)
                qm, dom = keep(halves[half], q), keep(halves[half], dos[pair])
                p = jnp.exp(mm(k, qm, NT) + away - lse_in[h : h + 1, here])
                dp = mm(v, dom, NT)
                ds = (p * (dp - delta[h : h + 1, :])).astype(bf16)
                dqs[mine, :] = dqs[mine, :] + mm(k, ds, TN)[half * 64 : half * 64 + 64, :]
                ps.append(p.astype(bf16))
                dss.append(ds)
                qms.append(qm)
                doms.append(dom)
            kl, vl = slice(lanes, lanes + 128), slice(256 + lanes, 384 + lanes)
            dkv[there, kl] = dkv[there, kl] + mm(
                jnp.concatenate(dss, axis=1), jnp.concatenate(qms, axis=0)
            )
            dkv[there, vl] = dkv[there, vl] + mm(
                jnp.concatenate(ps, axis=1), jnp.concatenate(doms, axis=0)
            )
        return 0

    lax.fori_loop(0, index + 1, keys, 0)
    for pair in range(2):
        mine = slice(pair * 128, pair * 128 + 128)
        dproj[here, 1280 + pair * 128 : 1408 + pair * 128] = (dqs[mine, :] * 0.125).T.astype(bf16)
    dproj[here, 1536:2048] = dkv[here, :].astype(bf16)


def fwd_kernel(count, proj, step, seg, t0, t1, t2, bias, rate, skip, gain,
               mix_out, ssd_out, states_out, lse_out, segcol, uext, segx, state, oacc, stats):
    rows = proj.shape[0] // count
    fill_segments(seg, segcol)
    lse_out[...] = jnp.zeros_like(lse_out)
    state[...] = jnp.zeros_like(state)

    def chunk(index, _):
        mixer_fwd_chunk(index, rows, proj, step, seg, segcol, (t0, t1, t2), bias, rate, skip,
                        gain, uext, segx, state, oacc, stats, mix_out, ssd_out, states_out,
                        lse_out)
        return 0

    lax.fori_loop(0, count, chunk, 0)


def bwd_kernel(count, proj, step, seg, t0, t1, t2, bias, rate, skip, gain, mix, ssd_in,
               states_in, lse_in, dmix, dproj, dstep, dtaps, dheads, dgain, dskip,
               segcol, uext, segx, dext, dstate, dkv, dqs):
    rows = proj.shape[0] // count
    fill_segments(seg, segcol)
    for ref in (dtaps, dheads, dgain, dskip, dstate, dkv):
        ref[...] = jnp.zeros_like(ref)
    dext[0:8, :] = jnp.zeros((8, 768), f32)

    def chunk(turn, _):
        mixer_bwd_chunk(count - 1 - turn, rows, proj, step, seg, segcol, (t0, t1, t2), bias,
                        rate, skip, gain, uext, segx, dext, dstate, dkv, dqs, mix, ssd_in,
                        states_in, lse_in, dmix, dproj, dstep, dtaps, dheads, dgain, dskip)
        return 0

    lax.fori_loop(0, count, chunk, 0)
    dskip8 = head_sum(jnp.broadcast_to(dskip[...], (8, 512)))
    dskip[0:1, 0:8] = dskip8[0:1, :]


def mixer_fwd(count, proj, step, seg, taps, bias, rate, skip, gain):
    length = proj.shape[0]
    rows = length // count
    return pl.pallas_call(
        functools.partial(fwd_kernel, count),
        out_shape=(
            jax.ShapeDtypeStruct((length, 768), bf16),
            jax.ShapeDtypeStruct((length, 512), bf16),
            jax.ShapeDtypeStruct((count, NST, 512), bf16),
            jax.ShapeDtypeStruct((8, length), f32),
        ),
        scratch_shapes=[
            pltpu.VMEM((length + 16, 128), f32),
            pltpu.VMEM((rows + 8, 768), f32),
            pltpu.VMEM((rows + 16, 128), f32),
            pltpu.VMEM((NST, 512), f32),
            pltpu.VMEM((256, rows), f32),
            pltpu.VMEM((8, rows), f32),
        ],
        compiler_params=pltpu.CompilerParams(vmem_limit_bytes=60 * 2**20),
    )(proj, step, seg, *taps, bias, rate, skip, gain)


def mixer_bwd(count, proj, step, seg, taps, bias, rate, skip, gain, mix, ssd, states, lse, dmix):
    length = proj.shape[0]
    rows = length // count
    return pl.pallas_call(
        functools.partial(bwd_kernel, count),
        out_shape=(
            jax.ShapeDtypeStruct((length, 2048), bf16),
            jax.ShapeDtypeStruct((length, 8), bf16),
            jax.ShapeDtypeStruct((4, 768), f32),
            jax.ShapeDtypeStruct((2, 8), f32),
            jax.ShapeDtypeStruct((1, 512), f32),
            jax.ShapeDtypeStruct((1, 512), f32),
        ),
        scratch_shapes=[
            pltpu.VMEM((length + 16, 128), f32),
            pltpu.VMEM((rows + 8, 768), f32),
            pltpu.VMEM((rows + 16, 128), f32),
            pltpu.VMEM((rows + 8, 768), f32),
            pltpu.VMEM((NST, 512), f32),
            pltpu.VMEM((length, 512), f32),
            pltpu.VMEM((256, rows), f32),
        ],
        compiler_params=pltpu.CompilerParams(vmem_limit_bytes=60 * 2**20),
    )(proj, step, seg, *taps, bias, rate, skip, gain, mix, ssd, states, lse, dmix)


MESH = pl.DeviceIdType.MESH


class Line:
    def __init__(self, scratch, size):
        (self.own, self.left, self.right, self.full, self.acc,
         self.ss, self.sr, self.gs, self.gr) = scratch
        self.size = size
        self.steps = self.own.shape[1]
        self.me = lax.axis_index("tp")
        self.last = size - 1

    @staticmethod
    def scratch(size, steps, sub, width):
        return [
            pltpu.VMEM((size, steps, sub, width), f32),
            pltpu.VMEM((size, steps, sub, width), bf16),
            pltpu.VMEM((size, steps, sub, width), bf16),
            pltpu.VMEM((size, steps, sub, width), bf16),
            pltpu.VMEM((sub, width), f32),
            pltpu.SemaphoreType.DMA((2, size, steps)),
            pltpu.SemaphoreType.DMA((2, size, steps)),
            pltpu.SemaphoreType.DMA((2, size, steps)),
            pltpu.SemaphoreType.DMA((2, size, steps)),
        ]

    def sum_copy(self, way, d, j):
        buf = self.left if way == 0 else self.right
        return pltpu.make_async_remote_copy(
            src_ref=buf.at[d, j],
            dst_ref=buf.at[d, j],
            send_sem=self.ss.at[way, d, j],
            recv_sem=self.sr.at[way, d, j],
            device_id={"tp": self.me + 1 if way == 0 else self.me - 1},
            device_id_type=MESH,
        )

    def row_copy(self, way, d, j):
        return pltpu.make_async_remote_copy(
            src_ref=self.full.at[d, j],
            dst_ref=self.full.at[d, j],
            send_sem=self.gs.at[way, d, j],
            recv_sem=self.gr.at[way, d, j],
            device_id={"tp": self.me + 1 if way == 0 else self.me - 1},
            device_id_type=MESH,
        )

    def enter(self):
        barrier = pltpu.get_barrier_semaphore()
        me, last = self.me, self.last

        @pl.when(me > 0)
        def _():
            pl.semaphore_signal(barrier, inc=1, device_id={"tp": me - 1}, device_id_type=MESH)

        @pl.when(me < last)
        def _():
            pl.semaphore_signal(barrier, inc=1, device_id={"tp": me + 1}, device_id_type=MESH)

        peers = jnp.where(me > 0, 1, 0) + jnp.where(me < last, 1, 0)
        pl.semaphore_wait(barrier, peers)

    def relay(self, way, j):
        me, last = self.me, self.last
        buf = self.left if way == 0 else self.right
        first_one = me == 0 if way == 0 else me == last

        def one(d, _):
            @pl.when(first_one)
            def _():
                buf[d, j] = self.own[d, j].astype(bf16)

            @pl.when(jnp.logical_not(first_one))
            def _():
                self.sum_copy(way, d, j).wait_recv()
                buf[d, j] = (buf[d, j].astype(f32) + self.own[d, j]).astype(bf16)

            self.sum_copy(way, d, j).start()
            return 0

        if way == 0:
            lax.fori_loop(me + 1, self.size, one, 0)
        else:
            lax.fori_loop(0, me, one, 0)

    def settle(self, j, finish):
        me, last = self.me, self.last
        self.acc[...] = self.own[me, j]

        @pl.when(me > 0)
        def _():
            self.sum_copy(0, me, j).wait_recv()
            self.acc[...] = self.acc[...] + self.left[me, j].astype(f32)

        @pl.when(me < last)
        def _():
            self.sum_copy(1, me, j).wait_recv()
            self.acc[...] = self.acc[...] + self.right[me, j].astype(f32)

        self.full[me, j] = finish(j, self.acc[...])

        @pl.when(me < last)
        def _():
            self.row_copy(0, me, j).start()

        @pl.when(me > 0)
        def _():
            self.row_copy(1, me, j).start()

    def inside(self, j):
        return jnp.logical_and(j >= 0, j < self.steps)

    def pass_on(self, i):
        me, last = self.me, self.last

        def from_left(d, _):
            j = i - jnp.maximum(d, last - d) - (me - d)

            @pl.when(self.inside(j))
            def _():
                self.row_copy(0, d, j).wait_recv()

                @pl.when(me < last)
                def _():
                    self.row_copy(0, d, j).start()

            return 0

        def from_right(d, _):
            j = i - jnp.maximum(d, last - d) - (d - me)

            @pl.when(self.inside(j))
            def _():
                self.row_copy(1, d, j).wait_recv()

                @pl.when(me > 0)
                def _():
                    self.row_copy(1, d, j).start()

            return 0

        lax.fori_loop(0, me, from_left, 0)
        lax.fori_loop(me + 1, self.size, from_right, 0)

    def move(self, i, finish):
        me, last = self.me, self.last
        right_step = i - me
        left_step = i - (last - me)
        final_step = i - jnp.maximum(me, last - me)

        @pl.when(self.inside(right_step))
        def _():
            self.relay(0, right_step)

        @pl.when(self.inside(left_step))
        def _():
            self.relay(1, left_step)

        @pl.when(self.inside(final_step))
        def _():
            self.settle(final_step, finish)

        self.pass_on(i)

    def ready_step(self, i):
        return i - self.last - jnp.maximum(self.me, self.last - self.me)

    def lag(self):
        return 2 * self.last

    def leave(self):
        me, last = self.me, self.last

        def step(j, _):
            def right_sums(d, _):
                self.sum_copy(0, d, j).wait_send()
                return 0

            def left_sums(d, _):
                self.sum_copy(1, d, j).wait_send()
                return 0

            def right_rows(d, _):
                self.row_copy(0, d, j).wait_send()
                return 0

            def left_rows(d, _):
                self.row_copy(1, d, j).wait_send()
                return 0

            lax.fori_loop(me + 1, self.size, right_sums, 0)
            lax.fori_loop(0, me, left_sums, 0)

            @pl.when(me < last)
            def _():
                lax.fori_loop(0, me + 1, right_rows, 0)

            @pl.when(me > 0)
            def _():
                lax.fori_loop(me, self.size, left_rows, 0)

            return 0

        lax.fori_loop(0, self.steps, step, 0)


def flat(v):
    return v.reshape(v.shape[0] * v.shape[1], v.shape[2])


def normed(v, gain):
    return v * lax.rsqrt(jnp.mean(v * v, axis=1, keepdims=True) + eps) * gain


def normed_back(grad, v, gain):
    r = lax.rsqrt(jnp.mean(v * v, axis=1, keepdims=True) + eps)
    a = grad * gain
    back = r * a - (r * r * r) * v * jnp.mean(a * v, axis=1, keepdims=True)
    return back, jnp.sum(grad * v * r, axis=0, keepdims=True)


def embed_kernel(size, patches, embed, keep_rows, gain, wz, wx, wb, wc, wq, wk, wv, ws,
                 resid_out, full_out, proj_out, step_out, *scratch):
    line = Line(scratch, size)
    steps, sub = line.steps, line.own.shape[2]
    columns = []
    for ref in (wz, wx, wb, wc, wq, wk, wv):
        columns.append((ref, sum(c[0].shape[1] for c in columns)))

    def produce(j):
        line.own[:, j] = mm(flat(patches[:, j]), embed[...]).reshape(size, sub, line.own.shape[3])

    def finish(j, total):
        rows = total * keep_rows[j]
        resid_out[j] = rows
        return normed(rows, gain[...]).astype(bf16)

    def consume(j):
        x = line.full[:, j]
        full_out[:, j] = x
        x = flat(x)
        for ref, start in columns:
            width = ref.shape[1]
            proj_out[:, j, :, start : start + width] = (
                mm(x, ref[...]).astype(bf16).reshape(size, sub, width)
            )
        step_out[:, j] = mm(x, ws[...]).reshape(size, sub, ws.shape[1])

    line.enter()
    produce(0)

    def iteration(i, _):
        line.move(i, finish)

        @pl.when(i + 1 < steps)
        def _():
            produce(i + 1)

        ready = line.ready_step(i)

        @pl.when(line.inside(ready))
        def _():
            consume(ready)

        return 0

    lax.fori_loop(0, steps + line.lag(), iteration, 0)
    line.leave()


def ffn_kernel(size, mix, wmo, wao, resid_one, gain, wg, wu, wd, og_full, og_mine,
               resid_grad, full_out, hidden_out, gg_out, ug_out, ffn_out, resid_out, mixg_out,
               dmix, gain_grad, *scratch):
    half = len(scratch) // 2
    one, two = Line(scratch[:half], size), Line(scratch[half:], size)
    steps, sub, width = one.steps, one.own.shape[2], one.own.shape[3]
    inner = wmo.shape[0]

    def shaped(v):
        return v.reshape(size, sub, v.shape[1])

    def produce(j):
        x = flat(mix[:, j])
        one.own[:, j] = shaped(mm(x[:, 0:inner], wmo[...]) + mm(x[:, inner:], wao[...]))

    def finish_one(j, total):
        rows = resid_one[j] + total
        resid_out[j] = rows
        return normed(rows, gain[...]).astype(bf16)

    def middle(j):
        x = one.full[:, j]
        full_out[:, j] = x
        x = flat(x)
        og = flat(og_full[:, j])
        gate, up = mm(x, wg[...]), mm(x, wu[...])
        hg = mm(og, wd[...], NT)
        sig = jax.nn.sigmoid(gate)
        act = gate * sig
        hidden = (act * up).astype(bf16)
        gg = (hg * up * (sig * (1.0 + gate * (1.0 - sig)))).astype(bf16)
        ug = (hg * act).astype(bf16)
        hidden_out[:, j] = shaped(hidden)
        gg_out[:, j] = shaped(gg)
        ug_out[:, j] = shaped(ug)
        two.own[:, j] = shaped(mm(gg, wg[...], NT) + mm(ug, wu[...], NT))
        ffn_out[:, j] = shaped(mm(hidden, wd[...]).astype(bf16))

    def finish_two(j, total):
        back, part = normed_back(total, resid_out[j], gain[...])
        rows = og_mine[j].astype(f32) + back
        resid_grad[j] = rows
        gain_grad[...] = gain_grad[...] + part
        return rows.astype(bf16)

    def consume(j):
        x = two.full[:, j]
        mixg_out[:, j] = x
        x = flat(x)
        dmix[:, j, :, 0:inner] = shaped(mm(x, wmo[...], NT).astype(bf16))
        dmix[:, j, :, inner:] = shaped(mm(x, wao[...], NT).astype(bf16))

    one.enter()
    gain_grad[...] = jnp.zeros_like(gain_grad)
    produce(0)
    lag = one.lag() + 1

    def iteration(i, _):
        one.move(i, finish_one)
        two.move(i - lag, finish_two)

        @pl.when(i + 1 < steps)
        def _():
            produce(i + 1)

        ready_one = one.ready_step(i)

        @pl.when(one.inside(ready_one))
        def _():
            middle(ready_one)

        ready_two = two.ready_step(i - lag)

        @pl.when(two.inside(ready_two))
        def _():
            consume(ready_two)

        return 0

    lax.fori_loop(0, steps + lag + two.lag(), iteration, 0)
    one.leave()
    two.leave()


def entry_kernel(size, dproj, dstep, wz, wx, wb, wc, wq, wk, wv, ws, resid_one, gain, resid_grad,
                 keep_rows, embed, eg_out, patch_grad, gain_grad, *scratch):
    line = Line(scratch, size)
    steps, sub = line.steps, line.own.shape[2]
    columns = []
    for ref in (wz, wx, wb, wc, wq, wk, wv):
        columns.append((ref, sum(c[0].shape[1] for c in columns)))

    def produce(j):
        total = mm(flat(dstep[:, j]), ws[...], NT)
        for ref, start in columns:
            total = total + mm(flat(dproj[:, j, :, start : start + ref.shape[1]]), ref[...], NT)
        line.own[:, j] = total.reshape(size, sub, total.shape[1])

    def finish(j, total):
        back, part = normed_back(total, resid_one[j], gain[...])
        gain_grad[...] = gain_grad[...] + part
        return ((resid_grad[j] + back) * keep_rows[j]).astype(bf16)

    def consume(j):
        x = line.full[:, j]
        eg_out[:, j] = x
        patch_grad[:, j] = (
            mm(flat(x), embed[...], NT).astype(bf16).reshape(size, sub, embed.shape[0])
        )

    line.enter()
    gain_grad[...] = jnp.zeros_like(gain_grad)
    produce(0)

    def iteration(i, _):
        line.move(i, finish)

        @pl.when(i + 1 < steps)
        def _():
            produce(i + 1)

        ready = line.ready_step(i)

        @pl.when(line.inside(ready))
        def _():
            consume(ready)

        return 0

    lax.fori_loop(0, steps + line.lag(), iteration, 0)
    line.leave()


def comm_call(body, out_shape, scratch, identity, *args):
    return pl.pallas_call(
        body,
        out_shape=out_shape,
        in_specs=[pl.BlockSpec(memory_space=pltpu.VMEM)] * len(args),
        out_specs=tuple(pl.BlockSpec(memory_space=pltpu.VMEM) for _ in out_shape),
        scratch_shapes=scratch,
        compiler_params=pltpu.CompilerParams(
            collective_id=identity, has_side_effects=True, vmem_limit_bytes=62 * 2**20
        ),
    )(*args)


def sds(shape, kind):
    return jax.ShapeDtypeStruct(shape, kind)


def split_parts(matrix, widths, axis):
    pieces_out = []
    offset = 0
    for width in widths:
        pieces_out.append(lax.slice_in_dim(matrix, offset, offset + width, axis=axis))
        offset = offset + width
    return pieces_out


def reduce_weights(rows_first, cols_first):
    return (
        lax.psum_scatter(
            rows_first.astype(jnp.bfloat16), "dp", scatter_dimension=0, tiled=True
        ).astype(jnp.float32),
        lax.psum_scatter(
            cols_first.astype(jnp.bfloat16), "dp", scatter_dimension=1, tiled=True
        ).astype(jnp.float32),
    )


def shards(
    patches,
    keep_mask,
    segments,
    embed_weight,
    first_gain,
    mamba_gate,
    mamba_input,
    state_in,
    state_out,
    step_weight,
    conv_input,
    conv_statein,
    conv_stateout,
    step_bias,
    rate_log,
    skip_gain,
    inner_gain,
    mamba_output,
    query_weight,
    key_weight,
    value_weight,
    attn_output,
    second_gain,
    ffn_gate,
    ffn_up,
    ffn_down,
    out_grad,
):
    size = lax.axis_size("tp")
    segment = segments[0]
    length = patches.shape[0]
    mine = length // size
    sub = mine // STEPS
    shape = (size, STEPS, sub)
    width = embed_weight.shape[1]
    keep_rows = keep_mask.astype(f32).reshape(STEPS, sub, 1)
    seg_row = segment.astype(f32)[None]
    taps = (conv_input, conv_statein, conv_stateout)
    core_params = (step_bias[None], rate_log[None], skip_gain[None], inner_gain[None])
    in_list = (
        mamba_gate,
        mamba_input,
        state_in,
        state_out,
        query_weight,
        key_weight,
        value_weight,
        step_weight,
    )
    one_gain, two_gain = first_gain[None], second_gain[None]
    buffers = Line.scratch(size, STEPS, sub, width)
    og_full = lax.all_gather(out_grad, "tp", axis=0, tiled=True)

    resid_one, full_one, projected, step_raw = comm_call(
        functools.partial(embed_kernel, size),
        (
            sds((STEPS, sub, width), f32),
            sds((*shape, width), bf16),
            sds((*shape, PROJ), bf16),
            sds((*shape, step_weight.shape[1]), f32),
        ),
        buffers,
        1,
        patches.reshape(*shape, patches.shape[1]),
        embed_weight,
        keep_rows,
        one_gain,
        *in_list,
    )
    projected = projected.reshape(length, PROJ)
    step_raw = step_raw.reshape(length, step_weight.shape[1])
    mix_in, ssd, states, lse = mixer_fwd(size, projected, step_raw, seg_row, taps, *core_params)
    inner_width = mamba_output.shape[0]
    hidden_width = ffn_gate.shape[1]
    wide = sds((*shape, hidden_width), bf16)
    rows16 = sds((*shape, width), bf16)
    rows32 = sds((STEPS, sub, width), f32)
    (
        resid_grad, full_two, hidden, gate_grad, up_grad, ffn_part, resid_two, mix_full, dmix,
        second_gain_grad,
    ) = comm_call(
        functools.partial(ffn_kernel, size),
        (
            rows32, rows16, wide, wide, wide, rows16, rows32, rows16,
            sds((*shape, mix_in.shape[1]), bf16), sds((1, width), f32),
        ),
        buffers + buffers,
        2,
        mix_in.reshape(*shape, mix_in.shape[1]),
        mamba_output,
        attn_output,
        resid_one,
        two_gain,
        ffn_gate,
        ffn_up,
        ffn_down,
        og_full.reshape(*shape, width),
        out_grad.reshape(STEPS, sub, width),
    )
    ffn_sum = lax.psum_scatter(
        ffn_part.reshape(length, width), "tp", scatter_dimension=0, tiled=True
    )
    result = (resid_two.reshape(mine, width) + ffn_sum.astype(f32)).astype(bf16)

    def rows_of(v):
        return v.reshape(length, v.shape[-1])

    def outer(a, b):
        return mm(rows_of(a), rows_of(b), TN).astype(bf16)

    down_grad = outer(hidden, og_full)
    ffn_gate_part = outer(full_two, gate_grad)
    ffn_up_part = outer(full_two, up_grad)
    mixout_grad = outer(mix_in, mix_full)
    proj_grad, step_grad, dtaps, dheads, dgain, dskip = mixer_bwd(
        size, projected, step_raw, seg_row, taps, *core_params, mix_in, ssd, states, lse,
        rows_of(dmix),
    )
    in_part = jnp.concatenate([outer(full_one, proj_grad), outer(full_one, step_grad)], axis=1)
    embedded_full, patches_grad, first_gain_grad = comm_call(
        functools.partial(entry_kernel, size),
        (rows16, sds((*shape, patches.shape[1]), bf16), sds((1, width), f32)),
        buffers,
        3,
        proj_grad.reshape(*shape, PROJ),
        step_grad.reshape(*shape, step_grad.shape[1]),
        *in_list,
        resid_one,
        one_gain,
        resid_grad,
        keep_rows,
        embed_weight,
    )
    embed_grad = outer(patches, embedded_full)

    def scatter(v, axis):
        return lax.psum_scatter(v, "dp", scatter_dimension=axis, tiled=True).astype(f32)

    ffn_rows = scatter(jnp.concatenate([ffn_gate_part, ffn_up_part], axis=1), 0)
    mid_cols = scatter(jnp.concatenate([mixout_grad, down_grad], axis=0), 1)
    in_rows = scatter(in_part, 0)
    embed_cols = scatter(embed_grad, 1)
    head_sums = lax.psum(
        (
            dtaps[:, 0:512],
            dtaps[:, 512:640],
            dtaps[:, 640:768],
            dheads[0],
            dheads[1],
            dskip[0, 0:8],
            dgain[0],
        ),
        "dp",
    )
    gain_one_sum = lax.psum_scatter(
        first_gain_grad[0], ("dp", "tp"), scatter_dimension=0, tiled=True
    )
    gain_two_sum = lax.psum_scatter(
        second_gain_grad[0], ("dp", "tp"), scatter_dimension=0, tiled=True
    )
    in_parts = split_parts(in_rows, [member.shape[1] for member in in_list], 1)
    ffn_parts = split_parts(ffn_rows, [hidden_width, hidden_width], 1)
    mid_parts = split_parts(mid_cols, [inner_width, attn_output.shape[0], hidden_width], 0)
    return (
        result,
        patches_grad.reshape(length, patches.shape[1]),
        embed_cols,
        gain_one_sum,
        in_parts[0],
        in_parts[1],
        in_parts[2],
        in_parts[3],
        in_parts[7],
        *head_sums,
        mid_parts[0],
        in_parts[4],
        in_parts[5],
        in_parts[6],
        mid_parts[1],
        gain_two_sum,
        ffn_parts[0],
        ffn_parts[1],
        mid_parts[2],
    )


def solution(mesh):
    return jax.shard_map(
        shards,
        mesh=mesh,
        in_specs=(
            P("dp", "tp"),
            P(("dp", "tp")),
            P("dp", None),
            P("tp", None),
            P(),
            P(None, "tp"),
            P(None, "tp"),
            P(None, "tp"),
            P(None, "tp"),
            P(None, "tp"),
            P(None, "tp"),
            P(None, "tp"),
            P(None, "tp"),
            P("tp"),
            P("tp"),
            P("tp"),
            P("tp"),
            P("tp", None),
            P(None, "tp"),
            P(None, "tp"),
            P(None, "tp"),
            P("tp", None),
            P(),
            P(None, "tp"),
            P(None, "tp"),
            P("tp", None),
            P(("dp", "tp"), None),
        ),
        out_specs=(
            P(("dp", "tp"), None),
            P("dp", "tp"),
            P("tp", "dp"),
            P(("dp", "tp")),
            P("dp", "tp"),
            P("dp", "tp"),
            P("dp", "tp"),
            P("dp", "tp"),
            P("dp", "tp"),
            P(None, "tp"),
            P(None, "tp"),
            P(None, "tp"),
            P("tp"),
            P("tp"),
            P("tp"),
            P("tp"),
            P("tp", "dp"),
            P("dp", "tp"),
            P("dp", "tp"),
            P("dp", "tp"),
            P("tp", "dp"),
            P(("dp", "tp")),
            P("dp", "tp"),
            P("dp", "tp"),
            P("tp", "dp"),
        ),
        check_vma=False,
    )
```

```python
import functools

import jax
import jax.numpy as jnp
from jax import lax
from jax.experimental import pallas as pl
from jax.experimental.pallas import tpu as pltpu
from jax.sharding import PartitionSpec as P

f32 = jnp.float32
bf16 = jnp.bfloat16
eps = 1e-05
NST = 128
LOG2E = 1.4426950408889634
LOW = -1e30
NN = ((1,), (0,))
NT = ((1,), (1,))
TN = ((0,), (0,))
PROJ = 2048
STEPS = 8


def mm(a, b, dims=NN):
    return lax.dot_general(a, b, (dims, ((), ())), preferred_element_type=f32)


def mmx(a, b, dims=NN):
    return lax.dot_general(
        a, b, (dims, ((), ())), preferred_element_type=f32, precision=lax.Precision.HIGHEST
    )


def iota(shape, axis):
    return lax.broadcasted_iota(jnp.int32, shape, axis)


def expand(v):
    low_half = iota((1, 128), 1) < 64
    return jnp.concatenate(
        [
            jnp.where(low_half, v[:, h : h + 1], v[:, h + 1 : h + 2])
            for h in range(0, v.shape[1], 2)
        ],
        axis=1,
    )


def head_sum(v):
    owner = (iota((512, 8), 0) // 64 == iota((512, 8), 1)).astype(f32)
    return mmx(v, owner)


def softplus(v):
    return jnp.maximum(v, 0.0) + jnp.log1p(jnp.exp(-jnp.abs(v)))


def tile4(v):
    return jnp.concatenate([v, v, v, v], axis=1)


def fill_segments(seg_ref, segcol):
    length = seg_ref.shape[1]
    segcol[0:8, :] = jnp.full((8, 128), -1.0, f32)
    segcol[length + 8 : length + 16, :] = jnp.full((8, 128), -2.0, f32)
    for row in range(0, length, 128):
        piece = jnp.broadcast_to(seg_ref[0:1, row : row + 128], (128, 128))
        segcol[8 + row : 8 + row + 128, :] = piece.T


def taps_of(taps, tile):
    if tile < 4:
        return taps[0][:, tile * 128 : tile * 128 + 128]
    return taps[tile - 3][...]


def conv_masks(rows, segx):
    here = segx[8 : 8 + rows, :]
    return [(segx[8 - lag : 8 - lag + rows, :] == here).astype(f32) for lag in (1, 2, 3)]


def conv_pre(tile, rows, uext, masks, taps):
    lanes = slice(tile * 128, tile * 128 + 128)
    w = taps_of(taps, tile)
    lags = [uext[8 : 8 + rows, lanes]]
    for lag in (1, 2, 3):
        lags.append(uext[8 - lag : 8 - lag + rows, lanes] * masks[lag - 1])
    pre = lags[0] * w[0:1, :]
    for lag in (1, 2, 3):
        pre = pre + lags[lag] * w[lag : lag + 1, :]
    return pre, lags


def load_inputs(first, rows, proj, segcol, uext, segx):
    @pl.when(first == 0)
    def _():
        uext[0:8, :] = jnp.zeros((8, 768), f32)

    @pl.when(first > 0)
    def _():
        uext[0:8, :] = proj[pl.ds(pl.multiple_of(first - 16, 16), 16), 512:1280].astype(f32)[8:16]

    uext[8 : 8 + rows, :] = proj[pl.ds(first, rows), 512:1280].astype(f32)
    segx[...] = segcol[pl.ds(first, rows + 16), :]


def decays(first, rows, step, bias, rate):
    raw = step[pl.ds(first, rows), :] + bias[...]
    size = softplus(raw)
    logs = size * -jnp.exp(rate[...])
    scaled = logs * LOG2E
    lower = (iota((rows, rows), 0) >= iota((rows, rows), 1)).astype(f32)
    cum = mmx(lower, scaled)
    wide = jnp.concatenate([cum, jnp.zeros((rows, 120), f32)], axis=1)
    return raw, size, logs, cum, wide.T[0:8, :]


def half_masks():
    low_half = iota((1, 128), 1) < 64
    return low_half, jnp.logical_not(low_half)


def keep(mask, v):
    return jnp.where(mask, v, jnp.zeros_like(v))


def mixer_fwd_chunk(
    index, rows, proj, step, seg, segcol, taps, bias, rate, skip, gain, uext, segx, state,
    oacc, stats, mix_out, ssd_out, states_out, lse_out,
):
    first = pl.multiple_of(index * rows, rows)
    here = pl.ds(first, rows)
    halves = half_masks()
    load_inputs(first, rows, proj, segcol, uext, segx)
    masks = conv_masks(rows, segx)
    acts = []
    for tile in range(6):
        pre, _ = conv_pre(tile, rows, uext, masks, taps)
        acts.append(pre * jax.nn.sigmoid(pre))
    xc = jnp.concatenate(acts[0:4], axis=1)
    bc, cc = acts[4].astype(bf16), acts[5].astype(bf16)
    _, size, _, cum, cumr = decays(first, rows, step, bias, rate)
    segc = segx[8 : 8 + rows, :]
    before = segx[7:8, :]
    goes_on = (segc == before).astype(f32)
    segr = seg[0:1, here]
    wide_seg = jnp.concatenate([segc] * (rows // 128), axis=1)
    allowed = (iota((rows, rows), 0) >= iota((rows, rows), 1)) & (wide_seg == segr)
    away = jnp.where(allowed, 0.0, LOW)
    cb = mm(cc, bc, NT)
    xs = xc * expand(size)
    xsb = xs.astype(bf16)
    parts = []
    for pair in range(4):
        lhs = []
        for h in (2 * pair, 2 * pair + 1):
            gap = cum[:, h : h + 1] - cumr[h : h + 1, :] + away
            lhs.append((cb * jnp.exp2(gap)).astype(bf16))
        xp = xsb[:, pair * 128 : pair * 128 + 128]
        rhs = jnp.concatenate([keep(halves[0], xp), keep(halves[1], xp)], axis=0)
        parts.append(mm(jnp.concatenate(lhs, axis=1), rhs))
    ssd = jnp.concatenate(parts, axis=1) + xc * expand(skip[...])
    st = state[...]
    stb = st.astype(bf16)
    states_out[index] = stb
    ssd = ssd + mm(cc, stb) * expand(jnp.exp2(cum)) * tile4(goes_on)
    last = cum[rows - 1 : rows, :]
    fits = (segc == segc[rows - 1 : rows, :]).astype(f32)
    weight = expand(jnp.exp2(last - cum)) * tile4(fits)
    added = mm(bc, (xs * weight).astype(bf16), TN)
    passes = (segc[rows - 1 : rows, :] == before).astype(f32)
    state[...] = st * (expand(jnp.exp2(last)) * tile4(passes)) + added
    ssd_out[here, :] = ssd.astype(bf16)
    z = proj[here, 0:512].astype(f32)
    g = ssd * (z * jax.nn.sigmoid(z))
    r = lax.rsqrt(jnp.mean(g * g, axis=1, keepdims=True) + eps)
    mix_out[here, 0:512] = (g * r * gain[...]).astype(bf16)
    own_seg = seg[0:1, here]

    def keys(block, fresh):
        start = pl.multiple_of(block * rows, rows)
        away = attention_away(start, first, rows, own_seg, segcol)
        for pair in range(2):
            lanes = pair * 128
            q = proj[here, 1280 + lanes : 1408 + lanes] * jnp.asarray(0.125, bf16)
            k = proj[pl.ds(start, rows), 1536 + lanes : 1664 + lanes]
            v = proj[pl.ds(start, rows), 1792 + lanes : 1920 + lanes]
            for half in range(2):
                h = 2 * pair + half
                mine = slice(h * 64, h * 64 + 64)
                s = mm(k, keep(halves[half], q), NT) + away
                peak = jnp.max(s, axis=0, keepdims=True)
                if not fresh:
                    old = stats[h : h + 1, :]
                    peak = jnp.maximum(peak, old)
                    fade = jnp.exp(old - peak)
                p = jnp.exp(s - peak)
                total = jnp.sum(p, axis=0, keepdims=True)
                o = mm(v, p.astype(bf16), TN)[half * 64 : half * 64 + 64, :]
                if not fresh:
                    total = total + stats[h + 4 : h + 5, :] * fade
                    o = o + oacc[mine, :] * fade
                stats[h : h + 1, :] = peak
                stats[h + 4 : h + 5, :] = total
                oacc[mine, :] = o

    keys(index, True)

    def earlier(block, _):
        keys(block, False)
        return 0

    lax.fori_loop(0, index, earlier, 0)
    lse_out[0:4, here] = stats[0:4, :] + jnp.log(stats[4:8, :])
    for h in range(4):
        mine = slice(h * 64, h * 64 + 64)
        oacc[mine, :] = oacc[mine, :] * (1.0 / stats[h + 4 : h + 5, :])
    for pair in range(2):
        mine = slice(pair * 128, pair * 128 + 128)
        mix_out[here, 512 + pair * 128 : 640 + pair * 128] = oacc[mine, :].T.astype(bf16)


def attention_away(start, first, rows, own_seg, segcol):
    key_seg = segcol[pl.ds(start + 8, rows), :]
    wide = jnp.concatenate([key_seg] * (rows // 128), axis=1)
    allowed = (wide == own_seg) & (
        iota((rows, rows), 0) + start <= iota((rows, rows), 1) + first
    )
    return jnp.where(allowed, 0.0, LOW)


def mixer_bwd_chunk(
    index, rows, proj, step, seg, segcol, taps, bias, rate, skip, gain, uext, segx, dext,
    dstate, dkv, dqs, mix, ssd_in, states_in, lse_in, dmix, dproj, dstep, dtaps, dheads, dgain, dskip,
):
    first = pl.multiple_of(index * rows, rows)
    here = pl.ds(first, rows)
    halves = half_masks()
    load_inputs(first, rows, proj, segcol, uext, segx)
    masks = conv_masks(rows, segx)
    acts = []
    for tile in range(6):
        pre, _ = conv_pre(tile, rows, uext, masks, taps)
        acts.append(pre * jax.nn.sigmoid(pre))
    xc = jnp.concatenate(acts[0:4], axis=1)
    bc, cc = acts[4].astype(bf16), acts[5].astype(bf16)
    raw, size, logs, cum, cumr = decays(first, rows, step, bias, rate)
    z = proj[here, 0:512].astype(f32)
    ssd = ssd_in[here, :].astype(f32)
    dmo = dmix[here, 0:512].astype(f32)
    sig = jax.nn.sigmoid(z)
    act = z * sig
    g = ssd * act
    r = lax.rsqrt(jnp.mean(g * g, axis=1, keepdims=True) + eps)
    gain_part = jnp.sum(dmo * g * r, axis=0, keepdims=True)
    a = dmo * gain[...]
    dg = r * a - (r * r * r) * g * jnp.mean(a * g, axis=1, keepdims=True)
    dssd = dg * act
    dproj[here, 0:512] = (dg * ssd * (sig * (1.0 + z * (1.0 - sig)))).astype(bf16)
    skip_part = jnp.sum(dssd * xc, axis=0, keepdims=True)
    dxc = dssd * expand(skip[...])
    dyb = dssd.astype(bf16)
    wide_size = expand(size)
    xs = xc * wide_size
    xsb = xs.astype(bf16)
    segc = segx[8 : 8 + rows, :]
    before = segx[7:8, :]
    goes_on = (segc == before).astype(f32)
    segr = seg[0:1, here]
    wide_seg = jnp.concatenate([segc] * (rows // 128), axis=1)
    allowed = (iota((rows, rows), 0) <= iota((rows, rows), 1)) & (wide_seg == segr)
    away = jnp.where(allowed, 0.0, LOW)
    cbt = mm(bc, cc, NT)
    dcbt = jnp.zeros((rows, rows), f32)
    to_rows = []
    from_rows = jnp.zeros((rows, 8), f32)
    parts = []
    for pair in range(4):
        lanes = slice(pair * 128, pair * 128 + 128)
        lhs, rhs = [], []
        for half in range(2):
            h = 2 * pair + half
            lt = jnp.exp2(cumr[h : h + 1, :] - cum[:, h : h + 1] + away)
            mt = cbt * lt
            lhs.append(mt.astype(bf16))
            rhs.append(keep(halves[half], dyb[:, lanes]))
            dl = mm(keep(halves[half], xsb[:, lanes]), dyb[:, lanes], NT)
            dcbt = dcbt + dl * lt
            gt = dl * mt
            to_rows.append(jnp.sum(gt, axis=0, keepdims=True))
            from_rows = jnp.where(
                iota((1, 8), 1) == h, jnp.sum(gt, axis=1, keepdims=True), from_rows
            )
        parts.append(mm(jnp.concatenate(lhs, axis=1), jnp.concatenate(rhs, axis=0)))
    dxs = jnp.concatenate(parts, axis=1)
    dcb = dcbt.astype(bf16)
    db = mm(dcb, cc)
    dc = mm(dcb, bc, TN)
    upper = (iota((rows, rows), 0) <= iota((rows, rows), 1)).astype(f32)
    late = -from_rows
    reach = expand(jnp.exp2(cum)) * tile4(goes_on)
    stb = states_in[index]
    dye = dssd * reach
    dyeb = dye.astype(bf16)
    dc = dc + mm(dyeb, stb, NT)
    late = late + head_sum(dye * mm(cc, stb))
    into_state = mm(cc, dyeb, TN)
    last = cum[rows - 1 : rows, :]
    fits = (segc == segc[rows - 1 : rows, :]).astype(f32)
    weight = expand(jnp.exp2(last - cum)) * tile4(fits)
    dst = dstate[...]
    dsb = dst.astype(bf16)
    dxi = mm(bc, dsb) * weight
    dxs = dxs + dxi
    db = db + mm((xs * weight).astype(bf16), dsb, NT)
    strict = (iota((rows, rows), 0) > iota((rows, rows), 1)).astype(f32)
    dlog = mmx(strict, head_sum(xs * dxi))
    passes = (segc[rows - 1 : rows, :] == before).astype(f32)
    fade = expand(jnp.exp2(last)) * tile4(passes)
    through = jnp.sum(stb.astype(f32) * dst, axis=0, keepdims=True) * fade
    dlog = dlog + head_sum(jnp.broadcast_to(through, (8, 512)))[0:1, :]
    dstate[...] = dst * fade + into_state
    dlog = dlog + mmx(upper, late) + mmx(upper, jnp.concatenate(to_rows, axis=0), NT)
    dsize = head_sum(dxs * xc) - dlog * jnp.exp(rate[...])
    rate_part = jnp.sum(dlog * logs, axis=0, keepdims=True)
    draw = dsize * jax.nn.sigmoid(raw)
    bias_part = jnp.sum(draw, axis=0, keepdims=True)
    dstep[here, :] = draw.astype(dstep.dtype)
    dxc = dxc + dxs * wide_size
    dacts = [dxc[:, t * 128 : t * 128 + 128] for t in range(4)] + [db, dc]
    dext[rows : rows + 8, :] = dext[0:8, :]
    ahead = [(segx[8 + lag : 8 + lag + rows, :] == segc).astype(f32) for lag in (1, 2, 3)]
    for tile in range(6):
        lanes = slice(tile * 128, tile * 128 + 128)
        w = taps_of(taps, tile)
        pre, lags = conv_pre(tile, rows, uext, masks, taps)
        sig = jax.nn.sigmoid(pre)
        dpre = dacts[tile] * (sig * (1.0 + pre * (1.0 - sig)))
        dext[0:rows, lanes] = dpre
        du = dpre * w[0:1, :]
        for lag in (1, 2, 3):
            du = du + dext[lag : lag + rows, lanes] * ahead[lag - 1] * w[lag : lag + 1, :]
        dproj[here, 512 + tile * 128 : 640 + tile * 128] = du.astype(bf16)
        sums = jnp.concatenate(
            [jnp.sum(dpre * shifted, axis=0, keepdims=True) for shifted in lags], axis=0
        )
        dtaps[:, lanes] = dtaps[:, lanes] + sums
    head_parts = jnp.concatenate([bias_part, rate_part], axis=0)
    dheads[...] = dheads[...] + head_parts
    dgain[...] = dgain[...] + gain_part
    dskip[...] = dskip[...] + skip_part
    own_seg = seg[0:1, here]
    dos = [dmix[here, 512 + pair * 128 : 640 + pair * 128] for pair in range(2)]
    owner = (iota((8, 256), 1) // 64 == iota((8, 256), 0)).astype(f32)
    delta = mmx(
        owner,
        jnp.concatenate(dos, axis=1).astype(f32) * mix[here, 512:768].astype(f32),
        NT,
    )
    dqs[...] = jnp.zeros_like(dqs)

    def keys(block, _):
        start = pl.multiple_of(block * rows, rows)
        there = pl.ds(start, rows)
        away = attention_away(start, first, rows, own_seg, segcol)
        for pair in range(2):
            lanes = pair * 128
            q = proj[here, 1280 + lanes : 1408 + lanes] * jnp.asarray(0.125, bf16)
            k = proj[there, 1536 + lanes : 1664 + lanes]
            v = proj[there, 1792 + lanes : 1920 + lanes]
            ps, dss, qms, doms = [], [], [], []
            for half in range(2):
                h = 2 * pair + half
                mine = slice(h * 64, h * 64 + 64)
                qm, dom = keep(halves[half], q), keep(halves[half], dos[pair])
                p = jnp.exp(mm(k, qm, NT) + away - lse_in[h : h + 1, here])
                dp = mm(v, dom, NT)
                ds = (p * (dp - delta[h : h + 1, :])).astype(bf16)
                dqs[mine, :] = dqs[mine, :] + mm(k, ds, TN)[half * 64 : half * 64 + 64, :]
                ps.append(p.astype(bf16))
                dss.append(ds)
                qms.append(qm)
                doms.append(dom)
            kl, vl = slice(lanes, lanes + 128), slice(256 + lanes, 384 + lanes)
            dkv[there, kl] = dkv[there, kl] + mm(
                jnp.concatenate(dss, axis=1), jnp.concatenate(qms, axis=0)
            )
            dkv[there, vl] = dkv[there, vl] + mm(
                jnp.concatenate(ps, axis=1), jnp.concatenate(doms, axis=0)
            )
        return 0

    lax.fori_loop(0, index + 1, keys, 0)
    for pair in range(2):
        mine = slice(pair * 128, pair * 128 + 128)
        dproj[here, 1280 + pair * 128 : 1408 + pair * 128] = (dqs[mine, :] * 0.125).T.astype(bf16)
    dproj[here, 1536:2048] = dkv[here, :].astype(bf16)


def fwd_kernel(count, proj, step, seg, t0, t1, t2, bias, rate, skip, gain,
               mix_out, ssd_out, states_out, lse_out, segcol, uext, segx, state, oacc, stats):
    rows = proj.shape[0] // count
    fill_segments(seg, segcol)
    lse_out[...] = jnp.zeros_like(lse_out)
    state[...] = jnp.zeros_like(state)

    def chunk(index, _):
        mixer_fwd_chunk(index, rows, proj, step, seg, segcol, (t0, t1, t2), bias, rate, skip,
                        gain, uext, segx, state, oacc, stats, mix_out, ssd_out, states_out,
                        lse_out)
        return 0

    lax.fori_loop(0, count, chunk, 0)


def bwd_kernel(count, proj, step, seg, t0, t1, t2, bias, rate, skip, gain, mix, ssd_in,
               states_in, lse_in, dmix, dproj, dstep, dtaps, dheads, dgain, dskip,
               segcol, uext, segx, dext, dstate, dkv, dqs):
    rows = proj.shape[0] // count
    fill_segments(seg, segcol)
    for ref in (dtaps, dheads, dgain, dskip, dstate, dkv):
        ref[...] = jnp.zeros_like(ref)
    dext[0:8, :] = jnp.zeros((8, 768), f32)

    def chunk(turn, _):
        mixer_bwd_chunk(count - 1 - turn, rows, proj, step, seg, segcol, (t0, t1, t2), bias,
                        rate, skip, gain, uext, segx, dext, dstate, dkv, dqs, mix, ssd_in,
                        states_in, lse_in, dmix, dproj, dstep, dtaps, dheads, dgain, dskip)
        return 0

    lax.fori_loop(0, count, chunk, 0)
    dskip8 = head_sum(jnp.broadcast_to(dskip[...], (8, 512)))
    dskip[0:1, 0:8] = dskip8[0:1, :]


def mixer_fwd(count, proj, step, seg, taps, bias, rate, skip, gain):
    length = proj.shape[0]
    rows = length // count
    return pl.pallas_call(
        functools.partial(fwd_kernel, count),
        out_shape=(
            jax.ShapeDtypeStruct((length, 768), bf16),
            jax.ShapeDtypeStruct((length, 512), bf16),
            jax.ShapeDtypeStruct((count, NST, 512), bf16),
            jax.ShapeDtypeStruct((8, length), f32),
        ),
        scratch_shapes=[
            pltpu.VMEM((length + 16, 128), f32),
            pltpu.VMEM((rows + 8, 768), f32),
            pltpu.VMEM((rows + 16, 128), f32),
            pltpu.VMEM((NST, 512), f32),
            pltpu.VMEM((256, rows), f32),
            pltpu.VMEM((8, rows), f32),
        ],
        compiler_params=pltpu.CompilerParams(vmem_limit_bytes=60 * 2**20),
    )(proj, step, seg, *taps, bias, rate, skip, gain)


def mixer_bwd(count, proj, step, seg, taps, bias, rate, skip, gain, mix, ssd, states, lse, dmix):
    length = proj.shape[0]
    rows = length // count
    return pl.pallas_call(
        functools.partial(bwd_kernel, count),
        out_shape=(
            jax.ShapeDtypeStruct((length, 2048), bf16),
            jax.ShapeDtypeStruct((length, 8), bf16),
            jax.ShapeDtypeStruct((4, 768), f32),
            jax.ShapeDtypeStruct((2, 8), f32),
            jax.ShapeDtypeStruct((1, 512), f32),
            jax.ShapeDtypeStruct((1, 512), f32),
        ),
        scratch_shapes=[
            pltpu.VMEM((length + 16, 128), f32),
            pltpu.VMEM((rows + 8, 768), f32),
            pltpu.VMEM((rows + 16, 128), f32),
            pltpu.VMEM((rows + 8, 768), f32),
            pltpu.VMEM((NST, 512), f32),
            pltpu.VMEM((length, 512), f32),
            pltpu.VMEM((256, rows), f32),
        ],
        compiler_params=pltpu.CompilerParams(vmem_limit_bytes=60 * 2**20),
    )(proj, step, seg, *taps, bias, rate, skip, gain, mix, ssd, states, lse, dmix)


MESH = pl.DeviceIdType.MESH


class Line:
    def __init__(self, scratch, size, hop=1):
        self.hop = hop
        (self.own, self.left, self.right, self.full, self.acc,
         self.ss, self.sr, self.gs, self.gr) = scratch
        self.size = size
        self.steps = self.own.shape[1]
        self.me = lax.axis_index("tp")
        self.last = size - 1

    @staticmethod
    def scratch(size, steps, sub, width):
        return [
            pltpu.VMEM((size, steps, sub, width), f32),
            pltpu.VMEM((size, steps, sub, width), bf16),
            pltpu.VMEM((size, steps, sub, width), bf16),
            pltpu.VMEM((size, steps, sub, width), bf16),
            pltpu.VMEM((sub, width), f32),
            pltpu.SemaphoreType.DMA((2, size, steps)),
            pltpu.SemaphoreType.DMA((2, size, steps)),
            pltpu.SemaphoreType.DMA((2, size, steps)),
            pltpu.SemaphoreType.DMA((2, size, steps)),
        ]

    def sum_copy(self, way, d, j):
        buf = self.left if way == 0 else self.right
        return pltpu.make_async_remote_copy(
            src_ref=buf.at[d, j],
            dst_ref=buf.at[d, j],
            send_sem=self.ss.at[way, d, j],
            recv_sem=self.sr.at[way, d, j],
            device_id={"tp": self.me + 1 if way == 0 else self.me - 1},
            device_id_type=MESH,
        )

    def row_copy(self, way, d, j):
        return pltpu.make_async_remote_copy(
            src_ref=self.full.at[d, j],
            dst_ref=self.full.at[d, j],
            send_sem=self.gs.at[way, d, j],
            recv_sem=self.gr.at[way, d, j],
            device_id={"tp": self.me + 1 if way == 0 else self.me - 1},
            device_id_type=MESH,
        )

    def enter(self):
        barrier = pltpu.get_barrier_semaphore()
        me, last = self.me, self.last

        @pl.when(me > 0)
        def _():
            pl.semaphore_signal(barrier, inc=1, device_id={"tp": me - 1}, device_id_type=MESH)

        @pl.when(me < last)
        def _():
            pl.semaphore_signal(barrier, inc=1, device_id={"tp": me + 1}, device_id_type=MESH)

        peers = jnp.where(me > 0, 1, 0) + jnp.where(me < last, 1, 0)
        pl.semaphore_wait(barrier, peers)

    def relay(self, way, j):
        me, last = self.me, self.last
        buf = self.left if way == 0 else self.right
        first_one = me == 0 if way == 0 else me == last

        def one(d, _):
            @pl.when(first_one)
            def _():
                buf[d, j] = self.own[d, j].astype(bf16)

            @pl.when(jnp.logical_not(first_one))
            def _():
                self.sum_copy(way, d, j).wait_recv()
                buf[d, j] = (buf[d, j].astype(f32) + self.own[d, j]).astype(bf16)

            self.sum_copy(way, d, j).start()
            return 0

        if way == 0:
            lax.fori_loop(me + 1, self.size, one, 0)
        else:
            lax.fori_loop(0, me, one, 0)

    def settle(self, j, finish):
        me, last = self.me, self.last
        self.acc[...] = self.own[me, j]

        @pl.when(me > 0)
        def _():
            self.sum_copy(0, me, j).wait_recv()
            self.acc[...] = self.acc[...] + self.left[me, j].astype(f32)

        @pl.when(me < last)
        def _():
            self.sum_copy(1, me, j).wait_recv()
            self.acc[...] = self.acc[...] + self.right[me, j].astype(f32)

        self.full[me, j] = finish(j, self.acc[...])

        @pl.when(me < last)
        def _():
            self.row_copy(0, me, j).start()

        @pl.when(me > 0)
        def _():
            self.row_copy(1, me, j).start()

    def inside(self, j):
        return jnp.logical_and(j >= 0, j < self.steps)

    def pass_on(self, i):
        me, last = self.me, self.last

        def from_left(d, _):
            j = i - self.hop * (jnp.maximum(d, last - d) + me - d)

            @pl.when(self.inside(j))
            def _():
                self.row_copy(0, d, j).wait_recv()

                @pl.when(me < last)
                def _():
                    self.row_copy(0, d, j).start()

            return 0

        def from_right(d, _):
            j = i - self.hop * (jnp.maximum(d, last - d) + d - me)

            @pl.when(self.inside(j))
            def _():
                self.row_copy(1, d, j).wait_recv()

                @pl.when(me > 0)
                def _():
                    self.row_copy(1, d, j).start()

            return 0

        lax.fori_loop(0, me, from_left, 0)
        lax.fori_loop(me + 1, self.size, from_right, 0)

    def move(self, i, finish):
        me, last = self.me, self.last
        right_step = i - self.hop * me
        left_step = i - self.hop * (last - me)
        final_step = i - self.hop * jnp.maximum(me, last - me)

        @pl.when(self.inside(right_step))
        def _():
            self.relay(0, right_step)

        @pl.when(self.inside(left_step))
        def _():
            self.relay(1, left_step)

        @pl.when(self.inside(final_step))
        def _():
            self.settle(final_step, finish)

        self.pass_on(i)

    def ready_step(self, i):
        return i - self.hop * (self.last + jnp.maximum(self.me, self.last - self.me))

    def lag(self):
        return 2 * self.hop * self.last

    def leave(self):
        me, last = self.me, self.last

        def step(j, _):
            def right_sums(d, _):
                self.sum_copy(0, d, j).wait_send()
                return 0

            def left_sums(d, _):
                self.sum_copy(1, d, j).wait_send()
                return 0

            def right_rows(d, _):
                self.row_copy(0, d, j).wait_send()
                return 0

            def left_rows(d, _):
                self.row_copy(1, d, j).wait_send()
                return 0

            lax.fori_loop(me + 1, self.size, right_sums, 0)
            lax.fori_loop(0, me, left_sums, 0)

            @pl.when(me < last)
            def _():
                lax.fori_loop(0, me + 1, right_rows, 0)

            @pl.when(me > 0)
            def _():
                lax.fori_loop(me, self.size, left_rows, 0)

            return 0

        lax.fori_loop(0, self.steps, step, 0)


def flat(v):
    return v.reshape(v.shape[0] * v.shape[1], v.shape[2])


def normed(v, gain):
    return v * lax.rsqrt(jnp.mean(v * v, axis=1, keepdims=True) + eps) * gain


def normed_back(grad, v, gain):
    r = lax.rsqrt(jnp.mean(v * v, axis=1, keepdims=True) + eps)
    a = grad * gain
    back = r * a - (r * r * r) * v * jnp.mean(a * v, axis=1, keepdims=True)
    return back, jnp.sum(grad * v * r, axis=0, keepdims=True)


def embed_kernel(size, patches, embed, keep_rows, gain, wz, wx, wb, wc, wq, wk, wv, ws,
                 resid_out, full_out, proj_out, step_out, *scratch):
    line = Line(scratch, size)
    steps, sub = line.steps, line.own.shape[2]
    columns = []
    for ref in (wz, wx, wb, wc, wq, wk, wv):
        columns.append((ref, sum(c[0].shape[1] for c in columns)))

    def produce(j):
        line.own[:, j] = mm(flat(patches[:, j]), embed[...]).reshape(size, sub, line.own.shape[3])

    def finish(j, total):
        rows = total * keep_rows[j]
        resid_out[j] = rows
        return normed(rows, gain[...]).astype(bf16)

    def consume(j):
        x = line.full[:, j]
        full_out[:, j] = x
        x = flat(x)
        for ref, start in columns:
            width = ref.shape[1]
            proj_out[:, j, :, start : start + width] = (
                mm(x, ref[...]).astype(bf16).reshape(size, sub, width)
            )
        step_out[:, j] = mm(x, ws[...]).reshape(size, sub, ws.shape[1])

    line.enter()
    produce(0)

    def iteration(i, _):
        line.move(i, finish)

        @pl.when(i + 1 < steps)
        def _():
            produce(i + 1)

        ready = line.ready_step(i)

        @pl.when(line.inside(ready))
        def _():
            consume(ready)

        return 0

    lax.fori_loop(0, steps + line.lag(), iteration, 0)
    line.leave()


def ffn_kernel(size, mix, wmo, wao, resid_one, gain, wg, wu, wd, og_low, og_high, og_mine,
               resid_grad, ffn_out, resid_out, dmix, grads, gain_grad, hidden_all, gg_all, ug_all,
               *scratch):
    half = len(scratch) // 2
    one, two = Line(scratch[:half], size), Line(scratch[half:], size)
    steps, sub, width = one.steps, one.own.shape[2], one.own.shape[3]
    length = size * steps * sub
    inner, mixed, units = wmo.shape[0], mix.shape[3], wg.shape[1]
    group = 256
    groups = width // group

    def shaped(v):
        return v.reshape(size, sub, v.shape[1])

    def all_rows(v):
        return v.reshape(length, v.shape[3])

    def produce(j):
        x = flat(mix[:, j])
        one.own[:, j] = shaped(mm(x[:, 0:inner], wmo[...]) + mm(x[:, inner:], wao[...]))

    def finish_one(j, total):
        rows = resid_one[j] + total
        resid_out[j] = rows
        return normed(rows, gain[...]).astype(bf16)

    def middle(j, og):
        x = flat(one.full[:, j])
        gate, up = mm(x, wg[...]), mm(x, wu[...])
        hg = mm(og, wd[...], NT)
        sig = jax.nn.sigmoid(gate)
        act = gate * sig
        hidden = (act * up).astype(bf16)
        gg = (hg * up * (sig * (1.0 + gate * (1.0 - sig)))).astype(bf16)
        ug = (hg * act).astype(bf16)
        hidden_all[:, j] = shaped(hidden)
        gg_all[:, j] = shaped(gg)
        ug_all[:, j] = shaped(ug)
        two.own[:, j] = shaped(mm(gg, wg[...], NT) + mm(ug, wu[...], NT))
        ffn_out[:, j] = shaped(mm(hidden, wd[...]).astype(bf16))

    def finish_two(j, total):
        back, part = normed_back(total, resid_out[j], gain[...])
        rows = og_mine[j].astype(f32) + back
        resid_grad[j] = rows
        gain_grad[...] = gain_grad[...] + part
        return rows.astype(bf16)

    def consume(j):
        x = flat(two.full[:, j])
        dmix[:, j, :, 0:inner] = shaped(mm(x, wmo[...], NT).astype(bf16))
        dmix[:, j, :, inner:] = shaped(mm(x, wao[...], NT).astype(bf16))

    def columns(ref, g):
        return all_rows(ref[:, :, :, pl.ds(pl.multiple_of(g * group, group), group)])

    def ffn_grads(g):
        here = pl.ds(pl.multiple_of(g * group, group), group)
        x = columns(one.full, g)
        grads[here, 0:units] = mm(x, all_rows(gg_all[...]), TN).astype(bf16)
        grads[here, units : 2 * units] = mm(x, all_rows(ug_all[...]), TN).astype(bf16)
        half_steps = steps // 2
        hidden = hidden_all[...]
        total = None
        for part, og in enumerate((og_low, og_high)):
            cols = og[:, :, :, pl.ds(pl.multiple_of(g * group, group), group)]
            cols = cols.reshape(length // 2, group)
            rows = hidden[:, part * half_steps : (part + 1) * half_steps]
            term = mm(cols, rows.reshape(length // 2, units), TN)
            total = term if total is None else total + term
        grads[here, 2 * units + mixed :] = total.astype(bf16)

    def mix_grads(g, _):
        here = pl.ds(pl.multiple_of(g * group, group), group)
        grads[here, 2 * units : 2 * units + mixed] = mm(
            columns(two.full, g), all_rows(mix[...]), TN
        ).astype(bf16)
        return 0

    one.enter()
    gain_grad[...] = jnp.zeros_like(gain_grad)
    produce(0)
    lag = one.lag() + 1

    def iteration(i, _):
        one.move(i, finish_one)
        two.move(i - lag, finish_two)

        @pl.when(i + 1 < steps)
        def _():
            produce(i + 1)

        ready_one = one.ready_step(i)

        @pl.when(jnp.logical_and(ready_one >= 0, ready_one < steps // 2))
        def _():
            middle(ready_one, flat(og_low[:, ready_one]))

        @pl.when(jnp.logical_and(ready_one >= steps // 2, ready_one < steps))
        def _():
            middle(ready_one, flat(og_high[:, ready_one - steps // 2]))

        ready_two = two.ready_step(i - lag)

        @pl.when(two.inside(ready_two))
        def _():
            consume(ready_two)

        turn = i - (steps + lag)

        @pl.when(jnp.logical_and(turn >= 0, turn < groups))
        def _():
            ffn_grads(turn)

        return 0

    lax.fori_loop(0, steps + lag + two.lag(), iteration, 0)
    lax.fori_loop(0, groups, mix_grads, 0)
    one.leave()
    two.leave()


def comm_call(body, out_shape, scratch, identity, *args):
    return pl.pallas_call(
        body,
        out_shape=out_shape,
        in_specs=[pl.BlockSpec(memory_space=pltpu.VMEM)] * len(args),
        out_specs=tuple(pl.BlockSpec(memory_space=pltpu.VMEM) for _ in out_shape),
        scratch_shapes=scratch,
        compiler_params=pltpu.CompilerParams(
            collective_id=identity, has_side_effects=True, vmem_limit_bytes=62 * 2**20
        ),
    )(*args)


def sds(shape, kind):
    return jax.ShapeDtypeStruct(shape, kind)


class Halving:
    def __init__(self, data, got, ss, sr):
        self.data, self.got, self.ss, self.sr = data, got, ss, sr
        self.count, self.rows = data.shape[0], data.shape[1]
        self.bits = self.count.bit_length() - 1
        self.me = lax.axis_index("dp")
        plain = list(range(self.bits))
        other = plain if self.bits < 3 else [0, 2, 1] + plain[3:]
        self.orders = (plain, other)

    @staticmethod
    def scratch(count, rows, columns):
        spare = max(count - 1, 1)
        return [
            pltpu.VMEM((count, rows, columns), bf16),
            pltpu.VMEM((spare, rows, columns), bf16),
            pltpu.SemaphoreType.DMA((2, spare)),
            pltpu.SemaphoreType.DMA((2, spare)),
        ]

    def bit(self, b):
        return lax.rem(self.me // 2**b, 2)

    def block(self, half, stage, e, theirs):
        order = self.orders[half]
        place = 0
        for b in order[:stage]:
            place = place + self.bit(b) * 2**b
        b = order[stage]
        place = place + (1 - self.bit(b) if theirs else self.bit(b)) * 2**b
        for t, b in enumerate(sorted(order[stage + 1 :])):
            place = place + lax.rem(e // 2**t, 2) * 2**b
        return place

    def open(self, stage):
        return 2 ** (self.bits - 1 - stage)

    def slot(self, stage, e):
        return sum(self.open(s) for s in range(stage)) + e

    def part(self, half):
        rows = self.rows // 2
        return pl.ds(half * rows, rows)

    def copy(self, half, stage, e):
        b = self.orders[half][stage]
        slot = self.slot(stage, e)
        return pltpu.make_async_remote_copy(
            src_ref=self.data.at[self.block(half, stage, e, True), self.part(half)],
            dst_ref=self.got.at[slot, self.part(half)],
            send_sem=self.ss.at[half, slot],
            recv_sem=self.sr.at[half, slot],
            device_id={"dp": self.me + (1 - 2 * self.bit(b)) * 2**b},
            device_id_type=MESH,
        )

    def start(self, stage, low=0, high=None):
        def one(e, _):
            self.copy(0, stage, e).start()
            self.copy(1, stage, e).start()
            return 0

        lax.fori_loop(low, self.open(stage) if high is None else high, one, 0)

    def finish(self, stage):
        def one(e, _):
            for half in range(2):
                self.copy(half, stage, e).wait_recv()
                place, part = self.block(half, stage, e, False), self.part(half)
                got = self.got[self.slot(stage, e), part]
                self.data[place, part] = (self.data[place, part].astype(f32) + got.astype(f32)).astype(bf16)
            return 0

        lax.fori_loop(0, self.open(stage), one, 0)

    def leave(self):
        for stage in range(self.bits):

            def one(e, _, stage=stage):
                self.copy(0, stage, e).wait_send()
                self.copy(1, stage, e).wait_send()
                return 0

            lax.fori_loop(0, self.open(stage), one, 0)


class Doubling:
    def __init__(self, parts, got, ss, sr, dp, tp):
        self.parts, self.got, self.ss, self.sr = parts, got, ss, sr
        self.hops = [("dp", b) for b in range(dp.bit_length() - 1)]
        self.hops += [("tp", b) for b in range(tp.bit_length() - 1)]

    @staticmethod
    def scratch(dp, tp, rows, columns):
        hops = dp.bit_length() + tp.bit_length() - 2
        return [
            pltpu.VMEM((hops + 1, rows, columns), f32),
            pltpu.VMEM((hops, rows, columns), f32),
            pltpu.SemaphoreType.DMA((hops,)),
            pltpu.SemaphoreType.DMA((hops,)),
        ]

    def copy(self, hop):
        axis, b = self.hops[hop]
        me = lax.axis_index(axis)
        flip = (1 - 2 * lax.rem(me // 2**b, 2)) * 2**b
        return pltpu.make_async_remote_copy(
            src_ref=self.parts.at[hop],
            dst_ref=self.got.at[hop],
            send_sem=self.ss.at[hop],
            recv_sem=self.sr.at[hop],
            device_id={axis: me + flip},
            device_id_type=MESH,
        )

    def start(self, hop):
        self.copy(hop).start()

    def finish(self, hop):
        self.copy(hop).wait_recv()
        self.parts[hop + 1] = self.parts[hop] + self.got[hop]

    def leave(self):
        for hop in range(len(self.hops)):
            self.copy(hop).wait_send()


def enter_both(dp, tp):
    barrier = pltpu.get_barrier_semaphore()
    me_t, me_d = lax.axis_index("tp"), lax.axis_index("dp")
    for away in range(1, tp):
        pl.semaphore_signal(
            barrier, inc=1, device_id={"tp": lax.rem(me_t + away, tp)}, device_id_type=MESH
        )
    bits = dp.bit_length() - 1
    for b in range(bits):
        flip = (1 - 2 * lax.rem(me_d // 2**b, 2)) * 2**b
        pl.semaphore_signal(barrier, inc=1, device_id={"dp": me_d + flip}, device_id_type=MESH)
    pl.semaphore_wait(barrier, tp - 1 + bits)


def entry_kernel(size, dp, dproj, dstep, wz, wx, wb, wc, wq, wk, wv, ws, resid_one, gain, resid_grad,
                 keep_rows, embed, full_one, patches, dtaps, dheads, dgain, dskip, two_gain_grad,
                 patch_grad, embed_out, in_out, small_out, *scratch):
    line = Line(scratch[0:9], size)
    ins = Halving(*scratch[9:13])
    emb = Halving(*scratch[13:17])
    small = Doubling(*scratch[17:21], dp, size)
    steps, sub, width = line.steps, line.own.shape[2], line.own.shape[3]
    length = size * steps * sub
    weights = (wz, wx, wb, wc, wq, wk, wv)
    columns = []
    for ref in weights:
        columns.append((ref, sum(c[0].shape[1] for c in columns)))
    group = 256
    groups = width // group
    in_group = group // ins.rows

    def all_rows(v):
        return v.reshape(length, v.shape[3])

    def produce(j):
        total = mm(flat(dstep[:, j]), ws[...], NT)
        for ref, start in columns:
            total = total + mm(flat(dproj[:, j, :, start : start + ref.shape[1]]), ref[...], NT)
        line.own[:, j] = total.reshape(size, sub, width)

    def finish(j, total):
        back, part = normed_back(total, resid_one[j], gain[...])
        small.parts[0, 9:10] = small.parts[0, 9:10] + part
        return ((resid_grad[j] + back) * keep_rows[j]).astype(bf16)

    def consume(d, _):
        x = flat(line.full[d])
        patch_grad[d] = mm(x, embed[...], NT).astype(bf16).reshape(steps, sub, embed.shape[0])
        return 0

    def weight_group(g):
        x = all_rows(full_one[:, :, :, pl.ds(pl.multiple_of(g * group, group), group)])
        here = pl.ds(g * in_group, in_group)
        grad = mm(x, all_rows(dproj[...]), TN).astype(bf16)
        ins.data[here, :, 0:PROJ] = grad.reshape(in_group, ins.rows, PROJ)
        grad = mm(x, all_rows(dstep[...]), TN).astype(bf16)
        grad = jnp.concatenate([grad, jnp.zeros((group, 120), bf16)], axis=1)
        ins.data[here, :, PROJ:] = grad.reshape(in_group, ins.rows, 128)
        if ins.bits:
            ins.start(0, g * in_group // 2, (g + 1) * in_group // 2)

    def embed_group(g):
        x = all_rows(line.full[:, :, :, pl.ds(pl.multiple_of(g * group, group), group)])
        grad = mm(x, all_rows(patches[...]), TN).astype(bf16)
        emb.data[pl.ds(g * in_group, in_group)] = grad.reshape(
            in_group, emb.rows, grad.shape[1]
        )
        if emb.bits:
            emb.start(0, g * in_group // 2, (g + 1) * in_group // 2)

    enter_both(dp, size)
    first = jnp.zeros((16, width), f32)
    small.parts[0] = first
    small.parts[0, 0:4, 0:768] = dtaps[...]
    small.parts[0, 4:5, 0:512] = dgain[...]
    small.parts[0, 5:6, 0:512] = dskip[...]
    small.parts[0, 6:8, 0:8] = dheads[...]
    small.parts[0, 8:9] = two_gain_grad[...]
    produce(0)

    def iteration(i, _):
        line.move(i, finish)

        @pl.when(i + 1 < steps)
        def _():
            produce(i + 1)

        @pl.when(i < groups)
        def _():
            weight_group(i)

        for stage in range(ins.bits):

            @pl.when(i == groups + (8 * stage) // max(ins.bits - 1, 1))
            def _(stage=stage):
                ins.finish(stage)
                if stage + 1 < ins.bits:
                    ins.start(stage + 1)

        return 0

    lax.fori_loop(0, steps + line.lag(), iteration, 0)
    small.start(0)

    def each_group(g, _):
        embed_group(g)
        return 0

    lax.fori_loop(0, groups, each_group, 0)
    lax.fori_loop(0, size, consume, 0)
    in_out[...] = ins.data[ins.me]
    hops = len(small.hops)
    for turn in range(max(hops, emb.bits)):
        if turn < hops:
            small.finish(turn)
            if turn + 1 < hops:
                small.start(turn + 1)
        if turn < emb.bits:
            emb.finish(turn)
            if turn + 1 < emb.bits:
                emb.start(turn + 1)
    small_out[0:8] = small.parts[dp.bit_length() - 1, 0:8]
    small_out[8:16] = small.parts[hops, 8:16]
    embed_out[...] = emb.data[emb.me]
    line.leave()
    ins.leave()
    emb.leave()
    small.leave()


def last_kernel(patch_in, embed_in, ins, mids, small, resid, ffn, place, patch_out, result,
                embed_out, gz, gx, gb, gc, gq, gk, gv, gs, t0, t1, t2, hb, hr, hs, inner_gain,
                gmo, gao, ggate, gup, gdown, gain_one, gain_two, sem):
    move = pltpu.make_async_copy(patch_in, patch_out, sem)
    move.start()
    result[...] = (resid[...] + ffn[...].astype(f32)).astype(bf16)
    start = 0
    for out in (gz, gx, gb, gc, gq, gk, gv, gs):
        out[...] = ins[:, start : start + out.shape[1]].astype(f32)
        start = start + out.shape[1]
    units, inner = ggate.shape[1], t0.shape[1]
    ggate[...] = mids[:, 0:units].astype(f32)
    gup[...] = mids[:, units : 2 * units].astype(f32)
    flipped = mids[:, 2 * units :].astype(f32)
    outs = ((gmo, flipped[:, 0:inner]), (gao, flipped[:, inner : flipped.shape[1] - units]),
            (gdown, flipped[:, flipped.shape[1] - units :]), (embed_out, embed_in[...].astype(f32)))
    for out, value in outs:
        out[...] = value.T if out.shape != value.shape else value
    t0[...] = small[0:4, 0 : t0.shape[1]]
    t1[...] = small[0:4, t0.shape[1] : t0.shape[1] + t1.shape[1]]
    t2[...] = small[0:4, t0.shape[1] + t1.shape[1] : t0.shape[1] + 2 * t1.shape[1]]
    hb[...] = small[6:7, 0 : hb.shape[1]]
    hr[...] = small[7:8, 0 : hr.shape[1]]
    hs[...] = small[5:6, 0 : hs.shape[1]]
    inner_gain[...] = small[4:5, 0 : inner_gain.shape[1]]
    width, share = small.shape[1], gain_one.shape[1]
    chosen = (iota((width, share), 0) == iota((width, share), 1) + place[0] * share).astype(f32)
    gains = mmx(small[8:16, :], chosen)
    gain_two[...] = gains[0:1, :]
    gain_one[...] = gains[1:2, :]
    move.wait()


def shards(
    patches,
    keep_mask,
    segments,
    embed_weight,
    first_gain,
    mamba_gate,
    mamba_input,
    state_in,
    state_out,
    step_weight,
    conv_input,
    conv_statein,
    conv_stateout,
    step_bias,
    rate_log,
    skip_gain,
    inner_gain,
    mamba_output,
    query_weight,
    key_weight,
    value_weight,
    attn_output,
    second_gain,
    ffn_gate,
    ffn_up,
    ffn_down,
    out_grad,
):
    size = lax.axis_size("tp")
    segment = segments[0]
    length = patches.shape[0]
    mine = length // size
    sub = mine // STEPS
    shape = (size, STEPS, sub)
    width = embed_weight.shape[1]
    keep_rows = keep_mask.astype(f32).reshape(STEPS, sub, 1)
    seg_row = segment.astype(f32)[None]
    taps = (conv_input, conv_statein, conv_stateout)
    core_params = (step_bias[None], rate_log[None], skip_gain[None], inner_gain[None])
    in_list = (
        mamba_gate,
        mamba_input,
        state_in,
        state_out,
        query_weight,
        key_weight,
        value_weight,
        step_weight,
    )
    one_gain, two_gain = first_gain[None], second_gain[None]
    buffers = Line.scratch(size, STEPS, sub, width)
    og_low, og_high = out_grad[: mine // 2], out_grad[mine // 2 :]
    og_low = lax.all_gather(og_low, "tp", axis=0)

    resid_one, full_one, projected, step_raw = comm_call(
        functools.partial(embed_kernel, size),
        (
            sds((STEPS, sub, width), f32),
            sds((*shape, width), bf16),
            sds((*shape, PROJ), bf16),
            sds((*shape, step_weight.shape[1]), f32),
        ),
        buffers,
        1,
        patches.reshape(*shape, patches.shape[1]),
        embed_weight,
        keep_rows,
        one_gain,
        *in_list,
    )
    og_low, og_high, projected = lax.optimization_barrier((og_low, og_high, projected))
    og_high = lax.all_gather(og_high, "tp", axis=0)
    projected = projected.reshape(length, PROJ)
    step_raw = step_raw.reshape(length, step_weight.shape[1])
    mix_in, ssd, states, lse = mixer_fwd(size, projected, step_raw, seg_row, taps, *core_params)
    inner_width = mamba_output.shape[0]
    hidden_width = ffn_gate.shape[1]
    rows16 = sds((*shape, width), bf16)
    rows32 = sds((STEPS, sub, width), f32)
    mixed = mix_in.shape[1]
    half_shape = (size, STEPS // 2, sub, width)
    resid_grad, ffn_part, resid_two, dmix, grads, second_gain_grad = comm_call(
        functools.partial(ffn_kernel, size),
        (
            rows32, rows16, rows32, sds((*shape, mixed), bf16),
            sds((width, 3 * hidden_width + mixed), bf16), sds((1, width), f32),
        ),
        [pltpu.VMEM((*shape, hidden_width), bf16)] * 3 + buffers + buffers,
        2,
        mix_in.reshape(*shape, mixed),
        mamba_output,
        attn_output,
        resid_one,
        two_gain,
        ffn_gate,
        ffn_up,
        ffn_down,
        og_low.reshape(half_shape),
        og_high.reshape(half_shape),
        out_grad.reshape(STEPS, sub, width),
    )
    ffn_sum = lax.psum_scatter(
        ffn_part.reshape(length, width), "tp", scatter_dimension=0, tiled=True
    )
    mid_sum = lax.psum_scatter(grads, "dp", scatter_dimension=0, tiled=True)
    proj_grad, step_grad, dtaps, dheads, dgain, dskip = mixer_bwd(
        size, projected, step_raw, seg_row, taps, *core_params, mix_in, ssd, states, lse,
        dmix.reshape(length, mixed),
    )
    dp = lax.axis_size("dp")
    block = width // dp
    features = patches.shape[1]
    patches_grad, embed_sum, in_sum, small = comm_call(
        functools.partial(entry_kernel, size, dp),
        (
            sds((*shape, features), bf16),
            sds((block, features), bf16),
            sds((block, PROJ + 128), bf16),
            sds((16, width), f32),
        ),
        buffers
        + Halving.scratch(dp, block, PROJ + 128)
        + Halving.scratch(dp, block, features)
        + Doubling.scratch(dp, size, 16, width),
        3,
        proj_grad.reshape(*shape, PROJ),
        step_grad.reshape(*shape, step_grad.shape[1]),
        *in_list,
        resid_one,
        one_gain,
        resid_grad,
        keep_rows,
        embed_weight,
        full_one,
        patches.reshape(*shape, features),
        dtaps,
        dheads,
        dgain,
        dskip,
        second_gain_grad,
    )
    place = (lax.axis_index("dp") * size + lax.axis_index("tp"))[None]
    flip = block % 128 == 0

    def turned(rows):
        return sds((rows, block) if flip else (block, rows), f32)

    outs = pl.pallas_call(
        last_kernel,
        out_shape=(
            sds((length, features), bf16),
            sds((mine, width), bf16),
            turned(features),
            *[sds((block, member.shape[1]), f32) for member in in_list],
            *[sds(member.shape, f32) for member in taps],
            *[sds((1, step_bias.shape[0]), f32)] * 3,
            sds((1, inner_width), f32),
            turned(inner_width),
            turned(attn_output.shape[0]),
            sds((block, hidden_width), f32),
            sds((block, hidden_width), f32),
            turned(hidden_width),
            sds((1, block // size), f32),
            sds((1, block // size), f32),
        ),
        in_specs=[pl.BlockSpec(memory_space=pl.ANY)]
        + [pl.BlockSpec(memory_space=pltpu.VMEM)] * 6
        + [pl.BlockSpec(memory_space=pltpu.SMEM)],
        out_specs=(
            pl.BlockSpec(memory_space=pl.ANY),
            *[pl.BlockSpec(memory_space=pltpu.VMEM)] * 24,
        ),
        scratch_shapes=[pltpu.SemaphoreType.DMA],
        compiler_params=pltpu.CompilerParams(vmem_limit_bytes=40 * 2**20),
    )(
        patches_grad.reshape(length, features),
        embed_sum,
        in_sum,
        mid_sum,
        small,
        resid_two.reshape(mine, width),
        ffn_sum,
        place,
    )
    (
        patches_grad, result, embed_cols, gz, gx, gb, gc, gq, gk, gv, gs, t0, t1, t2, hb, hr, hs,
        inner_grad, gmo, gao, ggate, gup, gdown, gain_one, gain_two,
    ) = outs
    if not flip:
        embed_cols, gmo, gao, gdown = embed_cols.T, gmo.T, gao.T, gdown.T
    return (
        result,
        patches_grad,
        embed_cols,
        gain_one[0],
        gz,
        gx,
        gb,
        gc,
        gs,
        t0,
        t1,
        t2,
        hb[0],
        hr[0],
        hs[0],
        inner_grad[0],
        gmo,
        gq,
        gk,
        gv,
        gao,
        gain_two[0],
        ggate,
        gup,
        gdown,
    )


def solution(mesh):
    return jax.shard_map(
        shards,
        mesh=mesh,
        in_specs=(
            P("dp", "tp"),
            P(("dp", "tp")),
            P("dp", None),
            P("tp", None),
            P(),
            P(None, "tp"),
            P(None, "tp"),
            P(None, "tp"),
            P(None, "tp"),
            P(None, "tp"),
            P(None, "tp"),
            P(None, "tp"),
            P(None, "tp"),
            P("tp"),
            P("tp"),
            P("tp"),
            P("tp"),
            P("tp", None),
            P(None, "tp"),
            P(None, "tp"),
            P(None, "tp"),
            P("tp", None),
            P(),
            P(None, "tp"),
            P(None, "tp"),
            P("tp", None),
            P(("dp", "tp"), None),
        ),
        out_specs=(
            P(("dp", "tp"), None),
            P("dp", "tp"),
            P("tp", "dp"),
            P(("dp", "tp")),
            P("dp", "tp"),
            P("dp", "tp"),
            P("dp", "tp"),
            P("dp", "tp"),
            P("dp", "tp"),
            P(None, "tp"),
            P(None, "tp"),
            P(None, "tp"),
            P("tp"),
            P("tp"),
            P("tp"),
            P("tp"),
            P("tp", "dp"),
            P("dp", "tp"),
            P("dp", "tp"),
            P("dp", "tp"),
            P("tp", "dp"),
            P(("dp", "tp")),
            P("dp", "tp"),
            P("dp", "tp"),
            P("tp", "dp"),
        ),
        check_vma=False,
    )
```

```python
import functools

import jax
import jax.numpy as jnp
from jax import lax
from jax.experimental import pallas as pl
from jax.experimental.pallas import tpu as pltpu
from jax.sharding import PartitionSpec as P

f32 = jnp.float32
bf16 = jnp.bfloat16
eps = 1e-05
NST = 128
LOG2E = 1.4426950408889634
LOW = -1e30
NN = ((1,), (0,))
NT = ((1,), (1,))
TN = ((0,), (0,))
PROJ = 2048
STEPS = 8


def mm(a, b, dims=NN):
    return lax.dot_general(a, b, (dims, ((), ())), preferred_element_type=f32)


def parts_of(v, count):
    terms = []
    for _ in range(count):
        term = v.astype(bf16)
        terms.append(term)
        v = v - term.astype(f32)
    return terms


def pick(chosen, v, dims=NN, count=3):
    total = None
    for term in parts_of(v, count):
        product = mm(chosen, term, dims)
        total = product if total is None else total + product
    return total


def iota(shape, axis):
    return lax.broadcasted_iota(jnp.int32, shape, axis)


def expand(v):
    low_half = iota((1, 128), 1) < 64
    return jnp.concatenate(
        [
            jnp.where(low_half, v[:, h : h + 1], v[:, h + 1 : h + 2])
            for h in range(0, v.shape[1], 2)
        ],
        axis=1,
    )


def head_sum(v):
    owner = (iota((512, 8), 0) // 64 == iota((512, 8), 1)).astype(bf16)
    high, low = parts_of(v, 2)
    return mm(high, owner) + mm(low, owner)


def softplus(v):
    return jnp.maximum(v, 0.0) + jnp.log1p(jnp.exp(-jnp.abs(v)))


def tile4(v):
    return jnp.concatenate([v, v, v, v], axis=1)


def fill_segments(seg_ref, segcol):
    length = seg_ref.shape[1]
    segcol[0:8, :] = jnp.full((8, 128), -1.0, f32)
    segcol[length + 8 : length + 16, :] = jnp.full((8, 128), -2.0, f32)
    for row in range(0, length, 128):
        piece = jnp.broadcast_to(seg_ref[0:1, row : row + 128], (128, 128))
        segcol[8 + row : 8 + row + 128, :] = piece.T


def taps_of(taps, tile):
    if tile < 4:
        return taps[0][:, tile * 128 : tile * 128 + 128]
    return taps[tile - 3][...]


def conv_masks(rows, segx):
    here = segx[8 : 8 + rows, :]
    return [(segx[8 - lag : 8 - lag + rows, :] == here).astype(f32) for lag in (1, 2, 3)]


def conv_pre(tile, rows, uext, masks, taps):
    lanes = slice(tile * 128, tile * 128 + 128)
    w = taps_of(taps, tile)
    pre = uext[8 : 8 + rows, lanes] * w[0:1, :]
    for lag in (1, 2, 3):
        shifted = uext[8 - lag : 8 - lag + rows, lanes] * masks[lag - 1]
        pre = pre + shifted * w[lag : lag + 1, :]
    return pre


def load_inputs(first, rows, proj, segcol, uext, segx):
    @pl.when(first == 0)
    def _():
        uext[0:8, :] = jnp.zeros((8, 768), f32)

    @pl.when(first > 0)
    def _():
        uext[0:8, :] = proj[pl.ds(pl.multiple_of(first - 16, 16), 16), 512:1280].astype(f32)[8:16]

    uext[8 : 8 + rows, :] = proj[pl.ds(first, rows), 512:1280].astype(f32)
    segx[...] = segcol[pl.ds(first, rows + 16), :]


def decays(first, rows, step, bias, rate):
    raw = step[pl.ds(first, rows), :] + bias[...]
    size = softplus(raw)
    logs = size * -jnp.exp(rate[...])
    scaled = logs * LOG2E
    lower = (iota((rows, rows), 0) >= iota((rows, rows), 1)).astype(bf16)
    cum = pick(lower, scaled)
    wide = jnp.concatenate([cum, jnp.zeros((rows, 120), f32)], axis=1)
    return raw, size, logs, cum, wide.T[0:8, :]


def half_masks():
    low_half = iota((1, 128), 1) < 64
    return low_half, jnp.logical_not(low_half)


def keep(mask, v):
    return jnp.where(mask, v, jnp.zeros_like(v))


def mixer_fwd_chunk(
    index, rows, proj, step, seg, segcol, taps, bias, rate, skip, gain, uext, segx, state,
    oacc, stats, mix_out, ssd_out, states_out, lse_out,
):
    first = pl.multiple_of(index * rows, rows)
    here = pl.ds(first, rows)
    halves = half_masks()
    load_inputs(first, rows, proj, segcol, uext, segx)
    masks = conv_masks(rows, segx)
    acts = []
    for tile in range(6):
        pre = conv_pre(tile, rows, uext, masks, taps)
        acts.append(pre * jax.nn.sigmoid(pre))
    xc = jnp.concatenate(acts[0:4], axis=1)
    bc, cc = acts[4].astype(bf16), acts[5].astype(bf16)
    _, size, _, cum, cumr = decays(first, rows, step, bias, rate)
    segc = segx[8 : 8 + rows, :]
    before = segx[7:8, :]
    goes_on = (segc == before).astype(f32)
    segr = seg[0:1, here]
    wide_seg = jnp.concatenate([segc] * (rows // 128), axis=1)
    allowed = (iota((rows, rows), 0) >= iota((rows, rows), 1)) & (wide_seg == segr)
    away = jnp.where(allowed, 0.0, LOW)
    cb = mm(cc, bc, NT)
    xs = xc * expand(size)
    xsb = xs.astype(bf16)
    parts = []
    for pair in range(4):
        lhs = []
        for h in (2 * pair, 2 * pair + 1):
            gap = cum[:, h : h + 1] - cumr[h : h + 1, :] + away
            lhs.append((cb * jnp.exp2(gap)).astype(bf16))
        xp = xsb[:, pair * 128 : pair * 128 + 128]
        rhs = jnp.concatenate([keep(halves[0], xp), keep(halves[1], xp)], axis=0)
        parts.append(mm(jnp.concatenate(lhs, axis=1), rhs))
    ssd = jnp.concatenate(parts, axis=1) + xc * expand(skip[...])
    st = state[...]
    stb = st.astype(bf16)
    states_out[index] = stb
    ssd = ssd + mm(cc, stb) * expand(jnp.exp2(cum)) * tile4(goes_on)
    last = cum[rows - 1 : rows, :]
    fits = (segc == segc[rows - 1 : rows, :]).astype(f32)
    weight = expand(jnp.exp2(last - cum)) * tile4(fits)
    added = mm(bc, (xs * weight).astype(bf16), TN)
    passes = (segc[rows - 1 : rows, :] == before).astype(f32)
    state[...] = st * (expand(jnp.exp2(last)) * tile4(passes)) + added
    ssd_out[here, :] = ssd.astype(bf16)
    z = proj[here, 0:512].astype(f32)
    g = ssd * (z * jax.nn.sigmoid(z))
    r = lax.rsqrt(jnp.mean(g * g, axis=1, keepdims=True) + eps)
    mix_out[here, 0:512] = (g * r * gain[...]).astype(bf16)
    own_seg = seg[0:1, here]

    def keys(block, fresh):
        start = pl.multiple_of(block * rows, rows)
        away = attention_away(start, first, rows, own_seg, segcol)
        for pair in range(2):
            lanes = pair * 128
            q = proj[here, 1280 + lanes : 1408 + lanes] * jnp.asarray(0.125, bf16)
            k = proj[pl.ds(start, rows), 1536 + lanes : 1664 + lanes]
            v = proj[pl.ds(start, rows), 1792 + lanes : 1920 + lanes]
            for half in range(2):
                h = 2 * pair + half
                mine = slice(h * 64, h * 64 + 64)
                s = mm(k, keep(halves[half], q), NT) + away
                peak = jnp.max(s, axis=0, keepdims=True)
                if not fresh:
                    old = stats[h : h + 1, :]
                    peak = jnp.maximum(peak, old)
                    fade = jnp.exp(old - peak)
                p = jnp.exp(s - peak)
                total = jnp.sum(p, axis=0, keepdims=True)
                o = mm(v, p.astype(bf16), TN)[half * 64 : half * 64 + 64, :]
                if not fresh:
                    total = total + stats[h + 4 : h + 5, :] * fade
                    o = o + oacc[mine, :] * fade
                stats[h : h + 1, :] = peak
                stats[h + 4 : h + 5, :] = total
                oacc[mine, :] = o

    keys(index, True)

    def earlier(block, _):
        keys(block, False)
        return 0

    lax.fori_loop(0, index, earlier, 0)
    lse_out[0:4, here] = stats[0:4, :] + jnp.log(stats[4:8, :])
    for h in range(4):
        mine = slice(h * 64, h * 64 + 64)
        oacc[mine, :] = oacc[mine, :] * (1.0 / stats[h + 4 : h + 5, :])
    for pair in range(2):
        mine = slice(pair * 128, pair * 128 + 128)
        mix_out[here, 512 + pair * 128 : 640 + pair * 128] = oacc[mine, :].T.astype(bf16)


def attention_away(start, first, rows, own_seg, segcol):
    key_seg = segcol[pl.ds(start + 8, rows), :]
    wide = jnp.concatenate([key_seg] * (rows // 128), axis=1)
    allowed = (wide == own_seg) & (
        iota((rows, rows), 0) + start <= iota((rows, rows), 1) + first
    )
    return jnp.where(allowed, 0.0, LOW)


def mixer_bwd_chunk(
    index, rows, proj, step, seg, segcol, taps, bias, rate, skip, gain, uext, segx, slopes, dext,
    dstate, dkv, dqs, mix, ssd_in, states_in, lse_in, dmix, dproj, dstep, dtaps, dheads, dgain, dskip,
):
    first = pl.multiple_of(index * rows, rows)
    here = pl.ds(first, rows)
    halves = half_masks()
    load_inputs(first, rows, proj, segcol, uext, segx)
    masks = conv_masks(rows, segx)
    acts = []
    for tile in range(6):
        pre = conv_pre(tile, rows, uext, masks, taps)
        sig = jax.nn.sigmoid(pre)
        acts.append(pre * sig)
        slopes[:, tile * 128 : tile * 128 + 128] = sig * (1.0 + pre * (1.0 - sig))
    xc = jnp.concatenate(acts[0:4], axis=1)
    bc, cc = acts[4].astype(bf16), acts[5].astype(bf16)
    raw, size, logs, cum, cumr = decays(first, rows, step, bias, rate)
    z = proj[here, 0:512].astype(f32)
    ssd = ssd_in[here, :].astype(f32)
    dmo = dmix[here, 0:512].astype(f32)
    sig = jax.nn.sigmoid(z)
    act = z * sig
    g = ssd * act
    r = lax.rsqrt(jnp.mean(g * g, axis=1, keepdims=True) + eps)
    gain_part = jnp.sum(dmo * g * r, axis=0, keepdims=True)
    a = dmo * gain[...]
    dg = r * a - (r * r * r) * g * jnp.mean(a * g, axis=1, keepdims=True)
    dssd = dg * act
    dproj[here, 0:512] = (dg * ssd * (sig * (1.0 + z * (1.0 - sig)))).astype(bf16)
    skip_part = jnp.sum(dssd * xc, axis=0, keepdims=True)
    dxc = dssd * expand(skip[...])
    dyb = dssd.astype(bf16)
    wide_size = expand(size)
    xs = xc * wide_size
    xsb = xs.astype(bf16)
    segc = segx[8 : 8 + rows, :]
    before = segx[7:8, :]
    goes_on = (segc == before).astype(f32)
    segr = seg[0:1, here]
    wide_seg = jnp.concatenate([segc] * (rows // 128), axis=1)
    allowed = (iota((rows, rows), 0) <= iota((rows, rows), 1)) & (wide_seg == segr)
    away = jnp.where(allowed, 0.0, LOW)
    cbt = mm(bc, cc, NT)
    dcbt = jnp.zeros((rows, rows), f32)
    to_rows = []
    from_rows = jnp.zeros((rows, 8), f32)
    parts = []
    for pair in range(4):
        lanes = slice(pair * 128, pair * 128 + 128)
        lhs, rhs = [], []
        for half in range(2):
            h = 2 * pair + half
            lt = jnp.exp2(cumr[h : h + 1, :] - cum[:, h : h + 1] + away)
            mt = cbt * lt
            lhs.append(mt.astype(bf16))
            rhs.append(keep(halves[half], dyb[:, lanes]))
            dl = mm(keep(halves[half], xsb[:, lanes]), dyb[:, lanes], NT)
            dcbt = dcbt + dl * lt
            gt = dl * mt
            to_rows.append(jnp.sum(gt, axis=0, keepdims=True))
            from_rows = jnp.where(
                iota((1, 8), 1) == h, jnp.sum(gt, axis=1, keepdims=True), from_rows
            )
        parts.append(mm(jnp.concatenate(lhs, axis=1), jnp.concatenate(rhs, axis=0)))
    dxs = jnp.concatenate(parts, axis=1)
    dcb = dcbt.astype(bf16)
    db = mm(dcb, cc)
    dc = mm(dcb, bc, TN)
    upper = (iota((rows, rows), 0) <= iota((rows, rows), 1)).astype(bf16)
    late = -from_rows
    reach = expand(jnp.exp2(cum)) * tile4(goes_on)
    stb = states_in[index]
    dye = dssd * reach
    dyeb = dye.astype(bf16)
    dc = dc + mm(dyeb, stb, NT)
    late = late + head_sum(dye * mm(cc, stb))
    into_state = mm(cc, dyeb, TN)
    last = cum[rows - 1 : rows, :]
    fits = (segc == segc[rows - 1 : rows, :]).astype(f32)
    weight = expand(jnp.exp2(last - cum)) * tile4(fits)
    dst = dstate[...]
    dsb = dst.astype(bf16)
    dxi = mm(bc, dsb) * weight
    dxs = dxs + dxi
    db = db + mm((xs * weight).astype(bf16), dsb, NT)
    strict = (iota((rows, rows), 0) > iota((rows, rows), 1)).astype(bf16)
    dlog = pick(strict, head_sum(xs * dxi))
    passes = (segc[rows - 1 : rows, :] == before).astype(f32)
    fade = expand(jnp.exp2(last)) * tile4(passes)
    through = jnp.sum(stb.astype(f32) * dst, axis=0, keepdims=True) * fade
    dlog = dlog + head_sum(jnp.broadcast_to(through, (8, 512)))[0:1, :]
    dstate[...] = dst * fade + into_state
    dlog = dlog + pick(upper, late) + pick(upper, jnp.concatenate(to_rows, axis=0), NT)
    dsize = head_sum(dxs * xc) - dlog * jnp.exp(rate[...])
    rate_part = jnp.sum(dlog * logs, axis=0, keepdims=True)
    draw = dsize * jax.nn.sigmoid(raw)
    bias_part = jnp.sum(draw, axis=0, keepdims=True)
    dstep[here, :] = draw.astype(dstep.dtype)
    dxc = dxc + dxs * wide_size
    dacts = [dxc[:, t * 128 : t * 128 + 128] for t in range(4)] + [db, dc]
    dext[rows : rows + 8, :] = dext[0:8, :]
    ahead = [(segx[8 + lag : 8 + lag + rows, :] == segc).astype(f32) for lag in (1, 2, 3)]
    for tile in range(6):
        lanes = slice(tile * 128, tile * 128 + 128)
        w = taps_of(taps, tile)
        dpre = dacts[tile] * slopes[:, lanes]
        dext[0:rows, lanes] = dpre
        u = uext[8 : 8 + rows, lanes]
        du = dpre * w[0:1, :]
        sums = [jnp.sum(dpre * u, axis=0, keepdims=True)]
        for lag in (1, 2, 3):
            later = dext[lag : lag + rows, lanes] * ahead[lag - 1]
            du = du + later * w[lag : lag + 1, :]
            sums.append(jnp.sum(later * u, axis=0, keepdims=True))
        dproj[here, 512 + tile * 128 : 640 + tile * 128] = du.astype(bf16)
        sums = jnp.concatenate(sums, axis=0)
        dtaps[:, lanes] = dtaps[:, lanes] + sums
    head_parts = jnp.concatenate([bias_part, rate_part], axis=0)
    dheads[...] = dheads[...] + head_parts
    dgain[...] = dgain[...] + gain_part
    dskip[...] = dskip[...] + skip_part
    own_seg = seg[0:1, here]
    dos = [dmix[here, 512 + pair * 128 : 640 + pair * 128] for pair in range(2)]
    owner = (iota((8, 256), 1) // 64 == iota((8, 256), 0)).astype(bf16)
    delta = pick(
        owner,
        jnp.concatenate(dos, axis=1).astype(f32) * mix[here, 512:768].astype(f32),
        NT,
        2,
    )
    dqs[...] = jnp.zeros_like(dqs)

    def keys(block, _):
        start = pl.multiple_of(block * rows, rows)
        there = pl.ds(start, rows)
        away = attention_away(start, first, rows, own_seg, segcol)
        for pair in range(2):
            lanes = pair * 128
            q = proj[here, 1280 + lanes : 1408 + lanes] * jnp.asarray(0.125, bf16)
            k = proj[there, 1536 + lanes : 1664 + lanes]
            v = proj[there, 1792 + lanes : 1920 + lanes]
            ps, dss, qms, doms = [], [], [], []
            for half in range(2):
                h = 2 * pair + half
                mine = slice(h * 64, h * 64 + 64)
                qm, dom = keep(halves[half], q), keep(halves[half], dos[pair])
                p = jnp.exp(mm(k, qm, NT) + away - lse_in[h : h + 1, here])
                dp = mm(v, dom, NT)
                ds = (p * (dp - delta[h : h + 1, :])).astype(bf16)
                dqs[mine, :] = dqs[mine, :] + mm(k, ds, TN)[half * 64 : half * 64 + 64, :]
                ps.append(p.astype(bf16))
                dss.append(ds)
                qms.append(qm)
                doms.append(dom)
            kl, vl = slice(lanes, lanes + 128), slice(256 + lanes, 384 + lanes)
            dkv[there, kl] = dkv[there, kl] + mm(
                jnp.concatenate(dss, axis=1), jnp.concatenate(qms, axis=0)
            )
            dkv[there, vl] = dkv[there, vl] + mm(
                jnp.concatenate(ps, axis=1), jnp.concatenate(doms, axis=0)
            )
        return 0

    lax.fori_loop(0, index + 1, keys, 0)
    for pair in range(2):
        mine = slice(pair * 128, pair * 128 + 128)
        dproj[here, 1280 + pair * 128 : 1408 + pair * 128] = (dqs[mine, :] * 0.125).T.astype(bf16)
    dproj[here, 1536:2048] = dkv[here, :].astype(bf16)


def fwd_kernel(count, proj, step, seg, t0, t1, t2, bias, rate, skip, gain,
               mix_out, ssd_out, states_out, lse_out, segcol, uext, segx, state, oacc, stats):
    rows = proj.shape[0] // count
    fill_segments(seg, segcol)
    lse_out[...] = jnp.zeros_like(lse_out)
    state[...] = jnp.zeros_like(state)

    def chunk(index, _):
        mixer_fwd_chunk(index, rows, proj, step, seg, segcol, (t0, t1, t2), bias, rate, skip,
                        gain, uext, segx, state, oacc, stats, mix_out, ssd_out, states_out,
                        lse_out)
        return 0

    lax.fori_loop(0, count, chunk, 0)


def bwd_kernel(count, proj, step, seg, t0, t1, t2, bias, rate, skip, gain, mix, ssd_in,
               states_in, lse_in, dmix, dproj, dstep, dtaps, dheads, dgain, dskip,
               segcol, uext, segx, slopes, dext, dstate, dkv, dqs):
    rows = proj.shape[0] // count
    fill_segments(seg, segcol)
    for ref in (dtaps, dheads, dgain, dskip, dstate, dkv):
        ref[...] = jnp.zeros_like(ref)
    dext[0:8, :] = jnp.zeros((8, 768), f32)

    def chunk(turn, _):
        mixer_bwd_chunk(count - 1 - turn, rows, proj, step, seg, segcol, (t0, t1, t2), bias,
                        rate, skip, gain, uext, segx, slopes, dext, dstate, dkv, dqs, mix, ssd_in,
                        states_in, lse_in, dmix, dproj, dstep, dtaps, dheads, dgain, dskip)
        return 0

    lax.fori_loop(0, count, chunk, 0)
    dskip8 = head_sum(jnp.broadcast_to(dskip[...], (8, 512)))
    dskip[0:1, 0:8] = dskip8[0:1, :]


def mixer_fwd(count, proj, step, seg, taps, bias, rate, skip, gain):
    length = proj.shape[0]
    rows = length // count
    return pl.pallas_call(
        functools.partial(fwd_kernel, count),
        out_shape=(
            jax.ShapeDtypeStruct((length, 768), bf16),
            jax.ShapeDtypeStruct((length, 512), bf16),
            jax.ShapeDtypeStruct((count, NST, 512), bf16),
            jax.ShapeDtypeStruct((8, length), f32),
        ),
        scratch_shapes=[
            pltpu.VMEM((length + 16, 128), f32),
            pltpu.VMEM((rows + 8, 768), f32),
            pltpu.VMEM((rows + 16, 128), f32),
            pltpu.VMEM((NST, 512), f32),
            pltpu.VMEM((256, rows), f32),
            pltpu.VMEM((8, rows), f32),
        ],
        compiler_params=pltpu.CompilerParams(vmem_limit_bytes=60 * 2**20),
    )(proj, step, seg, *taps, bias, rate, skip, gain)


def mixer_bwd(count, proj, step, seg, taps, bias, rate, skip, gain, mix, ssd, states, lse, dmix):
    length = proj.shape[0]
    rows = length // count
    return pl.pallas_call(
        functools.partial(bwd_kernel, count),
        out_shape=(
            jax.ShapeDtypeStruct((length, 2048), bf16),
            jax.ShapeDtypeStruct((length, 8), bf16),
            jax.ShapeDtypeStruct((4, 768), f32),
            jax.ShapeDtypeStruct((2, 8), f32),
            jax.ShapeDtypeStruct((1, 512), f32),
            jax.ShapeDtypeStruct((1, 512), f32),
        ),
        scratch_shapes=[
            pltpu.VMEM((length + 16, 128), f32),
            pltpu.VMEM((rows + 8, 768), f32),
            pltpu.VMEM((rows + 16, 128), f32),
            pltpu.VMEM((rows, 768), f32),
            pltpu.VMEM((rows + 8, 768), f32),
            pltpu.VMEM((NST, 512), f32),
            pltpu.VMEM((length, 512), f32),
            pltpu.VMEM((256, rows), f32),
        ],
        compiler_params=pltpu.CompilerParams(vmem_limit_bytes=60 * 2**20),
    )(proj, step, seg, *taps, bias, rate, skip, gain, mix, ssd, states, lse, dmix)


MESH = pl.DeviceIdType.MESH


class Line:
    def __init__(self, scratch, size, hop=1):
        self.hop = hop
        (self.own, self.left, self.right, self.full, self.acc,
         self.ss, self.sr, self.gs, self.gr) = scratch
        self.size = size
        self.steps = self.own.shape[1]
        self.me = lax.axis_index("tp")
        self.last = size - 1

    @staticmethod
    def scratch(size, steps, sub, width):
        return [
            pltpu.VMEM((size, steps, sub, width), f32),
            pltpu.VMEM((size, steps, sub, width), bf16),
            pltpu.VMEM((size, steps, sub, width), bf16),
            pltpu.VMEM((size, steps, sub, width), bf16),
            pltpu.VMEM((sub, width), f32),
            pltpu.SemaphoreType.DMA((2, size, steps)),
            pltpu.SemaphoreType.DMA((2, size, steps)),
            pltpu.SemaphoreType.DMA((2, size, steps)),
            pltpu.SemaphoreType.DMA((2, size, steps)),
        ]

    def sum_copy(self, way, d, j):
        buf = self.left if way == 0 else self.right
        return pltpu.make_async_remote_copy(
            src_ref=buf.at[d, j],
            dst_ref=buf.at[d, j],
            send_sem=self.ss.at[way, d, j],
            recv_sem=self.sr.at[way, d, j],
            device_id={"tp": self.me + 1 if way == 0 else self.me - 1},
            device_id_type=MESH,
        )

    def row_copy(self, way, d, j):
        return pltpu.make_async_remote_copy(
            src_ref=self.full.at[d, j],
            dst_ref=self.full.at[d, j],
            send_sem=self.gs.at[way, d, j],
            recv_sem=self.gr.at[way, d, j],
            device_id={"tp": self.me + 1 if way == 0 else self.me - 1},
            device_id_type=MESH,
        )

    def enter(self):
        barrier = pltpu.get_barrier_semaphore()
        me, last = self.me, self.last

        @pl.when(me > 0)
        def _():
            pl.semaphore_signal(barrier, inc=1, device_id={"tp": me - 1}, device_id_type=MESH)

        @pl.when(me < last)
        def _():
            pl.semaphore_signal(barrier, inc=1, device_id={"tp": me + 1}, device_id_type=MESH)

        peers = jnp.where(me > 0, 1, 0) + jnp.where(me < last, 1, 0)
        pl.semaphore_wait(barrier, peers)

    def relay(self, way, j):
        me, last = self.me, self.last
        buf = self.left if way == 0 else self.right
        first_one = me == 0 if way == 0 else me == last

        def one(d, _):
            @pl.when(first_one)
            def _():
                buf[d, j] = self.own[d, j].astype(bf16)

            @pl.when(jnp.logical_not(first_one))
            def _():
                self.sum_copy(way, d, j).wait_recv()
                buf[d, j] = (buf[d, j].astype(f32) + self.own[d, j]).astype(bf16)

            self.sum_copy(way, d, j).start()
            return 0

        if way == 0:
            lax.fori_loop(me + 1, self.size, one, 0)
        else:
            lax.fori_loop(0, me, one, 0)

    def settle(self, j, finish):
        me, last = self.me, self.last
        self.acc[...] = self.own[me, j]

        @pl.when(me > 0)
        def _():
            self.sum_copy(0, me, j).wait_recv()
            self.acc[...] = self.acc[...] + self.left[me, j].astype(f32)

        @pl.when(me < last)
        def _():
            self.sum_copy(1, me, j).wait_recv()
            self.acc[...] = self.acc[...] + self.right[me, j].astype(f32)

        self.full[me, j] = finish(j, self.acc[...])

        @pl.when(me < last)
        def _():
            self.row_copy(0, me, j).start()

        @pl.when(me > 0)
        def _():
            self.row_copy(1, me, j).start()

    def inside(self, j):
        return jnp.logical_and(j >= 0, j < self.steps)

    def pass_on(self, i):
        me, last = self.me, self.last

        def from_left(d, _):
            j = i - self.hop * (jnp.maximum(d, last - d) + me - d)

            @pl.when(self.inside(j))
            def _():
                self.row_copy(0, d, j).wait_recv()

                @pl.when(me < last)
                def _():
                    self.row_copy(0, d, j).start()

            return 0

        def from_right(d, _):
            j = i - self.hop * (jnp.maximum(d, last - d) + d - me)

            @pl.when(self.inside(j))
            def _():
                self.row_copy(1, d, j).wait_recv()

                @pl.when(me > 0)
                def _():
                    self.row_copy(1, d, j).start()

            return 0

        lax.fori_loop(0, me, from_left, 0)
        lax.fori_loop(me + 1, self.size, from_right, 0)

    def move(self, i, finish):
        me, last = self.me, self.last
        right_step = i - self.hop * me
        left_step = i - self.hop * (last - me)
        final_step = i - self.hop * jnp.maximum(me, last - me)

        @pl.when(self.inside(right_step))
        def _():
            self.relay(0, right_step)

        @pl.when(self.inside(left_step))
        def _():
            self.relay(1, left_step)

        @pl.when(self.inside(final_step))
        def _():
            self.settle(final_step, finish)

        self.pass_on(i)

    def ready_step(self, i):
        return i - self.hop * (self.last + jnp.maximum(self.me, self.last - self.me))

    def lag(self):
        return 2 * self.hop * self.last

    def leave(self):
        me, last = self.me, self.last

        def step(j, _):
            def right_sums(d, _):
                self.sum_copy(0, d, j).wait_send()
                return 0

            def left_sums(d, _):
                self.sum_copy(1, d, j).wait_send()
                return 0

            def right_rows(d, _):
                self.row_copy(0, d, j).wait_send()
                return 0

            def left_rows(d, _):
                self.row_copy(1, d, j).wait_send()
                return 0

            lax.fori_loop(me + 1, self.size, right_sums, 0)
            lax.fori_loop(0, me, left_sums, 0)

            @pl.when(me < last)
            def _():
                lax.fori_loop(0, me + 1, right_rows, 0)

            @pl.when(me > 0)
            def _():
                lax.fori_loop(me, self.size, left_rows, 0)

            return 0

        lax.fori_loop(0, self.steps, step, 0)


def flat(v):
    return v.reshape(v.shape[0] * v.shape[1], v.shape[2])


def normed(v, gain):
    return v * lax.rsqrt(jnp.mean(v * v, axis=1, keepdims=True) + eps) * gain


def normed_back(grad, v, gain):
    r = lax.rsqrt(jnp.mean(v * v, axis=1, keepdims=True) + eps)
    a = grad * gain
    back = r * a - (r * r * r) * v * jnp.mean(a * v, axis=1, keepdims=True)
    return back, jnp.sum(grad * v * r, axis=0, keepdims=True)


class Fetch:
    def __init__(self, sources, places, sems, first=0):
        self.copies = [
            pltpu.make_async_copy(source, place, sems.at[first + n])
            for n, (source, place) in enumerate(zip(sources, places))
        ]

    def start(self):
        for copy in self.copies:
            copy.start()

    def wait(self):
        for copy in self.copies:
            copy.wait()


def embed_kernel(size, patches, embed, keep_rows, gain, *refs):
    weights_in, ws = refs[0:7], refs[7]
    resid_out, full_out, proj_out, step_out = refs[8:12]
    wz, wx, wb, wc, wq, wk, wv = weights = refs[12:19]
    fetch = Fetch(weights_in, weights, refs[19])
    line = Line(refs[20:], size)
    steps, sub = line.steps, line.own.shape[2]
    columns = []
    for ref in (wz, wx, wb, wc, wq, wk, wv):
        columns.append((ref, sum(c[0].shape[1] for c in columns)))

    def produce(j):
        line.own[:, j] = mm(flat(patches[:, j]), embed[...]).reshape(size, sub, line.own.shape[3])

    def finish(j, total):
        rows = total * keep_rows[j]
        resid_out[j] = rows
        return normed(rows, gain[...]).astype(bf16)

    def consume(j):
        x = line.full[:, j]
        full_out[:, j] = x
        x = flat(x)
        for ref, start in columns:
            width = ref.shape[1]
            proj_out[:, j, :, start : start + width] = (
                mm(x, ref[...]).astype(bf16).reshape(size, sub, width)
            )
        step_out[:, j] = mm(x, ws[...], NT).reshape(size, sub, ws.shape[0])

    fetch.start()
    line.enter()
    produce(0)

    def iteration(i, _):
        line.move(i, finish)

        @pl.when(i + 1 < steps)
        def _():
            produce(i + 1)

        ready = line.ready_step(i)

        @pl.when(ready == 0)
        def _():
            fetch.wait()

        @pl.when(line.inside(ready))
        def _():
            consume(ready)

        return 0

    lax.fori_loop(0, steps + line.lag(), iteration, 0)
    line.leave()


def ffn_kernel(size, mix, wmo, wao, resid_one, gain, wg_in, wu_in, wd_in, low_in, high_in, og_mine,
               resid_grad, ffn_out, resid_out, dmix, grads_out, gain_grad, hidden_all, gg_all, ug_all,
               wg, wu, wd, og_low, og_high, grads, load, *scratch):
    fetch = Fetch((wg_in, wu_in, wd_in, low_in, high_in), (wg, wu, wd, og_low, og_high), load)
    half = len(scratch) // 2
    one, two = Line(scratch[:half], size), Line(scratch[half:], size)
    steps, sub, width = one.steps, one.own.shape[2], one.own.shape[3]
    length = size * steps * sub
    inner, mixed, units = wmo.shape[0], mix.shape[3], wg.shape[1]
    group = 256
    groups = width // group

    def shaped(v):
        return v.reshape(size, sub, v.shape[1])

    def all_rows(v):
        return v.reshape(length, v.shape[3])

    def produce(j):
        x = flat(mix[:, j])
        one.own[:, j] = shaped(mm(x[:, 0:inner], wmo[...]) + mm(x[:, inner:], wao[...]))

    def finish_one(j, total):
        rows = resid_one[j] + total
        resid_out[j] = rows
        return normed(rows, gain[...]).astype(bf16)

    def middle(j, og):
        x = flat(one.full[:, j])
        gate, up = mm(x, wg[...]), mm(x, wu[...])
        hg = mm(og, wd[...], NT)
        sig = jax.nn.sigmoid(gate)
        act = gate * sig
        hidden = (act * up).astype(bf16)
        gg = (hg * up * (sig * (1.0 + gate * (1.0 - sig)))).astype(bf16)
        ug = (hg * act).astype(bf16)
        hidden_all[:, j] = shaped(hidden)
        gg_all[:, j] = shaped(gg)
        ug_all[:, j] = shaped(ug)
        two.own[:, j] = shaped(mm(gg, wg[...], NT) + mm(ug, wu[...], NT))
        ffn_out[:, j] = shaped(mm(hidden, wd[...]).astype(bf16))

    def finish_two(j, total):
        back, part = normed_back(total, resid_out[j], gain[...])
        rows = og_mine[j].astype(f32) + back
        resid_grad[j] = rows
        gain_grad[...] = gain_grad[...] + part
        return rows.astype(bf16)

    def consume(j):
        x = flat(two.full[:, j])
        dmix[:, j, :, 0:inner] = shaped(mm(x, wmo[...], NT).astype(bf16))
        dmix[:, j, :, inner:] = shaped(mm(x, wao[...], NT).astype(bf16))

    def columns(ref, g):
        return all_rows(ref[:, :, :, pl.ds(pl.multiple_of(g * group, group), group)])

    def ffn_grads(g):
        here = pl.ds(pl.multiple_of(g * group, group), group)
        x = columns(one.full, g)
        grads[here, 0:units] = mm(x, all_rows(gg_all[...]), TN).astype(bf16)
        grads[here, units : 2 * units] = mm(x, all_rows(ug_all[...]), TN).astype(bf16)
        half_steps = steps // 2
        hidden = hidden_all[...]
        total = None
        for part, og in enumerate((og_low, og_high)):
            cols = og[:, :, :, pl.ds(pl.multiple_of(g * group, group), group)]
            cols = cols.reshape(length // 2, group)
            rows = hidden[:, part * half_steps : (part + 1) * half_steps]
            term = mm(cols, rows.reshape(length // 2, units), TN)
            total = term if total is None else total + term
        grads[here, 2 * units : 3 * units] = total.astype(bf16)
        give(g).start()

    def give(g):
        here = pl.ds(pl.multiple_of(g * group, group), group)
        return pltpu.make_async_copy(
            grads.at[here, 0 : 3 * units], grads_out.at[here, 0 : 3 * units], load.at[5 + g]
        )

    def given(g, _):
        give(g).wait()
        return 0

    def mix_grads(g, _):
        here = pl.ds(pl.multiple_of(g * group, group), group)
        grads[here, 3 * units :] = mm(
            columns(two.full, g), all_rows(mix[...]), TN
        ).astype(bf16)
        return 0

    fetch.start()
    one.enter()
    gain_grad[...] = jnp.zeros_like(gain_grad)
    produce(0)
    lag = one.lag() + 1

    def iteration(i, _):
        one.move(i, finish_one)
        two.move(i - lag, finish_two)

        @pl.when(i + 1 < steps)
        def _():
            produce(i + 1)

        ready_one = one.ready_step(i)

        @pl.when(ready_one == 0)
        def _():
            fetch.wait()

        @pl.when(jnp.logical_and(ready_one >= 0, ready_one < steps // 2))
        def _():
            middle(ready_one, flat(og_low[:, ready_one]))

        @pl.when(jnp.logical_and(ready_one >= steps // 2, ready_one < steps))
        def _():
            middle(ready_one, flat(og_high[:, ready_one - steps // 2]))

        ready_two = two.ready_step(i - lag)

        @pl.when(two.inside(ready_two))
        def _():
            consume(ready_two)

        turn = i - (steps + lag)

        @pl.when(jnp.logical_and(turn >= 0, turn < groups))
        def _():
            ffn_grads(turn)

        return 0

    lax.fori_loop(0, steps + lag + two.lag(), iteration, 0)
    lax.fori_loop(0, groups, mix_grads, 0)
    last = pltpu.make_async_copy(
        grads.at[:, 3 * units :], grads_out.at[:, 3 * units :], load.at[5 + groups]
    )
    last.start()
    lax.fori_loop(0, groups, given, 0)
    last.wait()
    one.leave()
    two.leave()


def comm_call(body, out_shape, scratch, identity, *args, kept=(), given=()):
    return pl.pallas_call(
        body,
        out_shape=out_shape,
        in_specs=[
            pl.BlockSpec(memory_space=pl.ANY if place in kept else pltpu.VMEM)
            for place in range(len(args))
        ],
        out_specs=tuple(
            pl.BlockSpec(memory_space=pl.ANY if place in given else pltpu.VMEM)
            for place in range(len(out_shape))
        ),
        scratch_shapes=scratch,
        compiler_params=pltpu.CompilerParams(
            collective_id=identity, has_side_effects=True, vmem_limit_bytes=62 * 2**20
        ),
    )(*args)


def sds(shape, kind):
    return jax.ShapeDtypeStruct(shape, kind)


class Halving:
    def __init__(self, data, got, ss, sr):
        self.data, self.got, self.ss, self.sr = data, got, ss, sr
        self.count, self.rows = data.shape[0], data.shape[1]
        self.bits = self.count.bit_length() - 1
        self.me = lax.axis_index("dp")
        plain = list(range(self.bits))
        other = plain if self.bits < 3 else [0, 2, 1] + plain[3:]
        self.orders = (plain, other)

    @staticmethod
    def scratch(count, rows, columns):
        spare = max(count - 1, 1)
        return [
            pltpu.VMEM((count, rows, columns), bf16),
            pltpu.VMEM((spare, rows, columns), bf16),
            pltpu.SemaphoreType.DMA((2, spare)),
            pltpu.SemaphoreType.DMA((2, spare)),
        ]

    def bit(self, b):
        return lax.rem(self.me // 2**b, 2)

    def block(self, half, stage, e, theirs):
        order = self.orders[half]
        place = 0
        for b in order[:stage]:
            place = place + self.bit(b) * 2**b
        b = order[stage]
        place = place + (1 - self.bit(b) if theirs else self.bit(b)) * 2**b
        for t, b in enumerate(sorted(order[stage + 1 :])):
            place = place + lax.rem(e // 2**t, 2) * 2**b
        return place

    def open(self, stage):
        return 2 ** (self.bits - 1 - stage)

    def slot(self, stage, e):
        return sum(self.open(s) for s in range(stage)) + e

    def part(self, half):
        rows = self.rows // 2
        return pl.ds(half * rows, rows)

    def copy(self, half, stage, e):
        b = self.orders[half][stage]
        slot = self.slot(stage, e)
        return pltpu.make_async_remote_copy(
            src_ref=self.data.at[self.block(half, stage, e, True), self.part(half)],
            dst_ref=self.got.at[slot, self.part(half)],
            send_sem=self.ss.at[half, slot],
            recv_sem=self.sr.at[half, slot],
            device_id={"dp": self.me + (1 - 2 * self.bit(b)) * 2**b},
            device_id_type=MESH,
        )

    def start(self, stage, low=0, high=None):
        def one(e, _):
            self.copy(0, stage, e).start()
            self.copy(1, stage, e).start()
            return 0

        lax.fori_loop(low, self.open(stage) if high is None else high, one, 0)

    def finish(self, stage):
        def one(e, _):
            for half in range(2):
                self.copy(half, stage, e).wait_recv()
                place, part = self.block(half, stage, e, False), self.part(half)
                got = self.got[self.slot(stage, e), part]
                self.data[place, part] = (self.data[place, part].astype(f32) + got.astype(f32)).astype(bf16)
            return 0

        lax.fori_loop(0, self.open(stage), one, 0)

    def leave(self):
        for stage in range(self.bits):

            def one(e, _, stage=stage):
                self.copy(0, stage, e).wait_send()
                self.copy(1, stage, e).wait_send()
                return 0

            lax.fori_loop(0, self.open(stage), one, 0)


class Doubling:
    def __init__(self, parts, got, ss, sr, dp, tp):
        self.parts, self.got, self.ss, self.sr = parts, got, ss, sr
        self.hops = [("dp", b) for b in range(dp.bit_length() - 1)]
        self.hops += [("tp", b) for b in range(tp.bit_length() - 1)]

    @staticmethod
    def scratch(dp, tp, rows, columns):
        hops = dp.bit_length() + tp.bit_length() - 2
        return [
            pltpu.VMEM((hops + 1, rows, columns), f32),
            pltpu.VMEM((hops, rows, columns), f32),
            pltpu.SemaphoreType.DMA((hops,)),
            pltpu.SemaphoreType.DMA((hops,)),
        ]

    def copy(self, hop):
        axis, b = self.hops[hop]
        me = lax.axis_index(axis)
        flip = (1 - 2 * lax.rem(me // 2**b, 2)) * 2**b
        return pltpu.make_async_remote_copy(
            src_ref=self.parts.at[hop],
            dst_ref=self.got.at[hop],
            send_sem=self.ss.at[hop],
            recv_sem=self.sr.at[hop],
            device_id={axis: me + flip},
            device_id_type=MESH,
        )

    def start(self, hop):
        self.copy(hop).start()

    def finish(self, hop):
        self.copy(hop).wait_recv()
        self.parts[hop + 1] = self.parts[hop] + self.got[hop]

    def leave(self):
        for hop in range(len(self.hops)):
            self.copy(hop).wait_send()


def enter_both(dp, tp):
    barrier = pltpu.get_barrier_semaphore()
    me_t, me_d = lax.axis_index("tp"), lax.axis_index("dp")
    for away in range(1, tp):
        pl.semaphore_signal(
            barrier, inc=1, device_id={"tp": lax.rem(me_t + away, tp)}, device_id_type=MESH
        )
    bits = dp.bit_length() - 1
    for b in range(bits):
        flip = (1 - 2 * lax.rem(me_d // 2**b, 2)) * 2**b
        pl.semaphore_signal(barrier, inc=1, device_id={"dp": me_d + flip}, device_id_type=MESH)
    pl.semaphore_wait(barrier, tp - 1 + bits)


def entry_kernel(size, dp, dproj, dstep, wz, wx, wb, wc, wq, wk, wv, ws, resid_one, gain, resid_grad,
                 keep_rows, embed_in, full_in, patches_in, dtaps, dheads, dgain, dskip, two_gain_grad,
                 patch_out, embed_out, in_out, small_out, full_one, embed, patches, patch_grad, load,
                 *scratch):
    fetch = Fetch((full_in, embed_in, patches_in), (full_one, embed, patches), load)
    line = Line(scratch[0:9], size)
    ins = Halving(*scratch[9:13])
    emb = Halving(*scratch[13:17])
    small = Doubling(*scratch[17:21], dp, size)
    steps, sub, width = line.steps, line.own.shape[2], line.own.shape[3]
    length = size * steps * sub
    weights = (wz, wx, wb, wc, wq, wk, wv)
    columns = []
    for ref in weights:
        columns.append((ref, sum(c[0].shape[1] for c in columns)))
    group = 256
    groups = width // group
    in_group = group // ins.rows

    def all_rows(v):
        return v.reshape(length, v.shape[3])

    def produce(j):
        total = mm(flat(dstep[:, j]), ws[...])
        for ref, start in columns:
            total = total + mm(flat(dproj[:, j, :, start : start + ref.shape[1]]), ref[...], NT)
        line.own[:, j] = total.reshape(size, sub, width)

    def finish(j, total):
        back, part = normed_back(total, resid_one[j], gain[...])
        small.parts[0, 9:10] = small.parts[0, 9:10] + part
        return ((resid_grad[j] + back) * keep_rows[j]).astype(bf16)

    def consume(d, _):
        x = flat(line.full[d])
        patch_grad[d] = mm(x, embed[...], NT).astype(bf16).reshape(steps, sub, embed.shape[0])
        give(d).start()
        return 0

    def give(d):
        return pltpu.make_async_copy(patch_grad.at[d], patch_out.at[d], load.at[3 + d])

    def given(d, _):
        give(d).wait()
        return 0

    def weight_group(g):
        x = full_one[:, pl.ds(pl.multiple_of(g * group, group), group)]
        here = pl.ds(g * in_group, in_group)
        grad = mm(x, all_rows(dproj[...]), TN).astype(bf16)
        ins.data[here, :, 0:PROJ] = grad.reshape(in_group, ins.rows, PROJ)
        grad = mm(x, all_rows(dstep[...]), TN).astype(bf16)
        grad = jnp.concatenate([grad, jnp.zeros((group, 120), bf16)], axis=1)
        ins.data[here, :, PROJ:] = grad.reshape(in_group, ins.rows, 128)
        if ins.bits:
            ins.start(0, g * in_group // 2, (g + 1) * in_group // 2)

    def embed_group(g):
        x = all_rows(line.full[:, :, :, pl.ds(pl.multiple_of(g * group, group), group)])
        grad = mm(x, all_rows(patches[...]), TN).astype(bf16)
        emb.data[pl.ds(g * in_group, in_group)] = grad.reshape(
            in_group, emb.rows, grad.shape[1]
        )
        if emb.bits:
            emb.start(0, g * in_group // 2, (g + 1) * in_group // 2)

    fetch.start()
    enter_both(dp, size)
    first = jnp.zeros((16, width), f32)
    small.parts[0] = first
    small.parts[0, 0:4, 0:768] = dtaps[...]
    small.parts[0, 4:5, 0:512] = dgain[...]
    small.parts[0, 5:6, 0:512] = dskip[...]
    small.parts[0, 6:8, 0:8] = dheads[...]
    small.parts[0, 8:9] = two_gain_grad[...]
    produce(0)
    fetch.copies[0].wait()

    def iteration(i, _):
        line.move(i, finish)

        @pl.when(i + 1 < steps)
        def _():
            produce(i + 1)

        @pl.when(i < groups)
        def _():
            weight_group(i)

        for stage in range(ins.bits):

            @pl.when(i == groups + (8 * stage) // max(ins.bits - 1, 1))
            def _(stage=stage):
                ins.finish(stage)
                if stage + 1 < ins.bits:
                    ins.start(stage + 1)

        return 0

    lax.fori_loop(0, steps + line.lag(), iteration, 0)
    small.start(0)
    fetch.copies[1].wait()
    fetch.copies[2].wait()

    def each_group(g, _):
        embed_group(g)
        return 0

    lax.fori_loop(0, groups, each_group, 0)
    lax.fori_loop(0, size, consume, 0)
    in_out[...] = ins.data[ins.me]
    hops = len(small.hops)
    for turn in range(max(hops, emb.bits)):
        if turn < hops:
            small.finish(turn)
            if turn + 1 < hops:
                small.start(turn + 1)
        if turn < emb.bits:
            emb.finish(turn)
            if turn + 1 < emb.bits:
                emb.start(turn + 1)
    small_out[0:8] = small.parts[dp.bit_length() - 1, 0:8]
    small_out[8:16] = small.parts[hops, 8:16]
    embed_out[...] = emb.data[emb.me]
    lax.fori_loop(0, size, given, 0)
    line.leave()
    ins.leave()
    emb.leave()
    small.leave()


def last_kernel(patch_in, embed_in, ins, mids, small, resid, ffn, place, patch_out, result,
                embed_out, gz, gx, gb, gc, gq, gk, gv, gs, t0, t1, t2, hb, hr, hs, inner_gain,
                gmo, gao, ggate, gup, gdown, gain_one, gain_two, held, sem):
    rows = patch_in.shape[0] // 4
    pieces = [pl.ds(n * rows, rows) for n in range(4)]
    takes = [pltpu.make_async_copy(patch_in.at[p], held.at[p], sem.at[n]) for n, p in enumerate(pieces)]
    gives = [pltpu.make_async_copy(held.at[p], patch_out.at[p], sem.at[4 + n]) for n, p in enumerate(pieces)]
    for take in takes:
        take.start()
    result[...] = (resid[...] + ffn[...].astype(f32)).astype(bf16)
    start = 0
    for out in (gz, gx, gb, gc, gq, gk, gv):
        out[...] = ins[:, start : start + out.shape[1]].astype(f32)
        start = start + out.shape[1]
    steps_part = ins[:, start:].astype(f32)
    gs[...] = steps_part.T[0 : gs.shape[0], :] if gs.shape[1] % 128 == 0 else steps_part[:, 0 : gs.shape[1]]
    units, inner = ggate.shape[1], t0.shape[1]
    ggate[...] = mids[:, 0:units].astype(f32)
    gup[...] = mids[:, units : 2 * units].astype(f32)
    for take, give in zip(takes, gives):
        take.wait()
        give.start()
    flipped = mids[:, 2 * units :].astype(f32)
    outs = ((gdown, flipped[:, 0:units]), (gmo, flipped[:, units : units + inner]),
            (gao, flipped[:, units + inner :]), (embed_out, embed_in[...].astype(f32)))
    for out, value in outs:
        out[...] = value.T if out.shape != value.shape else value
    t0[...] = small[0:4, 0 : t0.shape[1]]
    t1[...] = small[0:4, t0.shape[1] : t0.shape[1] + t1.shape[1]]
    t2[...] = small[0:4, t0.shape[1] + t1.shape[1] : t0.shape[1] + 2 * t1.shape[1]]
    hb[...] = small[6:7, 0 : hb.shape[1]]
    hr[...] = small[7:8, 0 : hr.shape[1]]
    hs[...] = small[5:6, 0 : hs.shape[1]]
    inner_gain[...] = small[4:5, 0 : inner_gain.shape[1]]
    width, share = small.shape[1], gain_one.shape[1]
    chosen = (iota((width, share), 0) == iota((width, share), 1) + place[0] * share).astype(bf16)
    gains = sum(mm(term, chosen) for term in parts_of(small[8:16, :], 3))
    gain_two[...] = gains[0:1, :]
    gain_one[...] = gains[1:2, :]
    for give in gives:
        give.wait()


def shards(
    patches,
    keep_mask,
    segments,
    embed_weight,
    first_gain,
    mamba_gate,
    mamba_input,
    state_in,
    state_out,
    step_weight,
    conv_input,
    conv_statein,
    conv_stateout,
    step_bias,
    rate_log,
    skip_gain,
    inner_gain,
    mamba_output,
    query_weight,
    key_weight,
    value_weight,
    attn_output,
    second_gain,
    ffn_gate,
    ffn_up,
    ffn_down,
    out_grad,
):
    size = lax.axis_size("tp")
    segment = segments[0]
    length = patches.shape[0]
    mine = length // size
    sub = mine // STEPS
    shape = (size, STEPS, sub)
    width = embed_weight.shape[1]
    keep_rows = keep_mask.astype(f32).reshape(STEPS, sub, 1)
    seg_row = segment.astype(f32)[None]
    taps = (conv_input, conv_statein, conv_stateout)
    core_params = (step_bias[None], rate_log[None], skip_gain[None], inner_gain[None])
    in_list = (
        mamba_gate,
        mamba_input,
        state_in,
        state_out,
        query_weight,
        key_weight,
        value_weight,
        step_weight.T,
    )
    one_gain, two_gain = first_gain[None], second_gain[None]
    buffers = Line.scratch(size, STEPS, sub, width)
    og_low, og_high = out_grad[: mine // 2], out_grad[mine // 2 :]
    og_low = lax.all_gather(og_low, "tp", axis=0)

    resid_one, full_one, projected, step_raw = comm_call(
        functools.partial(embed_kernel, size),
        (
            sds((STEPS, sub, width), f32),
            sds((*shape, width), bf16),
            sds((*shape, PROJ), bf16),
            sds((*shape, step_weight.shape[1]), f32),
        ),
        [pltpu.VMEM(member.shape, bf16) for member in in_list[:7]]
        + [pltpu.SemaphoreType.DMA((7,))]
        + buffers,
        1,
        patches.reshape(*shape, patches.shape[1]),
        embed_weight,
        keep_rows,
        one_gain,
        *in_list,
        kept=(4, 5, 6, 7, 8, 9, 10),
    )
    og_low, og_high, projected = lax.optimization_barrier((og_low, og_high, projected))
    og_high = lax.all_gather(og_high, "tp", axis=0)
    projected = projected.reshape(length, PROJ)
    step_raw = step_raw.reshape(length, step_weight.shape[1])
    mix_in, ssd, states, lse = mixer_fwd(size, projected, step_raw, seg_row, taps, *core_params)
    inner_width = mamba_output.shape[0]
    hidden_width = ffn_gate.shape[1]
    rows16 = sds((*shape, width), bf16)
    rows32 = sds((STEPS, sub, width), f32)
    mixed = mix_in.shape[1]
    half_shape = (size, STEPS // 2, sub, width)
    resid_grad, ffn_part, resid_two, dmix, grads, second_gain_grad = comm_call(
        functools.partial(ffn_kernel, size),
        (
            rows32, rows16, rows32, sds((*shape, mixed), bf16),
            sds((width, 3 * hidden_width + mixed), bf16), sds((1, width), f32),
        ),
        [pltpu.VMEM((*shape, hidden_width), bf16)] * 3
        + [
            pltpu.VMEM(ffn_gate.shape, bf16),
            pltpu.VMEM(ffn_up.shape, bf16),
            pltpu.VMEM(ffn_down.shape, bf16),
            pltpu.VMEM(half_shape, bf16),
            pltpu.VMEM(half_shape, bf16),
            pltpu.VMEM((width, 3 * hidden_width + mixed), bf16),
            pltpu.SemaphoreType.DMA((6 + width // 256,)),
        ]
        + buffers
        + buffers,
        2,
        mix_in.reshape(*shape, mixed),
        mamba_output,
        attn_output,
        resid_one,
        two_gain,
        ffn_gate,
        ffn_up,
        ffn_down,
        og_low.reshape(half_shape),
        og_high.reshape(half_shape),
        out_grad.reshape(STEPS, sub, width),
        kept=(5, 6, 7, 8, 9),
        given=(4,),
    )
    ffn_sum = lax.psum_scatter(
        ffn_part.reshape(length, width), "tp", scatter_dimension=0, tiled=True
    )
    mid_sum = lax.psum_scatter(grads, "dp", scatter_dimension=0, tiled=True)
    proj_grad, step_grad, dtaps, dheads, dgain, dskip = mixer_bwd(
        size, projected, step_raw, seg_row, taps, *core_params, mix_in, ssd, states, lse,
        dmix.reshape(length, mixed),
    )
    dp = lax.axis_size("dp")
    block = width // dp
    features = patches.shape[1]
    patches_grad, embed_sum, in_sum, small = comm_call(
        functools.partial(entry_kernel, size, dp),
        (
            sds((*shape, features), bf16),
            sds((block, features), bf16),
            sds((block, PROJ + 128), bf16),
            sds((16, width), f32),
        ),
        [
            pltpu.VMEM((length, width), bf16),
            pltpu.VMEM(embed_weight.shape, bf16),
            pltpu.VMEM((*shape, features), bf16),
            pltpu.VMEM((*shape, features), bf16),
            pltpu.SemaphoreType.DMA((3 + size,)),
        ]
        + buffers
        + Halving.scratch(dp, block, PROJ + 128)
        + Halving.scratch(dp, block, features)
        + Doubling.scratch(dp, size, 16, width),
        3,
        proj_grad.reshape(*shape, PROJ),
        step_grad.reshape(*shape, step_grad.shape[1]),
        *in_list,
        resid_one,
        one_gain,
        resid_grad,
        keep_rows,
        embed_weight,
        full_one.reshape(length, width),
        patches.reshape(*shape, features),
        dtaps,
        dheads,
        dgain,
        dskip,
        second_gain_grad,
        kept=(14, 15, 16),
        given=(0,),
    )
    place = (lax.axis_index("dp") * size + lax.axis_index("tp"))[None]
    flip = block % 128 == 0

    def turned(rows):
        return sds((rows, block) if flip else (block, rows), f32)

    outs = pl.pallas_call(
        last_kernel,
        out_shape=(
            sds((length, features), bf16),
            sds((mine, width), bf16),
            turned(features),
            *[sds((block, member.shape[1]), f32) for member in in_list[:7]],
            turned(step_weight.shape[1]),
            *[sds(member.shape, f32) for member in taps],
            *[sds((1, step_bias.shape[0]), f32)] * 3,
            sds((1, inner_width), f32),
            turned(inner_width),
            turned(attn_output.shape[0]),
            sds((block, hidden_width), f32),
            sds((block, hidden_width), f32),
            turned(hidden_width),
            sds((1, block // size), f32),
            sds((1, block // size), f32),
        ),
        in_specs=[pl.BlockSpec(memory_space=pl.ANY)]
        + [pl.BlockSpec(memory_space=pltpu.VMEM)] * 6
        + [pl.BlockSpec(memory_space=pltpu.SMEM)],
        out_specs=(
            pl.BlockSpec(memory_space=pl.ANY),
            *[pl.BlockSpec(memory_space=pltpu.VMEM)] * 24,
        ),
        scratch_shapes=[pltpu.VMEM((length, features), bf16), pltpu.SemaphoreType.DMA((8,))],
        compiler_params=pltpu.CompilerParams(vmem_limit_bytes=60 * 2**20),
    )(
        patches_grad.reshape(length, features),
        embed_sum,
        in_sum,
        mid_sum,
        small,
        resid_two.reshape(mine, width),
        ffn_sum,
        place,
    )
    (
        patches_grad, result, embed_cols, gz, gx, gb, gc, gq, gk, gv, gs, t0, t1, t2, hb, hr, hs,
        inner_grad, gmo, gao, ggate, gup, gdown, gain_one, gain_two,
    ) = outs
    if flip:
        gs = gs.T
    else:
        embed_cols, gmo, gao, gdown = embed_cols.T, gmo.T, gao.T, gdown.T
    return (
        result,
        patches_grad,
        embed_cols,
        gain_one[0],
        gz,
        gx,
        gb,
        gc,
        gs,
        t0,
        t1,
        t2,
        hb[0],
        hr[0],
        hs[0],
        inner_grad[0],
        gmo,
        gq,
        gk,
        gv,
        gao,
        gain_two[0],
        ggate,
        gup,
        gdown,
    )


def solution(mesh):
    return jax.shard_map(
        shards,
        mesh=mesh,
        in_specs=(
            P("dp", "tp"),
            P(("dp", "tp")),
            P("dp", None),
            P("tp", None),
            P(),
            P(None, "tp"),
            P(None, "tp"),
            P(None, "tp"),
            P(None, "tp"),
            P(None, "tp"),
            P(None, "tp"),
            P(None, "tp"),
            P(None, "tp"),
            P("tp"),
            P("tp"),
            P("tp"),
            P("tp"),
            P("tp", None),
            P(None, "tp"),
            P(None, "tp"),
            P(None, "tp"),
            P("tp", None),
            P(),
            P(None, "tp"),
            P(None, "tp"),
            P("tp", None),
            P(("dp", "tp"), None),
        ),
        out_specs=(
            P(("dp", "tp"), None),
            P("dp", "tp"),
            P("tp", "dp"),
            P(("dp", "tp")),
            P("dp", "tp"),
            P("dp", "tp"),
            P("dp", "tp"),
            P("dp", "tp"),
            P("dp", "tp"),
            P(None, "tp"),
            P(None, "tp"),
            P(None, "tp"),
            P("tp"),
            P("tp"),
            P("tp"),
            P("tp"),
            P("tp", "dp"),
            P("dp", "tp"),
            P("dp", "tp"),
            P("dp", "tp"),
            P("tp", "dp"),
            P(("dp", "tp")),
            P("dp", "tp"),
            P("dp", "tp"),
            P("tp", "dp"),
        ),
        check_vma=False,
    )
```

```python
import functools

import jax
import jax.numpy as jnp
from jax import lax
from jax.experimental import pallas as pl
from jax.experimental.pallas import tpu as pltpu
from jax.sharding import PartitionSpec as P

f32 = jnp.float32
bf16 = jnp.bfloat16
eps = 1e-05
NST = 128
LOG2E = 1.4426950408889634
LOW = -1e30
NN = ((1,), (0,))
NT = ((1,), (1,))
TN = ((0,), (0,))
PROJ = 2048
STEPS = 8


def mm(a, b, dims=NN):
    return lax.dot_general(a, b, (dims, ((), ())), preferred_element_type=f32)


def parts_of(v, count):
    terms = []
    for _ in range(count):
        term = v.astype(bf16)
        terms.append(term)
        v = v - term.astype(f32)
    return terms


def pick(chosen, v, dims=NN, count=3):
    total = None
    for term in parts_of(v, count):
        product = mm(chosen, term, dims)
        total = product if total is None else total + product
    return total


def iota(shape, axis):
    return lax.broadcasted_iota(jnp.int32, shape, axis)


def expand(v):
    low_half = iota((1, 128), 1) < 64
    return jnp.concatenate(
        [
            jnp.where(low_half, v[:, h : h + 1], v[:, h + 1 : h + 2])
            for h in range(0, v.shape[1], 2)
        ],
        axis=1,
    )


def head_sum(v):
    owner = (iota((512, 8), 0) // 64 == iota((512, 8), 1)).astype(bf16)
    high, low = parts_of(v, 2)
    return mm(high, owner) + mm(low, owner)


def softplus(v):
    return jnp.maximum(v, 0.0) + jnp.log1p(jnp.exp(-jnp.abs(v)))


def tile4(v):
    return jnp.concatenate([v, v, v, v], axis=1)


def fill_segments(seg_ref, segcol):
    length = seg_ref.shape[1]
    segcol[0:8, :] = jnp.full((8, 128), -1.0, f32)
    segcol[length + 8 : length + 16, :] = jnp.full((8, 128), -2.0, f32)
    for row in range(0, length, 128):
        piece = jnp.broadcast_to(seg_ref[0:1, row : row + 128], (128, 128))
        segcol[8 + row : 8 + row + 128, :] = piece.T


def taps_of(taps, tile):
    if tile < 4:
        return taps[0][:, tile * 128 : tile * 128 + 128]
    return taps[tile - 3][...]


def conv_masks(rows, segx):
    here = segx[8 : 8 + rows, :]
    return [(segx[8 - lag : 8 - lag + rows, :] == here).astype(f32) for lag in (1, 2, 3)]


def conv_pre(tile, rows, uext, masks, taps):
    lanes = slice(tile * 128, tile * 128 + 128)
    w = taps_of(taps, tile)
    pre = uext[8 : 8 + rows, lanes] * w[0:1, :]
    for lag in (1, 2, 3):
        shifted = uext[8 - lag : 8 - lag + rows, lanes] * masks[lag - 1]
        pre = pre + shifted * w[lag : lag + 1, :]
    return pre


def load_inputs(first, rows, proj, segcol, uext, segx):
    @pl.when(first == 0)
    def _():
        uext[0:8, :] = jnp.zeros((8, 768), f32)

    @pl.when(first > 0)
    def _():
        uext[0:8, :] = proj[pl.ds(pl.multiple_of(first - 16, 16), 16), 512:1280].astype(f32)[8:16]

    uext[8 : 8 + rows, :] = proj[pl.ds(first, rows), 512:1280].astype(f32)
    segx[...] = segcol[pl.ds(first, rows + 16), :]


def decays(first, rows, step, bias, rate):
    raw = step[pl.ds(first, rows), :] + bias[...]
    size = softplus(raw)
    logs = size * -jnp.exp(rate[...])
    scaled = logs * LOG2E
    lower = (iota((rows, rows), 0) >= iota((rows, rows), 1)).astype(bf16)
    cum = pick(lower, scaled)
    wide = jnp.concatenate([cum, jnp.zeros((rows, 120), f32)], axis=1)
    return raw, size, logs, cum, wide.T[0:8, :]


def half_masks():
    low_half = iota((1, 128), 1) < 64
    return low_half, jnp.logical_not(low_half)


def keep(mask, v):
    return jnp.where(mask, v, jnp.zeros_like(v))


def mixer_fwd_chunk(
    index, rows, proj, step, seg, segcol, taps, bias, rate, skip, gain, uext, segx, state,
    oacc, stats, mix_out, ssd_out, states_out, lse_out, hook,
):
    first = pl.multiple_of(index * rows, rows)
    here = pl.ds(first, rows)
    halves = half_masks()
    load_inputs(first, rows, proj, segcol, uext, segx)
    masks = conv_masks(rows, segx)
    acts = []
    for tile in range(6):
        pre = conv_pre(tile, rows, uext, masks, taps)
        acts.append(pre * jax.nn.sigmoid(pre))
    xc = jnp.concatenate(acts[0:4], axis=1)
    bc, cc = acts[4].astype(bf16), acts[5].astype(bf16)
    _, size, _, cum, cumr = decays(first, rows, step, bias, rate)
    segc = segx[8 : 8 + rows, :]
    before = segx[7:8, :]
    goes_on = (segc == before).astype(f32)
    segr = seg[0:1, here]
    wide_seg = jnp.concatenate([segc] * (rows // 128), axis=1)
    allowed = (iota((rows, rows), 0) >= iota((rows, rows), 1)) & (wide_seg == segr)
    away = jnp.where(allowed, 0.0, LOW)
    hook(0)
    cb = mm(cc, bc, NT)
    xs = xc * expand(size)
    xsb = xs.astype(bf16)
    parts = []
    for pair in range(4):
        lhs = []
        for h in (2 * pair, 2 * pair + 1):
            gap = cum[:, h : h + 1] - cumr[h : h + 1, :] + away
            lhs.append((cb * jnp.exp2(gap)).astype(bf16))
        xp = xsb[:, pair * 128 : pair * 128 + 128]
        rhs = jnp.concatenate([keep(halves[0], xp), keep(halves[1], xp)], axis=0)
        parts.append(mm(jnp.concatenate(lhs, axis=1), rhs))
        if pair == 1:
            hook(1)
    ssd = jnp.concatenate(parts, axis=1) + xc * expand(skip[...])
    st = state[...]
    stb = st.astype(bf16)
    states_out[index] = stb
    ssd = ssd + mm(cc, stb) * expand(jnp.exp2(cum)) * tile4(goes_on)
    last = cum[rows - 1 : rows, :]
    fits = (segc == segc[rows - 1 : rows, :]).astype(f32)
    weight = expand(jnp.exp2(last - cum)) * tile4(fits)
    added = mm(bc, (xs * weight).astype(bf16), TN)
    passes = (segc[rows - 1 : rows, :] == before).astype(f32)
    state[...] = st * (expand(jnp.exp2(last)) * tile4(passes)) + added
    hook(2)
    ssd_out[here, :] = ssd.astype(bf16)
    z = proj[here, 0:512].astype(f32)
    g = ssd * (z * jax.nn.sigmoid(z))
    r = lax.rsqrt(jnp.mean(g * g, axis=1, keepdims=True) + eps)
    mix_out[here, 0:512] = (g * r * gain[...]).astype(bf16)
    hook(3)
    own_seg = seg[0:1, here]

    def keys(block, fresh):
        start = pl.multiple_of(block * rows, rows)
        away = attention_away(start, first, rows, own_seg, segcol)
        for pair in range(2):
            lanes = pair * 128
            q = proj[here, 1280 + lanes : 1408 + lanes] * jnp.asarray(0.125, bf16)
            k = proj[pl.ds(start, rows), 1536 + lanes : 1664 + lanes]
            v = proj[pl.ds(start, rows), 1792 + lanes : 1920 + lanes]
            for half in range(2):
                h = 2 * pair + half
                mine = slice(h * 64, h * 64 + 64)
                s = mm(k, keep(halves[half], q), NT) + away
                peak = jnp.max(s, axis=0, keepdims=True)
                if not fresh:
                    old = stats[h : h + 1, :]
                    peak = jnp.maximum(peak, old)
                    fade = jnp.exp(old - peak)
                p = jnp.exp(s - peak)
                total = jnp.sum(p, axis=0, keepdims=True)
                o = mm(v, p.astype(bf16), TN)[half * 64 : half * 64 + 64, :]
                if not fresh:
                    total = total + stats[h + 4 : h + 5, :] * fade
                    o = o + oacc[mine, :] * fade
                stats[h : h + 1, :] = peak
                stats[h + 4 : h + 5, :] = total
                oacc[mine, :] = o

    keys(index, True)

    def earlier(block, _):
        keys(block, False)
        return 0

    lax.fori_loop(0, index, earlier, 0)
    lse_out[0:4, here] = stats[0:4, :] + jnp.log(stats[4:8, :])
    for h in range(4):
        mine = slice(h * 64, h * 64 + 64)
        oacc[mine, :] = oacc[mine, :] * (1.0 / stats[h + 4 : h + 5, :])
    for pair in range(2):
        mine = slice(pair * 128, pair * 128 + 128)
        mix_out[here, 512 + pair * 128 : 640 + pair * 128] = oacc[mine, :].T.astype(bf16)


def attention_away(start, first, rows, own_seg, segcol):
    key_seg = segcol[pl.ds(start + 8, rows), :]
    wide = jnp.concatenate([key_seg] * (rows // 128), axis=1)
    allowed = (wide == own_seg) & (
        iota((rows, rows), 0) + start <= iota((rows, rows), 1) + first
    )
    return jnp.where(allowed, 0.0, LOW)


def mixer_bwd_chunk(
    index, rows, proj, step, seg, segcol, taps, bias, rate, skip, gain, uext, segx, slopes, dext,
    dstate, dkv, dqs, mix, ssd_in, states_in, lse_in, dmix, dproj, dstep, dtaps, dheads, dgain, dskip,
    begin,
):
    first = pl.multiple_of(index * rows, rows)
    here = pl.ds(first, rows)
    halves = half_masks()
    load_inputs(first, rows, proj, segcol, uext, segx)
    masks = conv_masks(rows, segx)
    acts = []
    for tile in range(6):
        pre = conv_pre(tile, rows, uext, masks, taps)
        sig = jax.nn.sigmoid(pre)
        acts.append(pre * sig)
        slopes[:, tile * 128 : tile * 128 + 128] = sig * (1.0 + pre * (1.0 - sig))
    xc = jnp.concatenate(acts[0:4], axis=1)
    bc, cc = acts[4].astype(bf16), acts[5].astype(bf16)
    begin()
    raw, size, logs, cum, cumr = decays(first, rows, step, bias, rate)
    z = proj[here, 0:512].astype(f32)
    ssd = ssd_in[here, :].astype(f32)
    dmo = dmix[here, 0:512].astype(f32)
    sig = jax.nn.sigmoid(z)
    act = z * sig
    g = ssd * act
    r = lax.rsqrt(jnp.mean(g * g, axis=1, keepdims=True) + eps)
    gain_part = jnp.sum(dmo * g * r, axis=0, keepdims=True)
    a = dmo * gain[...]
    dg = r * a - (r * r * r) * g * jnp.mean(a * g, axis=1, keepdims=True)
    dssd = dg * act
    dproj[here, 0:512] = (dg * ssd * (sig * (1.0 + z * (1.0 - sig)))).astype(bf16)
    skip_part = jnp.sum(dssd * xc, axis=0, keepdims=True)
    dxc = dssd * expand(skip[...])
    dyb = dssd.astype(bf16)
    wide_size = expand(size)
    xs = xc * wide_size
    xsb = xs.astype(bf16)
    segc = segx[8 : 8 + rows, :]
    before = segx[7:8, :]
    goes_on = (segc == before).astype(f32)
    segr = seg[0:1, here]
    wide_seg = jnp.concatenate([segc] * (rows // 128), axis=1)
    allowed = (iota((rows, rows), 0) <= iota((rows, rows), 1)) & (wide_seg == segr)
    away = jnp.where(allowed, 0.0, LOW)
    cbt = mm(bc, cc, NT)
    dcbt = jnp.zeros((rows, rows), f32)
    to_rows = []
    from_rows = jnp.zeros((rows, 8), f32)
    parts = []
    for pair in range(4):
        lanes = slice(pair * 128, pair * 128 + 128)
        lhs, rhs = [], []
        for half in range(2):
            h = 2 * pair + half
            lt = jnp.exp2(cumr[h : h + 1, :] - cum[:, h : h + 1] + away)
            mt = cbt * lt
            lhs.append(mt.astype(bf16))
            rhs.append(keep(halves[half], dyb[:, lanes]))
            dl = mm(keep(halves[half], xsb[:, lanes]), dyb[:, lanes], NT)
            dcbt = dcbt + dl * lt
            gt = dl * mt
            to_rows.append(jnp.sum(gt, axis=0, keepdims=True))
            from_rows = jnp.where(
                iota((1, 8), 1) == h, jnp.sum(gt, axis=1, keepdims=True), from_rows
            )
        parts.append(mm(jnp.concatenate(lhs, axis=1), jnp.concatenate(rhs, axis=0)))
    dxs = jnp.concatenate(parts, axis=1)
    dcb = dcbt.astype(bf16)
    db = mm(dcb, cc)
    dc = mm(dcb, bc, TN)
    upper = (iota((rows, rows), 0) <= iota((rows, rows), 1)).astype(bf16)
    late = -from_rows
    reach = expand(jnp.exp2(cum)) * tile4(goes_on)
    stb = states_in[index]
    dye = dssd * reach
    dyeb = dye.astype(bf16)
    dc = dc + mm(dyeb, stb, NT)
    late = late + head_sum(dye * mm(cc, stb))
    into_state = mm(cc, dyeb, TN)
    last = cum[rows - 1 : rows, :]
    fits = (segc == segc[rows - 1 : rows, :]).astype(f32)
    weight = expand(jnp.exp2(last - cum)) * tile4(fits)
    dst = dstate[...]
    dsb = dst.astype(bf16)
    dxi = mm(bc, dsb) * weight
    dxs = dxs + dxi
    db = db + mm((xs * weight).astype(bf16), dsb, NT)
    strict = (iota((rows, rows), 0) > iota((rows, rows), 1)).astype(bf16)
    dlog = pick(strict, head_sum(xs * dxi))
    passes = (segc[rows - 1 : rows, :] == before).astype(f32)
    fade = expand(jnp.exp2(last)) * tile4(passes)
    through = jnp.sum(stb.astype(f32) * dst, axis=0, keepdims=True) * fade
    dlog = dlog + head_sum(jnp.broadcast_to(through, (8, 512)))[0:1, :]
    dstate[...] = dst * fade + into_state
    dlog = dlog + pick(upper, late) + pick(upper, jnp.concatenate(to_rows, axis=0), NT)
    dsize = head_sum(dxs * xc) - dlog * jnp.exp(rate[...])
    rate_part = jnp.sum(dlog * logs, axis=0, keepdims=True)
    draw = dsize * jax.nn.sigmoid(raw)
    bias_part = jnp.sum(draw, axis=0, keepdims=True)
    dstep[here, :] = draw.astype(dstep.dtype)
    dxc = dxc + dxs * wide_size
    dacts = [dxc[:, t * 128 : t * 128 + 128] for t in range(4)] + [db, dc]
    dext[rows : rows + 8, :] = dext[0:8, :]
    ahead = [(segx[8 + lag : 8 + lag + rows, :] == segc).astype(f32) for lag in (1, 2, 3)]
    for tile in range(6):
        lanes = slice(tile * 128, tile * 128 + 128)
        w = taps_of(taps, tile)
        dpre = dacts[tile] * slopes[:, lanes]
        dext[0:rows, lanes] = dpre
        u = uext[8 : 8 + rows, lanes]
        du = dpre * w[0:1, :]
        sums = [jnp.sum(dpre * u, axis=0, keepdims=True)]
        for lag in (1, 2, 3):
            later = dext[lag : lag + rows, lanes] * ahead[lag - 1]
            du = du + later * w[lag : lag + 1, :]
            sums.append(jnp.sum(later * u, axis=0, keepdims=True))
        dproj[here, 512 + tile * 128 : 640 + tile * 128] = du.astype(bf16)
        sums = jnp.concatenate(sums, axis=0)
        dtaps[:, lanes] = dtaps[:, lanes] + sums
    head_parts = jnp.concatenate([bias_part, rate_part], axis=0)
    dheads[...] = dheads[...] + head_parts
    dgain[...] = dgain[...] + gain_part
    dskip[...] = dskip[...] + skip_part
    own_seg = seg[0:1, here]
    dos = [dmix[here, 512 + pair * 128 : 640 + pair * 128] for pair in range(2)]
    owner = (iota((8, 256), 1) // 64 == iota((8, 256), 0)).astype(bf16)
    delta = pick(
        owner,
        jnp.concatenate(dos, axis=1).astype(f32) * mix[here, 512:768].astype(f32),
        NT,
        2,
    )
    dqs[...] = jnp.zeros_like(dqs)

    def keys(block, _):
        start = pl.multiple_of(block * rows, rows)
        there = pl.ds(start, rows)
        away = attention_away(start, first, rows, own_seg, segcol)
        for pair in range(2):
            lanes = pair * 128
            q = proj[here, 1280 + lanes : 1408 + lanes] * jnp.asarray(0.125, bf16)
            k = proj[there, 1536 + lanes : 1664 + lanes]
            v = proj[there, 1792 + lanes : 1920 + lanes]
            ps, dss, qms, doms = [], [], [], []
            for half in range(2):
                h = 2 * pair + half
                mine = slice(h * 64, h * 64 + 64)
                qm, dom = keep(halves[half], q), keep(halves[half], dos[pair])
                p = jnp.exp(mm(k, qm, NT) + away - lse_in[h : h + 1, here])
                dp = mm(v, dom, NT)
                ds = (p * (dp - delta[h : h + 1, :])).astype(bf16)
                dqs[mine, :] = dqs[mine, :] + mm(k, ds, TN)[half * 64 : half * 64 + 64, :]
                ps.append(p.astype(bf16))
                dss.append(ds)
                qms.append(qm)
                doms.append(dom)
            kl, vl = slice(lanes, lanes + 128), slice(256 + lanes, 384 + lanes)
            dkv[there, kl] = dkv[there, kl] + mm(
                jnp.concatenate(dss, axis=1), jnp.concatenate(qms, axis=0)
            )
            dkv[there, vl] = dkv[there, vl] + mm(
                jnp.concatenate(ps, axis=1), jnp.concatenate(doms, axis=0)
            )
        return 0

    lax.fori_loop(0, index + 1, keys, 0)
    for pair in range(2):
        mine = slice(pair * 128, pair * 128 + 128)
        dproj[here, 1280 + pair * 128 : 1408 + pair * 128] = (dqs[mine, :] * 0.125).T.astype(bf16)
    dproj[here, 1536:2048] = dkv[here, :].astype(bf16)


def bwd_kernel(count, dp, proj, step, seg, t0, t1, t2, bias, rate, skip, gain, mix, ssd_in,
               states_in, lse_in, dmix, grads_in, dproj, dstep, dtaps, dheads, dgain, dskip,
               grads_out, segcol, uext, segx, slopes, dext, dstate, dkv, dqs, load, *scratch):
    rows = proj.shape[0] // count
    sums = Halving(*scratch)
    take = pltpu.make_async_copy(grads_in, sums.data, load)
    take.start()
    enter_pairs(dp)
    fill_segments(seg, segcol)
    for ref in (dtaps, dheads, dgain, dskip, dstate, dkv):
        ref[...] = jnp.zeros_like(ref)
    dext[0:8, :] = jnp.zeros((8, 768), f32)

    def chunk(turn, _):
        def begin():
            @pl.when(turn == 0)
            def _():
                take.wait()
                if sums.bits:
                    sums.start(0)

        mixer_bwd_chunk(count - 1 - turn, rows, proj, step, seg, segcol, (t0, t1, t2), bias,
                        rate, skip, gain, uext, segx, slopes, dext, dstate, dkv, dqs, mix, ssd_in,
                        states_in, lse_in, dmix, dproj, dstep, dtaps, dheads, dgain, dskip,
                        begin)
        for stage in range(sums.bits):

            @pl.when(turn == -(-stage * (count - 1) // max(sums.bits - 1, 1)))
            def _(stage=stage):
                sums.finish(stage)
                if stage + 1 < sums.bits:
                    sums.start(stage + 1)

        return 0

    lax.fori_loop(0, count, chunk, 0)
    grads_out[...] = sums.data[sums.me]
    sums.leave()
    dskip8 = head_sum(jnp.broadcast_to(dskip[...], (8, 512)))
    dskip[0:1, 0:8] = dskip8[0:1, :]


def mixer_bwd(count, proj, step, seg, taps, bias, rate, skip, gain, mix, ssd, states, lse, dmix, grads):
    length = proj.shape[0]
    rows = length // count
    dp, block, columns = grads.shape
    return pl.pallas_call(
        functools.partial(bwd_kernel, count, dp),
        out_shape=(
            jax.ShapeDtypeStruct((length, 2048), bf16),
            jax.ShapeDtypeStruct((length, 8), bf16),
            jax.ShapeDtypeStruct((4, 768), f32),
            jax.ShapeDtypeStruct((2, 8), f32),
            jax.ShapeDtypeStruct((1, 512), f32),
            jax.ShapeDtypeStruct((1, 512), f32),
            jax.ShapeDtypeStruct((block, columns), bf16),
        ),
        in_specs=[pl.BlockSpec(memory_space=pltpu.VMEM)] * 15
        + [pl.BlockSpec(memory_space=pl.ANY)],
        scratch_shapes=[
            pltpu.VMEM((length + 16, 128), f32),
            pltpu.VMEM((rows + 8, 768), f32),
            pltpu.VMEM((rows + 16, 128), f32),
            pltpu.VMEM((rows, 768), f32),
            pltpu.VMEM((rows + 8, 768), f32),
            pltpu.VMEM((NST, 512), f32),
            pltpu.VMEM((length, 512), f32),
            pltpu.VMEM((256, rows), f32),
            pltpu.SemaphoreType.DMA,
        ]
        + Halving.scratch(dp, block, columns),
        compiler_params=pltpu.CompilerParams(
            collective_id=5, has_side_effects=True, vmem_limit_bytes=60 * 2**20
        ),
    )(proj, step, seg, *taps, bias, rate, skip, gain, mix, ssd, states, lse, dmix, grads)


MESH = pl.DeviceIdType.MESH


class Line:
    def __init__(self, scratch, size, hop=1):
        self.hop = hop
        (self.own, self.left, self.right, self.full, self.acc,
         self.ss, self.sr, self.gs, self.gr) = scratch
        self.size = size
        self.steps = self.own.shape[1]
        self.me = lax.axis_index("tp")
        self.last = size - 1

    @staticmethod
    def scratch(size, steps, sub, width):
        return [
            pltpu.VMEM((size, steps, sub, width), f32),
            pltpu.VMEM((size, steps, sub, width), bf16),
            pltpu.VMEM((size, steps, sub, width), bf16),
            pltpu.VMEM((size, steps, sub, width), bf16),
            pltpu.VMEM((sub, width), f32),
            pltpu.SemaphoreType.DMA((2, size, steps)),
            pltpu.SemaphoreType.DMA((2, size, steps)),
            pltpu.SemaphoreType.DMA((2, size, steps)),
            pltpu.SemaphoreType.DMA((2, size, steps)),
        ]

    def sum_copy(self, way, d, j):
        buf = self.left if way == 0 else self.right
        return pltpu.make_async_remote_copy(
            src_ref=buf.at[d, j],
            dst_ref=buf.at[d, j],
            send_sem=self.ss.at[way, d, j],
            recv_sem=self.sr.at[way, d, j],
            device_id={"tp": self.me + 1 if way == 0 else self.me - 1},
            device_id_type=MESH,
        )

    def row_copy(self, way, d, j):
        return pltpu.make_async_remote_copy(
            src_ref=self.full.at[d, j],
            dst_ref=self.full.at[d, j],
            send_sem=self.gs.at[way, d, j],
            recv_sem=self.gr.at[way, d, j],
            device_id={"tp": self.me + 1 if way == 0 else self.me - 1},
            device_id_type=MESH,
        )

    def enter(self):
        barrier = pltpu.get_barrier_semaphore()
        me, last = self.me, self.last

        @pl.when(me > 0)
        def _():
            pl.semaphore_signal(barrier, inc=1, device_id={"tp": me - 1}, device_id_type=MESH)

        @pl.when(me < last)
        def _():
            pl.semaphore_signal(barrier, inc=1, device_id={"tp": me + 1}, device_id_type=MESH)

        peers = jnp.where(me > 0, 1, 0) + jnp.where(me < last, 1, 0)
        pl.semaphore_wait(barrier, peers)

    def relay(self, way, j):
        me, last = self.me, self.last
        buf = self.left if way == 0 else self.right
        first_one = me == 0 if way == 0 else me == last

        def one(d, _):
            @pl.when(first_one)
            def _():
                buf[d, j] = self.own[d, j].astype(bf16)

            @pl.when(jnp.logical_not(first_one))
            def _():
                self.sum_copy(way, d, j).wait_recv()
                buf[d, j] = (buf[d, j].astype(f32) + self.own[d, j]).astype(bf16)

            self.sum_copy(way, d, j).start()
            return 0

        if way == 0:
            lax.fori_loop(me + 1, self.size, one, 0)
        else:
            lax.fori_loop(0, me, one, 0)

    def settle(self, j, finish):
        me, last = self.me, self.last
        self.acc[...] = self.own[me, j]

        @pl.when(me > 0)
        def _():
            self.sum_copy(0, me, j).wait_recv()
            self.acc[...] = self.acc[...] + self.left[me, j].astype(f32)

        @pl.when(me < last)
        def _():
            self.sum_copy(1, me, j).wait_recv()
            self.acc[...] = self.acc[...] + self.right[me, j].astype(f32)

        self.full[me, j] = finish(j, self.acc[...])

        @pl.when(me < last)
        def _():
            self.row_copy(0, me, j).start()

        @pl.when(me > 0)
        def _():
            self.row_copy(1, me, j).start()

    def inside(self, j):
        return jnp.logical_and(j >= 0, j < self.steps)

    def pass_on(self, i):
        me, last = self.me, self.last

        def from_left(d, _):
            j = i - self.hop * (jnp.maximum(d, last - d) + me - d)

            @pl.when(self.inside(j))
            def _():
                self.row_copy(0, d, j).wait_recv()

                @pl.when(me < last)
                def _():
                    self.row_copy(0, d, j).start()

            return 0

        def from_right(d, _):
            j = i - self.hop * (jnp.maximum(d, last - d) + d - me)

            @pl.when(self.inside(j))
            def _():
                self.row_copy(1, d, j).wait_recv()

                @pl.when(me > 0)
                def _():
                    self.row_copy(1, d, j).start()

            return 0

        lax.fori_loop(0, me, from_left, 0)
        lax.fori_loop(me + 1, self.size, from_right, 0)

    def move(self, i, finish):
        me, last = self.me, self.last
        right_step = i - self.hop * me
        left_step = i - self.hop * (last - me)
        final_step = i - self.hop * jnp.maximum(me, last - me)

        @pl.when(self.inside(right_step))
        def _():
            self.relay(0, right_step)

        @pl.when(self.inside(left_step))
        def _():
            self.relay(1, left_step)

        @pl.when(self.inside(final_step))
        def _():
            self.settle(final_step, finish)

        self.pass_on(i)

    def ready_step(self, i):
        return i - self.hop * (self.last + jnp.maximum(self.me, self.last - self.me))

    def lag(self):
        return 2 * self.hop * self.last

    def leave(self):
        me, last = self.me, self.last

        def step(j, _):
            def right_sums(d, _):
                self.sum_copy(0, d, j).wait_send()
                return 0

            def left_sums(d, _):
                self.sum_copy(1, d, j).wait_send()
                return 0

            def right_rows(d, _):
                self.row_copy(0, d, j).wait_send()
                return 0

            def left_rows(d, _):
                self.row_copy(1, d, j).wait_send()
                return 0

            lax.fori_loop(me + 1, self.size, right_sums, 0)
            lax.fori_loop(0, me, left_sums, 0)

            @pl.when(me < last)
            def _():
                lax.fori_loop(0, me + 1, right_rows, 0)

            @pl.when(me > 0)
            def _():
                lax.fori_loop(me, self.size, left_rows, 0)

            return 0

        lax.fori_loop(0, self.steps, step, 0)


HOOKS = 4


def fwd_kernel(count, proj, step, seg, t0, t1, t2, bias, rate, skip, gain, rows_in,
               mix_out, ssd_out, states_out, lse_out, rows_out, segcol, uext, segx, state, oacc, stats,
               gathered, ss, sr, load):
    rows = proj.shape[0] // count
    ring = Gather(gathered, ss, sr)
    mine = pltpu.make_async_copy(rows_in, gathered.at[ring.me], load.at[0])
    mine.start()
    ring.enter()
    mine.wait()
    ring.send_own()
    fill_segments(seg, segcol)
    lse_out[...] = jnp.zeros_like(lse_out)
    state[...] = jnp.zeros_like(state)

    hooks = count * (HOOKS + 1)
    assert hooks >= ring.turns

    def chunk(index, _):
        def hook(k):
            place = index * (HOOKS + 1) + k
            turn = place * ring.turns // hooks

            @pl.when((place + 1) * ring.turns // hooks > turn)
            def _():
                ring.move(turn)

        mixer_fwd_chunk(index, rows, proj, step, seg, segcol, (t0, t1, t2), bias, rate, skip,
                        gain, uext, segx, state, oacc, stats, mix_out, ssd_out, states_out,
                        lse_out, hook)
        hook(HOOKS)
        return 0

    lax.fori_loop(0, count, chunk, 0)

    give = pltpu.make_async_copy(gathered, rows_out, load.at[1])
    give.start()
    ring.leave()
    give.wait()


def mixer_fwd(count, proj, step, seg, taps, bias, rate, skip, gain, own_rows):
    length = proj.shape[0]
    rows = length // count
    width = own_rows.shape[2]
    pieces = own_rows.shape[0]
    shape = (count, *own_rows.shape)
    return pl.pallas_call(
        functools.partial(fwd_kernel, count),
        out_shape=(
            jax.ShapeDtypeStruct((length, 768), bf16),
            jax.ShapeDtypeStruct((length, 512), bf16),
            jax.ShapeDtypeStruct((count, NST, 512), bf16),
            jax.ShapeDtypeStruct((8, length), f32),
            jax.ShapeDtypeStruct(shape, bf16),
        ),
        in_specs=[pl.BlockSpec(memory_space=pltpu.VMEM)] * 10
        + [pl.BlockSpec(memory_space=pl.ANY)],
        out_specs=(
            *[pl.BlockSpec(memory_space=pltpu.VMEM)] * 4,
            pl.BlockSpec(memory_space=pl.ANY),
        ),
        scratch_shapes=[
            pltpu.VMEM((length + 16, 128), f32),
            pltpu.VMEM((rows + 8, 768), f32),
            pltpu.VMEM((rows + 16, 128), f32),
            pltpu.VMEM((NST, 512), f32),
            pltpu.VMEM((256, rows), f32),
            pltpu.VMEM((8, rows), f32),
            pltpu.VMEM(shape, bf16),
            pltpu.SemaphoreType.DMA((2, count, pieces)),
            pltpu.SemaphoreType.DMA((2, count, pieces)),
            pltpu.SemaphoreType.DMA((2,)),
        ],
        compiler_params=pltpu.CompilerParams(
            collective_id=4, has_side_effects=True, vmem_limit_bytes=60 * 2**20
        ),
    )(proj, step, seg, *taps, bias, rate, skip, gain, own_rows)


def enter_pairs(dp):
    barrier = pltpu.get_barrier_semaphore()
    me = lax.axis_index("dp")
    bits = dp.bit_length() - 1
    for b in range(bits):
        flip = (1 - 2 * lax.rem(me // 2**b, 2)) * 2**b
        pl.semaphore_signal(barrier, inc=1, device_id={"dp": me + flip}, device_id_type=MESH)
    pl.semaphore_wait(barrier, bits)


def flat(v):
    return v.reshape(v.shape[0] * v.shape[1], v.shape[2])


def normed(v, gain):
    return v * lax.rsqrt(jnp.mean(v * v, axis=1, keepdims=True) + eps) * gain


def normed_back(grad, v, gain):
    r = lax.rsqrt(jnp.mean(v * v, axis=1, keepdims=True) + eps)
    a = grad * gain
    back = r * a - (r * r * r) * v * jnp.mean(a * v, axis=1, keepdims=True)
    return back, jnp.sum(grad * v * r, axis=0, keepdims=True)


class Gather:
    def __init__(self, full, ss, sr):
        self.full, self.ss, self.sr = full, ss, sr
        self.size, self.pieces = full.shape[0], full.shape[1]
        self.me = lax.axis_index("tp")
        self.last = self.size - 1
        self.turns = self.pieces + 2 * self.last

    enter = Line.enter

    def copy(self, way, d, j):
        return pltpu.make_async_remote_copy(
            src_ref=self.full.at[d, j],
            dst_ref=self.full.at[d, j],
            send_sem=self.ss.at[way, d, j],
            recv_sem=self.sr.at[way, d, j],
            device_id={"tp": self.me + 1 if way == 0 else self.me - 1},
            device_id_type=MESH,
        )

    def sends(self, way):
        return self.me < self.last if way == 0 else self.me > 0

    def send_own(self):
        def piece(j, _):
            for way in range(2):

                @pl.when(self.sends(way))
                def _(way=way):
                    self.copy(way, self.me, j).start()

            return 0

        lax.fori_loop(0, self.pieces, piece, 0)

    def arrived(self, way, d, j):
        @pl.when(jnp.logical_and(j >= 0, j < self.pieces))
        def _():
            self.copy(way, d, j).wait_recv()

            @pl.when(self.sends(way))
            def _():
                self.copy(way, d, j).start()

    def move(self, turn):
        def from_left(d, _):
            self.arrived(0, d, turn - 2 * (self.me - d) + 1)
            return 0

        def from_right(d, _):
            self.arrived(1, d, turn - 2 * (d - self.me) + 1)
            return 0

        lax.fori_loop(0, self.me, from_left, 0)
        lax.fori_loop(self.me + 1, self.size, from_right, 0)

    def leave(self):
        def piece(j, _):
            def right(d, _):
                self.copy(0, d, j).wait_send()
                return 0

            def left(d, _):
                self.copy(1, d, j).wait_send()
                return 0

            @pl.when(self.me < self.last)
            def _():
                lax.fori_loop(0, self.me + 1, right, 0)

            @pl.when(self.me > 0)
            def _():
                lax.fori_loop(self.me, self.size, left, 0)

            return 0

        lax.fori_loop(0, self.pieces, piece, 0)


class Fetch:
    def __init__(self, sources, places, sems, first=0):
        self.copies = [
            pltpu.make_async_copy(source, place, sems.at[first + n])
            for n, (source, place) in enumerate(zip(sources, places))
        ]

    def start(self):
        for copy in self.copies:
            copy.start()

    def wait(self):
        for copy in self.copies:
            copy.wait()


def embed_kernel(size, patches, embed, keep_rows, gain, *refs):
    weights_in, ws = refs[0:7], refs[7]
    resid_out, full_out, proj_out, step_out = refs[8:12]
    wz, wx, wb, wc, wq, wk, wv = weights = refs[12:19]
    fetch = Fetch(weights_in, weights, refs[19])
    line = Line(refs[20:], size)
    steps, sub = line.steps, line.own.shape[2]
    columns = []
    for ref in (wz, wx, wb, wc, wq, wk, wv):
        columns.append((ref, sum(c[0].shape[1] for c in columns)))

    def produce(j):
        line.own[:, j] = mm(flat(patches[:, j]), embed[...]).reshape(size, sub, line.own.shape[3])

    def finish(j, total):
        rows = total * keep_rows[j]
        resid_out[j] = rows
        return normed(rows, gain[...]).astype(bf16)

    def consume(j):
        x = line.full[:, j]
        full_out[:, j] = x
        x = flat(x)
        for ref, start in columns:
            width = ref.shape[1]
            proj_out[:, j, :, start : start + width] = (
                mm(x, ref[...]).astype(bf16).reshape(size, sub, width)
            )
        step_out[:, j] = mm(x, ws[...], NT).reshape(size, sub, ws.shape[0])

    fetch.start()
    line.enter()
    produce(0)

    def iteration(i, _):
        line.move(i, finish)

        @pl.when(i + 1 < steps)
        def _():
            produce(i + 1)

        ready = line.ready_step(i)

        @pl.when(ready == 0)
        def _():
            fetch.wait()

        @pl.when(line.inside(ready))
        def _():
            consume(ready)

        return 0

    lax.fori_loop(0, steps + line.lag(), iteration, 0)
    line.leave()


def ffn_kernel(size, mix, wmo, wao, resid_one, gain, wg_in, wu_in, wd_in, og_in, og_mine,
               resid_grad, ffn_out, resid_out, dmix, grads_out, gain_grad, hidden_all, gg_all, ug_all,
               wg, wu, wd, og_full, grads, load, *scratch):
    fetch = Fetch((wg_in, wu_in, wd_in, og_in), (wg, wu, wd, og_full), load)
    half = len(scratch) // 2
    one, two = Line(scratch[:half], size), Line(scratch[half:], size)
    steps, sub, width = one.steps, one.own.shape[2], one.own.shape[3]
    length = size * steps * sub
    inner, mixed, units = wmo.shape[0], mix.shape[3], wg.shape[1]
    group = 256
    groups = width // group

    def shaped(v):
        return v.reshape(size, sub, v.shape[1])

    def all_rows(v):
        return v.reshape(length, v.shape[3])

    def produce(j):
        x = flat(mix[:, j])
        one.own[:, j] = shaped(mm(x[:, 0:inner], wmo[...]) + mm(x[:, inner:], wao[...]))

    def finish_one(j, total):
        rows = resid_one[j] + total
        resid_out[j] = rows
        return normed(rows, gain[...]).astype(bf16)

    def middle(j):
        x = flat(one.full[:, j])
        og = flat(og_full[:, j])
        gate, up = mm(x, wg[...]), mm(x, wu[...])
        hg = mm(og, wd[...], NT)
        sig = jax.nn.sigmoid(gate)
        act = gate * sig
        hidden = (act * up).astype(bf16)
        gg = (hg * up * (sig * (1.0 + gate * (1.0 - sig)))).astype(bf16)
        ug = (hg * act).astype(bf16)
        hidden_all[:, j] = shaped(hidden)
        gg_all[:, j] = shaped(gg)
        ug_all[:, j] = shaped(ug)
        two.own[:, j] = shaped(mm(gg, wg[...], NT) + mm(ug, wu[...], NT))
        ffn_out[:, j] = shaped(mm(hidden, wd[...]).astype(bf16))

    def finish_two(j, total):
        back, part = normed_back(total, resid_out[j], gain[...])
        rows = og_mine[j].astype(f32) + back
        resid_grad[j] = rows
        gain_grad[...] = gain_grad[...] + part
        return rows.astype(bf16)

    def consume(j):
        x = flat(two.full[:, j])
        dmix[:, j, :, 0:inner] = shaped(mm(x, wmo[...], NT).astype(bf16))
        dmix[:, j, :, inner:] = shaped(mm(x, wao[...], NT).astype(bf16))

    def columns(ref, g):
        return all_rows(ref[:, :, :, pl.ds(pl.multiple_of(g * group, group), group)])

    def ffn_grads(g):
        here = pl.ds(pl.multiple_of(g * group, group), group)
        x = columns(one.full, g)
        grads[here, 0:units] = mm(x, all_rows(gg_all[...]), TN).astype(bf16)
        grads[here, units : 2 * units] = mm(x, all_rows(ug_all[...]), TN).astype(bf16)
        total = mm(columns(og_full, g), all_rows(hidden_all[...]), TN)
        grads[here, 2 * units : 3 * units] = total.astype(bf16)
        give(g).start()

    def give(g):
        here = pl.ds(pl.multiple_of(g * group, group), group)
        return pltpu.make_async_copy(
            grads.at[here, 0 : 3 * units], grads_out.at[here, 0 : 3 * units], load.at[4 + g]
        )

    def given(g, _):
        give(g).wait()
        return 0

    def mix_grads(g, _):
        here = pl.ds(pl.multiple_of(g * group, group), group)
        grads[here, 3 * units :] = mm(
            columns(two.full, g), all_rows(mix[...]), TN
        ).astype(bf16)
        return 0

    fetch.start()
    one.enter()
    gain_grad[...] = jnp.zeros_like(gain_grad)
    produce(0)
    lag = one.lag() + 1

    def iteration(i, _):
        one.move(i, finish_one)
        two.move(i - lag, finish_two)

        @pl.when(i + 1 < steps)
        def _():
            produce(i + 1)

        ready_one = one.ready_step(i)

        @pl.when(ready_one == 0)
        def _():
            fetch.wait()

        @pl.when(one.inside(ready_one))
        def _():
            middle(ready_one)

        ready_two = two.ready_step(i - lag)

        @pl.when(two.inside(ready_two))
        def _():
            consume(ready_two)

        turn = i - (steps + lag)

        @pl.when(jnp.logical_and(turn >= 0, turn < groups))
        def _():
            ffn_grads(turn)

        return 0

    lax.fori_loop(0, steps + lag + two.lag(), iteration, 0)
    lax.fori_loop(0, groups, mix_grads, 0)
    last = pltpu.make_async_copy(
        grads.at[:, 3 * units :], grads_out.at[:, 3 * units :], load.at[4 + groups]
    )
    last.start()
    lax.fori_loop(0, groups, given, 0)
    last.wait()
    one.leave()
    two.leave()


def comm_call(body, out_shape, scratch, identity, *args, kept=(), given=()):
    return pl.pallas_call(
        body,
        out_shape=out_shape,
        in_specs=[
            pl.BlockSpec(memory_space=pl.ANY if place in kept else pltpu.VMEM)
            for place in range(len(args))
        ],
        out_specs=tuple(
            pl.BlockSpec(memory_space=pl.ANY if place in given else pltpu.VMEM)
            for place in range(len(out_shape))
        ),
        scratch_shapes=scratch,
        compiler_params=pltpu.CompilerParams(
            collective_id=identity, has_side_effects=True, vmem_limit_bytes=62 * 2**20
        ),
    )(*args)


def sds(shape, kind):
    return jax.ShapeDtypeStruct(shape, kind)


class Halving:
    def __init__(self, data, got, ss, sr):
        self.data, self.got, self.ss, self.sr = data, got, ss, sr
        self.count, self.rows = data.shape[0], data.shape[1]
        self.bits = self.count.bit_length() - 1
        self.me = lax.axis_index("dp")
        plain = list(range(self.bits))
        other = plain if self.bits < 3 else [0, 2, 1] + plain[3:]
        self.orders = (plain, other)

    @staticmethod
    def scratch(count, rows, columns):
        spare = max(count - 1, 1)
        return [
            pltpu.VMEM((count, rows, columns), bf16),
            pltpu.VMEM((spare, rows, columns), bf16),
            pltpu.SemaphoreType.DMA((2, spare)),
            pltpu.SemaphoreType.DMA((2, spare)),
        ]

    def bit(self, b):
        return lax.rem(self.me // 2**b, 2)

    def block(self, half, stage, e, theirs):
        order = self.orders[half]
        place = 0
        for b in order[:stage]:
            place = place + self.bit(b) * 2**b
        b = order[stage]
        place = place + (1 - self.bit(b) if theirs else self.bit(b)) * 2**b
        for t, b in enumerate(sorted(order[stage + 1 :])):
            place = place + lax.rem(e // 2**t, 2) * 2**b
        return place

    def open(self, stage):
        return 2 ** (self.bits - 1 - stage)

    def slot(self, stage, e):
        return sum(self.open(s) for s in range(stage)) + e

    def part(self, half):
        rows = self.rows // 2
        return pl.ds(half * rows, rows)

    def copy(self, half, stage, e):
        b = self.orders[half][stage]
        slot = self.slot(stage, e)
        return pltpu.make_async_remote_copy(
            src_ref=self.data.at[self.block(half, stage, e, True), self.part(half)],
            dst_ref=self.got.at[slot, self.part(half)],
            send_sem=self.ss.at[half, slot],
            recv_sem=self.sr.at[half, slot],
            device_id={"dp": self.me + (1 - 2 * self.bit(b)) * 2**b},
            device_id_type=MESH,
        )

    def start(self, stage, low=0, high=None):
        def one(e, _):
            self.copy(0, stage, e).start()
            self.copy(1, stage, e).start()
            return 0

        lax.fori_loop(low, self.open(stage) if high is None else high, one, 0)

    def take(self, half, stage, e):
        self.copy(half, stage, e).wait_recv()
        place, part = self.block(half, stage, e, False), self.part(half)
        got = self.got[self.slot(stage, e), part]
        self.data[place, part] = self.data[place, part] + got

    def finish(self, stage):
        def one(e, _):
            for half in range(2):
                self.copy(half, stage, e).wait_recv()
                place, part = self.block(half, stage, e, False), self.part(half)
                got = self.got[self.slot(stage, e), part]
                self.data[place, part] = self.data[place, part] + got
            return 0

        lax.fori_loop(0, self.open(stage), one, 0)

    def leave(self):
        for stage in range(self.bits):

            def one(e, _, stage=stage):
                self.copy(0, stage, e).wait_send()
                self.copy(1, stage, e).wait_send()
                return 0

            lax.fori_loop(0, self.open(stage), one, 0)


class Doubling:
    def __init__(self, parts, got, ss, sr, dp, tp):
        self.parts, self.got, self.ss, self.sr = parts, got, ss, sr
        self.hops = [("dp", b) for b in range(dp.bit_length() - 1)]
        self.hops += [("tp", b) for b in range(tp.bit_length() - 1)]

    @staticmethod
    def scratch(dp, tp, rows, columns):
        hops = dp.bit_length() + tp.bit_length() - 2
        return [
            pltpu.VMEM((hops + 1, rows, columns), f32),
            pltpu.VMEM((hops, rows, columns), f32),
            pltpu.SemaphoreType.DMA((hops,)),
            pltpu.SemaphoreType.DMA((hops,)),
        ]

    def copy(self, hop):
        axis, b = self.hops[hop]
        me = lax.axis_index(axis)
        flip = (1 - 2 * lax.rem(me // 2**b, 2)) * 2**b
        return pltpu.make_async_remote_copy(
            src_ref=self.parts.at[hop],
            dst_ref=self.got.at[hop],
            send_sem=self.ss.at[hop],
            recv_sem=self.sr.at[hop],
            device_id={axis: me + flip},
            device_id_type=MESH,
        )

    def start(self, hop):
        self.copy(hop).start()

    def finish(self, hop):
        self.copy(hop).wait_recv()
        self.parts[hop + 1] = self.parts[hop] + self.got[hop]

    def leave(self):
        for hop in range(len(self.hops)):
            self.copy(hop).wait_send()


def enter_both(dp, tp):
    barrier = pltpu.get_barrier_semaphore()
    me_t, me_d = lax.axis_index("tp"), lax.axis_index("dp")
    for away in range(1, tp):
        pl.semaphore_signal(
            barrier, inc=1, device_id={"tp": lax.rem(me_t + away, tp)}, device_id_type=MESH
        )
    bits = dp.bit_length() - 1
    for b in range(bits):
        flip = (1 - 2 * lax.rem(me_d // 2**b, 2)) * 2**b
        pl.semaphore_signal(barrier, inc=1, device_id={"dp": me_d + flip}, device_id_type=MESH)
    pl.semaphore_wait(barrier, tp - 1 + bits)


def entry_kernel(size, dp, dproj, dstep, wz, wx, wb, wc, wq, wk, wv, ws, resid_one, gain, resid_grad,
                 keep_rows, embed_in, full_in, patches_in, dtaps, dheads, dgain, dskip, two_gain_grad,
                 patch_out, embed_out, in_out, small_out, full_one, embed, patches, patch_grad, load,
                 *scratch):
    fetch = Fetch((full_in, embed_in, patches_in), (full_one, embed, patches), load)
    line = Line(scratch[0:9], size)
    ins = Halving(*scratch[9:13])
    emb = Halving(*scratch[13:17])
    small = Doubling(*scratch[17:21], dp, size)
    steps, sub, width = line.steps, line.own.shape[2], line.own.shape[3]
    length = size * steps * sub
    weights = (wz, wx, wb, wc, wq, wk, wv)
    columns = []
    for ref in weights:
        columns.append((ref, sum(c[0].shape[1] for c in columns)))
    group = 256
    groups = width // group
    in_group = group // ins.rows

    def all_rows(v):
        return v.reshape(length, v.shape[3])

    def produce(j):
        total = mm(flat(dstep[:, j]), ws[...])
        for ref, start in columns:
            total = total + mm(flat(dproj[:, j, :, start : start + ref.shape[1]]), ref[...], NT)
        line.own[:, j] = total.reshape(size, sub, width)

    def finish(j, total):
        back, part = normed_back(total, resid_one[j], gain[...])
        small.parts[0, 9:10] = small.parts[0, 9:10] + part
        return ((resid_grad[j] + back) * keep_rows[j]).astype(bf16)

    def consume(d, _):
        x = flat(line.full[d])
        patch_grad[d] = mm(x, embed[...], NT).astype(bf16).reshape(steps, sub, embed.shape[0])
        give(d).start()
        return 0

    def give(d):
        return pltpu.make_async_copy(patch_grad.at[d], patch_out.at[d], load.at[3 + d])

    def given(d, _):
        give(d).wait()
        return 0

    def weight_group(g):
        x = full_one[:, pl.ds(pl.multiple_of(g * group, group), group)]
        here = pl.ds(g * in_group, in_group)
        grad = mm(x, all_rows(dproj[...]), TN).astype(bf16)
        ins.data[here, :, 0:PROJ] = grad.reshape(in_group, ins.rows, PROJ)
        grad = mm(x, all_rows(dstep[...]), TN).astype(bf16)
        grad = jnp.concatenate([grad, jnp.zeros((group, 120), bf16)], axis=1)
        ins.data[here, :, PROJ:] = grad.reshape(in_group, ins.rows, 128)
        if ins.bits:
            ins.start(0, g * in_group // 2, (g + 1) * in_group // 2)

    def embed_group(g):
        x = all_rows(line.full[:, :, :, pl.ds(pl.multiple_of(g * group, group), group)])
        grad = mm(x, all_rows(patches[...]), TN).astype(bf16)
        emb.data[pl.ds(g * in_group, in_group)] = grad.reshape(
            in_group, emb.rows, grad.shape[1]
        )
        if emb.bits:
            emb.start(0, g * in_group // 2, (g + 1) * in_group // 2)

    fetch.start()
    enter_both(dp, size)
    first = jnp.zeros((16, width), f32)
    small.parts[0] = first
    small.parts[0, 0:4, 0:768] = dtaps[...]
    small.parts[0, 4:5, 0:512] = dgain[...]
    small.parts[0, 5:6, 0:512] = dskip[...]
    small.parts[0, 6:8, 0:8] = dheads[...]
    small.parts[0, 8:9] = two_gain_grad[...]
    produce(0)
    fetch.copies[0].wait()

    def iteration(i, _):
        line.move(i, finish)

        @pl.when(i + 1 < steps)
        def _():
            produce(i + 1)

        @pl.when(i < groups)
        def _():
            weight_group(i)

        for stage in range(ins.bits):

            @pl.when(i == groups + (8 * stage) // max(ins.bits - 1, 1))
            def _(stage=stage):
                ins.finish(stage)
                if stage + 1 < ins.bits:
                    ins.start(stage + 1)

        return 0

    lax.fori_loop(0, steps + line.lag(), iteration, 0)
    small.start(0)
    fetch.copies[1].wait()
    fetch.copies[2].wait()

    in_out[...] = ins.data[ins.me]
    hops = len(small.hops)

    def small_turn(turn):
        if turn < hops:
            small.finish(turn)
            if turn + 1 < hops:
                small.start(turn + 1)

    if emb.bits == 3:
        mid, top = emb.bit(1), emb.bit(2)
        far_mid, far_top = 1 - mid, 1 - top

        def each_turn(t, _):
            g_mid = mid + (1 - t // 2) * (far_mid - mid)
            g_top = top + (1 - lax.rem(t, 2)) * (far_top - top)
            embed_group(g_mid + 2 * g_top)

            @pl.when(t == 1)
            def _():
                for half in range(2):
                    emb.take(half, 0, far_mid + 2 * far_top)
                emb.copy(0, 1, far_top).start()
                emb.copy(1, 1, far_mid).start()

            @pl.when(t == 2)
            def _():
                for half in range(2):
                    emb.take(half, 0, far_mid + 2 * top)
                emb.copy(0, 1, top).start()

            @pl.when(t == 3)
            def _():
                for half in range(2):
                    emb.take(half, 0, mid + 2 * far_top)
                emb.copy(1, 1, mid).start()

            return 0

        lax.fori_loop(0, groups, each_turn, 0)
        small_turn(0)
        for half in range(2):
            emb.take(half, 0, mid + 2 * top)
        lax.fori_loop(0, size // 2, consume, 0)
        small_turn(1)
        emb.take(0, 1, far_top)
        emb.copy(0, 2, 0).start()
        emb.take(1, 1, far_mid)
        emb.copy(1, 2, 0).start()
        lax.fori_loop(size // 2, size, consume, 0)
        small_turn(2)
        emb.take(0, 1, top)
        emb.take(1, 1, mid)
        small_turn(3)
        emb.take(0, 2, 0)
        emb.take(1, 2, 0)
        for turn in range(4, hops):
            small_turn(turn)
    else:

        def each_group(g, _):
            embed_group(g)
            return 0

        lax.fori_loop(0, groups, each_group, 0)
        lax.fori_loop(0, size, consume, 0)
        for turn in range(max(hops, emb.bits)):
            small_turn(turn)
            if turn < emb.bits:
                emb.finish(turn)
                if turn + 1 < emb.bits:
                    emb.start(turn + 1)
    small_out[0:8] = small.parts[dp.bit_length() - 1, 0:8]
    small_out[8:16] = small.parts[hops, 8:16]
    embed_out[...] = emb.data[emb.me]
    lax.fori_loop(0, size, given, 0)
    line.leave()
    ins.leave()
    emb.leave()
    small.leave()


def last_kernel(patch_in, embed_in, ins, mids, small, resid, ffn, place, patch_out, result,
                embed_out, gz, gx, gb, gc, gq, gk, gv, gs, t0, t1, t2, hb, hr, hs, inner_gain,
                gmo, gao, ggate, gup, gdown, gain_one, gain_two, held, sem):
    rows = patch_in.shape[0] // 4
    pieces = [pl.ds(n * rows, rows) for n in range(4)]
    takes = [pltpu.make_async_copy(patch_in.at[p], held.at[p], sem.at[n]) for n, p in enumerate(pieces)]
    gives = [pltpu.make_async_copy(held.at[p], patch_out.at[p], sem.at[4 + n]) for n, p in enumerate(pieces)]
    for take in takes:
        take.start()
    result[...] = (resid[...] + ffn[...].astype(f32)).astype(bf16)
    start = 0
    for out in (gz, gx, gb, gc, gq, gk, gv):
        out[...] = ins[:, start : start + out.shape[1]].astype(f32)
        start = start + out.shape[1]
    steps_part = ins[:, start:].astype(f32)
    gs[...] = steps_part.T[0 : gs.shape[0], :] if gs.shape[1] % 128 == 0 else steps_part[:, 0 : gs.shape[1]]
    units, inner = ggate.shape[1], t0.shape[1]
    ggate[...] = mids[:, 0:units].astype(f32)
    gup[...] = mids[:, units : 2 * units].astype(f32)
    for take, give in zip(takes, gives):
        take.wait()
        give.start()
    flipped = mids[:, 2 * units :].astype(f32)
    outs = ((gdown, flipped[:, 0:units]), (gmo, flipped[:, units : units + inner]),
            (gao, flipped[:, units + inner :]), (embed_out, embed_in[...].astype(f32)))
    for out, value in outs:
        out[...] = value.T if out.shape != value.shape else value
    t0[...] = small[0:4, 0 : t0.shape[1]]
    t1[...] = small[0:4, t0.shape[1] : t0.shape[1] + t1.shape[1]]
    t2[...] = small[0:4, t0.shape[1] + t1.shape[1] : t0.shape[1] + 2 * t1.shape[1]]
    hb[...] = small[6:7, 0 : hb.shape[1]]
    hr[...] = small[7:8, 0 : hr.shape[1]]
    hs[...] = small[5:6, 0 : hs.shape[1]]
    inner_gain[...] = small[4:5, 0 : inner_gain.shape[1]]
    width, share = small.shape[1], gain_one.shape[1]
    chosen = (iota((width, share), 0) == iota((width, share), 1) + place[0] * share).astype(bf16)
    gains = sum(mm(term, chosen) for term in parts_of(small[8:16, :], 3))
    gain_two[...] = gains[0:1, :]
    gain_one[...] = gains[1:2, :]
    for give in gives:
        give.wait()


def shards(
    patches,
    keep_mask,
    segments,
    embed_weight,
    first_gain,
    mamba_gate,
    mamba_input,
    state_in,
    state_out,
    step_weight,
    conv_input,
    conv_statein,
    conv_stateout,
    step_bias,
    rate_log,
    skip_gain,
    inner_gain,
    mamba_output,
    query_weight,
    key_weight,
    value_weight,
    attn_output,
    second_gain,
    ffn_gate,
    ffn_up,
    ffn_down,
    out_grad,
):
    size = lax.axis_size("tp")
    segment = segments[0]
    length = patches.shape[0]
    mine = length // size
    sub = mine // STEPS
    shape = (size, STEPS, sub)
    width = embed_weight.shape[1]
    keep_rows = keep_mask.astype(f32).reshape(STEPS, sub, 1)
    seg_row = segment.astype(f32)[None]
    taps = (conv_input, conv_statein, conv_stateout)
    core_params = (step_bias[None], rate_log[None], skip_gain[None], inner_gain[None])
    in_list = (
        mamba_gate,
        mamba_input,
        state_in,
        state_out,
        query_weight,
        key_weight,
        value_weight,
        step_weight.T,
    )
    one_gain, two_gain = first_gain[None], second_gain[None]
    buffers = Line.scratch(size, STEPS, sub, width)
    resid_one, full_one, projected, step_raw = comm_call(
        functools.partial(embed_kernel, size),
        (
            sds((STEPS, sub, width), f32),
            sds((*shape, width), bf16),
            sds((*shape, PROJ), bf16),
            sds((*shape, step_weight.shape[1]), f32),
        ),
        [pltpu.VMEM(member.shape, bf16) for member in in_list[:7]]
        + [pltpu.SemaphoreType.DMA((7,))]
        + buffers,
        1,
        patches.reshape(*shape, patches.shape[1]),
        embed_weight,
        keep_rows,
        one_gain,
        *in_list,
        kept=(4, 5, 6, 7, 8, 9, 10),
    )
    projected = projected.reshape(length, PROJ)
    step_raw = step_raw.reshape(length, step_weight.shape[1])
    own_grad = out_grad.reshape(STEPS, sub, width)
    mix_in, ssd, states, lse, og_full = mixer_fwd(
        size, projected, step_raw, seg_row, taps, *core_params, own_grad
    )
    inner_width = mamba_output.shape[0]
    hidden_width = ffn_gate.shape[1]
    rows16 = sds((*shape, width), bf16)
    rows32 = sds((STEPS, sub, width), f32)
    mixed = mix_in.shape[1]
    resid_grad, ffn_part, resid_two, dmix, grads, second_gain_grad = comm_call(
        functools.partial(ffn_kernel, size),
        (
            rows32, rows16, rows32, sds((*shape, mixed), bf16),
            sds((width, 3 * hidden_width + mixed), bf16), sds((1, width), f32),
        ),
        [pltpu.VMEM((*shape, hidden_width), bf16)] * 3
        + [
            pltpu.VMEM(ffn_gate.shape, bf16),
            pltpu.VMEM(ffn_up.shape, bf16),
            pltpu.VMEM(ffn_down.shape, bf16),
            pltpu.VMEM((*shape, width), bf16),
            pltpu.VMEM((width, 3 * hidden_width + mixed), bf16),
            pltpu.SemaphoreType.DMA((5 + width // 256,)),
        ]
        + buffers
        + buffers,
        2,
        mix_in.reshape(*shape, mixed),
        mamba_output,
        attn_output,
        resid_one,
        two_gain,
        ffn_gate,
        ffn_up,
        ffn_down,
        og_full,
        own_grad,
        kept=(5, 6, 7, 8),
        given=(4,),
    )
    ffn_sum = lax.psum_scatter(
        ffn_part.reshape(length, width), "tp", scatter_dimension=0, tiled=True
    )
    blocks = lax.axis_size("dp")
    grads = grads.reshape(blocks, width // blocks, grads.shape[1])
    proj_grad, step_grad, dtaps, dheads, dgain, dskip, mid_sum = mixer_bwd(
        size, projected, step_raw, seg_row, taps, *core_params, mix_in, ssd, states, lse,
        dmix.reshape(length, mixed),
        grads,
    )
    dp = lax.axis_size("dp")
    block = width // dp
    features = patches.shape[1]
    patches_grad, embed_sum, in_sum, small = comm_call(
        functools.partial(entry_kernel, size, dp),
        (
            sds((*shape, features), bf16),
            sds((block, features), bf16),
            sds((block, PROJ + 128), bf16),
            sds((16, width), f32),
        ),
        [
            pltpu.VMEM((length, width), bf16),
            pltpu.VMEM(embed_weight.shape, bf16),
            pltpu.VMEM((*shape, features), bf16),
            pltpu.VMEM((*shape, features), bf16),
            pltpu.SemaphoreType.DMA((3 + size,)),
        ]
        + buffers
        + Halving.scratch(dp, block, PROJ + 128)
        + Halving.scratch(dp, block, features)
        + Doubling.scratch(dp, size, 16, width),
        3,
        proj_grad.reshape(*shape, PROJ),
        step_grad.reshape(*shape, step_grad.shape[1]),
        *in_list,
        resid_one,
        one_gain,
        resid_grad,
        keep_rows,
        embed_weight,
        full_one.reshape(length, width),
        patches.reshape(*shape, features),
        dtaps,
        dheads,
        dgain,
        dskip,
        second_gain_grad,
        kept=(14, 15, 16),
        given=(0,),
    )
    place = (lax.axis_index("dp") * size + lax.axis_index("tp"))[None]
    flip = block % 128 == 0

    def turned(rows):
        return sds((rows, block) if flip else (block, rows), f32)

    outs = pl.pallas_call(
        last_kernel,
        out_shape=(
            sds((length, features), bf16),
            sds((mine, width), bf16),
            turned(features),
            *[sds((block, member.shape[1]), f32) for member in in_list[:7]],
            turned(step_weight.shape[1]),
            *[sds(member.shape, f32) for member in taps],
            *[sds((1, step_bias.shape[0]), f32)] * 3,
            sds((1, inner_width), f32),
            turned(inner_width),
            turned(attn_output.shape[0]),
            sds((block, hidden_width), f32),
            sds((block, hidden_width), f32),
            turned(hidden_width),
            sds((1, block // size), f32),
            sds((1, block // size), f32),
        ),
        in_specs=[pl.BlockSpec(memory_space=pl.ANY)]
        + [pl.BlockSpec(memory_space=pltpu.VMEM)] * 6
        + [pl.BlockSpec(memory_space=pltpu.SMEM)],
        out_specs=(
            pl.BlockSpec(memory_space=pl.ANY),
            *[pl.BlockSpec(memory_space=pltpu.VMEM)] * 24,
        ),
        scratch_shapes=[pltpu.VMEM((length, features), bf16), pltpu.SemaphoreType.DMA((8,))],
        compiler_params=pltpu.CompilerParams(vmem_limit_bytes=60 * 2**20),
    )(
        patches_grad.reshape(length, features),
        embed_sum,
        in_sum,
        mid_sum,
        small,
        resid_two.reshape(mine, width),
        ffn_sum,
        place,
    )
    (
        patches_grad, result, embed_cols, gz, gx, gb, gc, gq, gk, gv, gs, t0, t1, t2, hb, hr, hs,
        inner_grad, gmo, gao, ggate, gup, gdown, gain_one, gain_two,
    ) = outs
    if flip:
        gs = gs.T
    else:
        embed_cols, gmo, gao, gdown = embed_cols.T, gmo.T, gao.T, gdown.T
    return (
        result,
        patches_grad,
        embed_cols,
        gain_one[0],
        gz,
        gx,
        gb,
        gc,
        gs,
        t0,
        t1,
        t2,
        hb[0],
        hr[0],
        hs[0],
        inner_grad[0],
        gmo,
        gq,
        gk,
        gv,
        gao,
        gain_two[0],
        ggate,
        gup,
        gdown,
    )


def solution(mesh):
    return jax.shard_map(
        shards,
        mesh=mesh,
        in_specs=(
            P("dp", "tp"),
            P(("dp", "tp")),
            P("dp", None),
            P("tp", None),
            P(),
            P(None, "tp"),
            P(None, "tp"),
            P(None, "tp"),
            P(None, "tp"),
            P(None, "tp"),
            P(None, "tp"),
            P(None, "tp"),
            P(None, "tp"),
            P("tp"),
            P("tp"),
            P("tp"),
            P("tp"),
            P("tp", None),
            P(None, "tp"),
            P(None, "tp"),
            P(None, "tp"),
            P("tp", None),
            P(),
            P(None, "tp"),
            P(None, "tp"),
            P("tp", None),
            P(("dp", "tp"), None),
        ),
        out_specs=(
            P(("dp", "tp"), None),
            P("dp", "tp"),
            P("tp", "dp"),
            P(("dp", "tp")),
            P("dp", "tp"),
            P("dp", "tp"),
            P("dp", "tp"),
            P("dp", "tp"),
            P("dp", "tp"),
            P(None, "tp"),
            P(None, "tp"),
            P(None, "tp"),
            P("tp"),
            P("tp"),
            P("tp"),
            P("tp"),
            P("tp", "dp"),
            P("dp", "tp"),
            P("dp", "tp"),
            P("dp", "tp"),
            P("tp", "dp"),
            P(("dp", "tp")),
            P("dp", "tp"),
            P("dp", "tp"),
            P("tp", "dp"),
        ),
        check_vma=False,
    )
```

```python
import functools

import jax
import jax.numpy as jnp
from jax import lax
from jax.experimental import pallas as pl
from jax.experimental.pallas import tpu as pltpu
from jax.sharding import PartitionSpec as P

f32 = jnp.float32
bf16 = jnp.bfloat16
eps = 1e-05
NST = 128
LOG2E = 1.4426950408889634
LOW = -1e30
NN = ((1,), (0,))
NT = ((1,), (1,))
TN = ((0,), (0,))
PROJ = 2048
STEPS = 8


def mm(a, b, dims=NN):
    return lax.dot_general(a, b, (dims, ((), ())), preferred_element_type=f32)


def parts_of(v, count):
    terms = []
    for _ in range(count):
        term = v.astype(bf16)
        terms.append(term)
        v = v - term.astype(f32)
    return terms


def pick(chosen, v, dims=NN, count=3):
    total = None
    for term in parts_of(v, count):
        product = mm(chosen, term, dims)
        total = product if total is None else total + product
    return total


def iota(shape, axis):
    return lax.broadcasted_iota(jnp.int32, shape, axis)


def expand(v):
    low_half = iota((1, 128), 1) < 64
    return jnp.concatenate(
        [
            jnp.where(low_half, v[:, h : h + 1], v[:, h + 1 : h + 2])
            for h in range(0, v.shape[1], 2)
        ],
        axis=1,
    )


def head_sum(v):
    owner = (iota((512, 8), 0) // 64 == iota((512, 8), 1)).astype(bf16)
    high, low = parts_of(v, 2)
    return mm(high, owner) + mm(low, owner)


def softplus(v):
    return jnp.maximum(v, 0.0) + jnp.log1p(jnp.exp(-jnp.abs(v)))


def tile4(v):
    return jnp.concatenate([v, v, v, v], axis=1)


def fill_segments(seg_ref, segcol):
    length = seg_ref.shape[1]
    segcol[0:8, :] = jnp.full((8, 128), -1.0, f32)
    segcol[length + 8 : length + 16, :] = jnp.full((8, 128), -2.0, f32)
    for row in range(0, length, 128):
        piece = jnp.broadcast_to(seg_ref[0:1, row : row + 128], (128, 128))
        segcol[8 + row : 8 + row + 128, :] = piece.T


def taps_of(taps, tile):
    if tile < 4:
        return taps[0][:, tile * 128 : tile * 128 + 128]
    return taps[tile - 3][...]


def conv_masks(rows, segx):
    here = segx[8 : 8 + rows, :]
    return [(segx[8 - lag : 8 - lag + rows, :] == here).astype(f32) for lag in (1, 2, 3)]


def conv_pre(tile, rows, uext, masks, taps):
    lanes = slice(tile * 128, tile * 128 + 128)
    w = taps_of(taps, tile)
    pre = uext[8 : 8 + rows, lanes] * w[0:1, :]
    for lag in (1, 2, 3):
        shifted = uext[8 - lag : 8 - lag + rows, lanes] * masks[lag - 1]
        pre = pre + shifted * w[lag : lag + 1, :]
    return pre


def load_inputs(first, rows, proj, segcol, uext, segx):
    @pl.when(first == 0)
    def _():
        uext[0:8, :] = jnp.zeros((8, 768), f32)

    @pl.when(first > 0)
    def _():
        uext[0:8, :] = proj[pl.ds(pl.multiple_of(first - 16, 16), 16), 512:1280].astype(f32)[8:16]

    uext[8 : 8 + rows, :] = proj[pl.ds(first, rows), 512:1280].astype(f32)
    segx[...] = segcol[pl.ds(first, rows + 16), :]


def decays(first, rows, step, bias, rate):
    raw = step[pl.ds(first, rows), :] + bias[...]
    size = softplus(raw)
    logs = size * -jnp.exp(rate[...])
    scaled = logs * LOG2E
    lower = (iota((rows, rows), 0) >= iota((rows, rows), 1)).astype(bf16)
    cum = pick(lower, scaled)
    wide = jnp.concatenate([cum, jnp.zeros((rows, 120), f32)], axis=1)
    return raw, size, logs, cum, wide.T[0:8, :]


def half_masks():
    low_half = iota((1, 128), 1) < 64
    return low_half, jnp.logical_not(low_half)


def keep(mask, v):
    return jnp.where(mask, v, jnp.zeros_like(v))


def mixer_fwd_chunk(
    index, rows, proj, step, seg, segcol, taps, bias, rate, skip, gain, uext, segx, state,
    oacc, stats, mix_out, ssd_out, states_out, lse_out, hook,
):
    first = pl.multiple_of(index * rows, rows)
    here = pl.ds(first, rows)
    halves = half_masks()
    load_inputs(first, rows, proj, segcol, uext, segx)
    masks = conv_masks(rows, segx)
    acts = []
    for tile in range(6):
        pre = conv_pre(tile, rows, uext, masks, taps)
        acts.append(pre * jax.nn.sigmoid(pre))
    xc = jnp.concatenate(acts[0:4], axis=1)
    bc, cc = acts[4].astype(bf16), acts[5].astype(bf16)
    _, size, _, cum, cumr = decays(first, rows, step, bias, rate)
    segc = segx[8 : 8 + rows, :]
    before = segx[7:8, :]
    goes_on = (segc == before).astype(f32)
    segr = seg[0:1, here]
    wide_seg = jnp.concatenate([segc] * (rows // 128), axis=1)
    allowed = (iota((rows, rows), 0) >= iota((rows, rows), 1)) & (wide_seg == segr)
    away = jnp.where(allowed, 0.0, LOW)
    hook(0)
    cb = mm(cc, bc, NT)
    xs = xc * expand(size)
    xsb = xs.astype(bf16)
    parts = []
    for pair in range(4):
        lhs = []
        for h in (2 * pair, 2 * pair + 1):
            gap = cum[:, h : h + 1] - cumr[h : h + 1, :] + away
            lhs.append((cb * jnp.exp2(gap)).astype(bf16))
        xp = xsb[:, pair * 128 : pair * 128 + 128]
        rhs = jnp.concatenate([keep(halves[0], xp), keep(halves[1], xp)], axis=0)
        parts.append(mm(jnp.concatenate(lhs, axis=1), rhs))
        if pair == 1:
            hook(1)
    ssd = jnp.concatenate(parts, axis=1) + xc * expand(skip[...])
    st = state[...]
    stb = st.astype(bf16)
    states_out[index] = stb
    ssd = ssd + mm(cc, stb) * expand(jnp.exp2(cum)) * tile4(goes_on)
    last = cum[rows - 1 : rows, :]
    fits = (segc == segc[rows - 1 : rows, :]).astype(f32)
    weight = expand(jnp.exp2(last - cum)) * tile4(fits)
    added = mm(bc, (xs * weight).astype(bf16), TN)
    passes = (segc[rows - 1 : rows, :] == before).astype(f32)
    state[...] = st * (expand(jnp.exp2(last)) * tile4(passes)) + added
    hook(2)
    ssd_out[here, :] = ssd.astype(bf16)
    z = proj[here, 0:512].astype(f32)
    g = ssd * (z * jax.nn.sigmoid(z))
    r = lax.rsqrt(jnp.mean(g * g, axis=1, keepdims=True) + eps)
    mix_out[here, 0:512] = (g * r * gain[...]).astype(bf16)
    hook(3)
    own_seg = seg[0:1, here]

    def keys(block, fresh):
        start = pl.multiple_of(block * rows, rows)
        away = attention_away(start, first, rows, own_seg, segcol)
        for pair in range(2):
            lanes = pair * 128
            q = proj[here, 1280 + lanes : 1408 + lanes] * jnp.asarray(0.125, bf16)
            k = proj[pl.ds(start, rows), 1536 + lanes : 1664 + lanes]
            v = proj[pl.ds(start, rows), 1792 + lanes : 1920 + lanes]
            for half in range(2):
                h = 2 * pair + half
                mine = slice(h * 64, h * 64 + 64)
                s = mm(k, keep(halves[half], q), NT) + away
                peak = jnp.max(s, axis=0, keepdims=True)
                if not fresh:
                    old = stats[h : h + 1, :]
                    peak = jnp.maximum(peak, old)
                    fade = jnp.exp(old - peak)
                p = jnp.exp(s - peak)
                total = jnp.sum(p, axis=0, keepdims=True)
                o = mm(v, p.astype(bf16), TN)[half * 64 : half * 64 + 64, :]
                if not fresh:
                    total = total + stats[h + 4 : h + 5, :] * fade
                    o = o + oacc[mine, :] * fade
                stats[h : h + 1, :] = peak
                stats[h + 4 : h + 5, :] = total
                oacc[mine, :] = o

    keys(index, True)

    def earlier(block, _):
        keys(block, False)
        return 0

    lax.fori_loop(0, index, earlier, 0)
    lse_out[0:4, here] = stats[0:4, :] + jnp.log(stats[4:8, :])
    for h in range(4):
        mine = slice(h * 64, h * 64 + 64)
        oacc[mine, :] = oacc[mine, :] * (1.0 / stats[h + 4 : h + 5, :])
    for pair in range(2):
        mine = slice(pair * 128, pair * 128 + 128)
        mix_out[here, 512 + pair * 128 : 640 + pair * 128] = oacc[mine, :].T.astype(bf16)


def attention_away(start, first, rows, own_seg, segcol):
    key_seg = segcol[pl.ds(start + 8, rows), :]
    wide = jnp.concatenate([key_seg] * (rows // 128), axis=1)
    allowed = (wide == own_seg) & (
        iota((rows, rows), 0) + start <= iota((rows, rows), 1) + first
    )
    return jnp.where(allowed, 0.0, LOW)


def mixer_bwd_chunk(
    index, rows, proj, step, seg, segcol, taps, bias, rate, skip, gain, uext, segx, slopes, dext,
    dstate, dkv, dqs, mix, ssd_in, states_in, lse_in, dmix, dproj, dstep, dtaps, dheads, dgain, dskip,
    begin,
):
    first = pl.multiple_of(index * rows, rows)
    here = pl.ds(first, rows)
    halves = half_masks()
    load_inputs(first, rows, proj, segcol, uext, segx)
    masks = conv_masks(rows, segx)
    acts = []
    for tile in range(6):
        pre = conv_pre(tile, rows, uext, masks, taps)
        sig = jax.nn.sigmoid(pre)
        acts.append(pre * sig)
        slopes[:, tile * 128 : tile * 128 + 128] = sig * (1.0 + pre * (1.0 - sig))
    xc = jnp.concatenate(acts[0:4], axis=1)
    bc, cc = acts[4].astype(bf16), acts[5].astype(bf16)
    begin()
    raw, size, logs, cum, cumr = decays(first, rows, step, bias, rate)
    z = proj[here, 0:512].astype(f32)
    ssd = ssd_in[here, :].astype(f32)
    dmo = dmix[here, 0:512].astype(f32)
    sig = jax.nn.sigmoid(z)
    act = z * sig
    g = ssd * act
    r = lax.rsqrt(jnp.mean(g * g, axis=1, keepdims=True) + eps)
    gain_part = jnp.sum(dmo * g * r, axis=0, keepdims=True)
    a = dmo * gain[...]
    dg = r * a - (r * r * r) * g * jnp.mean(a * g, axis=1, keepdims=True)
    dssd = dg * act
    dproj[here, 0:512] = (dg * ssd * (sig * (1.0 + z * (1.0 - sig)))).astype(bf16)
    skip_part = jnp.sum(dssd * xc, axis=0, keepdims=True)
    dxc = dssd * expand(skip[...])
    dyb = dssd.astype(bf16)
    wide_size = expand(size)
    xs = xc * wide_size
    xsb = xs.astype(bf16)
    segc = segx[8 : 8 + rows, :]
    before = segx[7:8, :]
    goes_on = (segc == before).astype(f32)
    segr = seg[0:1, here]
    wide_seg = jnp.concatenate([segc] * (rows // 128), axis=1)
    allowed = (iota((rows, rows), 0) <= iota((rows, rows), 1)) & (wide_seg == segr)
    away = jnp.where(allowed, 0.0, LOW)
    cbt = mm(bc, cc, NT)
    dcbt = jnp.zeros((rows, rows), f32)
    to_rows = []
    from_rows = jnp.zeros((rows, 8), f32)
    parts = []
    for pair in range(4):
        lanes = slice(pair * 128, pair * 128 + 128)
        lhs, rhs = [], []
        for half in range(2):
            h = 2 * pair + half
            lt = jnp.exp2(cumr[h : h + 1, :] - cum[:, h : h + 1] + away)
            mt = cbt * lt
            lhs.append(mt.astype(bf16))
            rhs.append(keep(halves[half], dyb[:, lanes]))
            dl = mm(keep(halves[half], xsb[:, lanes]), dyb[:, lanes], NT)
            dcbt = dcbt + dl * lt
            gt = dl * mt
            to_rows.append(jnp.sum(gt, axis=0, keepdims=True))
            from_rows = jnp.where(
                iota((1, 8), 1) == h, jnp.sum(gt, axis=1, keepdims=True), from_rows
            )
        parts.append(mm(jnp.concatenate(lhs, axis=1), jnp.concatenate(rhs, axis=0)))
    dxs = jnp.concatenate(parts, axis=1)
    dcb = dcbt.astype(bf16)
    db = mm(dcb, cc)
    dc = mm(dcb, bc, TN)
    upper = (iota((rows, rows), 0) <= iota((rows, rows), 1)).astype(bf16)
    late = -from_rows
    reach = expand(jnp.exp2(cum)) * tile4(goes_on)
    stb = states_in[index]
    dye = dssd * reach
    dyeb = dye.astype(bf16)
    dc = dc + mm(dyeb, stb, NT)
    late = late + head_sum(dye * mm(cc, stb))
    into_state = mm(cc, dyeb, TN)
    last = cum[rows - 1 : rows, :]
    fits = (segc == segc[rows - 1 : rows, :]).astype(f32)
    weight = expand(jnp.exp2(last - cum)) * tile4(fits)
    dst = dstate[...]
    dsb = dst.astype(bf16)
    dxi = mm(bc, dsb) * weight
    dxs = dxs + dxi
    db = db + mm((xs * weight).astype(bf16), dsb, NT)
    strict = (iota((rows, rows), 0) > iota((rows, rows), 1)).astype(bf16)
    dlog = pick(strict, head_sum(xs * dxi))
    passes = (segc[rows - 1 : rows, :] == before).astype(f32)
    fade = expand(jnp.exp2(last)) * tile4(passes)
    through = jnp.sum(stb.astype(f32) * dst, axis=0, keepdims=True) * fade
    dlog = dlog + head_sum(jnp.broadcast_to(through, (8, 512)))[0:1, :]
    dstate[...] = dst * fade + into_state
    dlog = dlog + pick(upper, late) + pick(upper, jnp.concatenate(to_rows, axis=0), NT)
    dsize = head_sum(dxs * xc) - dlog * jnp.exp(rate[...])
    rate_part = jnp.sum(dlog * logs, axis=0, keepdims=True)
    draw = dsize * jax.nn.sigmoid(raw)
    bias_part = jnp.sum(draw, axis=0, keepdims=True)
    dstep[here, :] = draw.astype(dstep.dtype)
    dxc = dxc + dxs * wide_size
    dacts = [dxc[:, t * 128 : t * 128 + 128] for t in range(4)] + [db, dc]
    dext[rows : rows + 8, :] = dext[0:8, :]
    ahead = [(segx[8 + lag : 8 + lag + rows, :] == segc).astype(f32) for lag in (1, 2, 3)]
    for tile in range(6):
        lanes = slice(tile * 128, tile * 128 + 128)
        w = taps_of(taps, tile)
        dpre = dacts[tile] * slopes[:, lanes]
        dext[0:rows, lanes] = dpre
        u = uext[8 : 8 + rows, lanes]
        du = dpre * w[0:1, :]
        sums = [jnp.sum(dpre * u, axis=0, keepdims=True)]
        for lag in (1, 2, 3):
            later = dext[lag : lag + rows, lanes] * ahead[lag - 1]
            du = du + later * w[lag : lag + 1, :]
            sums.append(jnp.sum(later * u, axis=0, keepdims=True))
        dproj[here, 512 + tile * 128 : 640 + tile * 128] = du.astype(bf16)
        sums = jnp.concatenate(sums, axis=0)
        dtaps[:, lanes] = dtaps[:, lanes] + sums
    head_parts = jnp.concatenate([bias_part, rate_part], axis=0)
    dheads[...] = dheads[...] + head_parts
    dgain[...] = dgain[...] + gain_part
    dskip[...] = dskip[...] + skip_part
    own_seg = seg[0:1, here]
    dos = [dmix[here, 512 + pair * 128 : 640 + pair * 128] for pair in range(2)]
    owner = (iota((8, 256), 1) // 64 == iota((8, 256), 0)).astype(bf16)
    delta = pick(
        owner,
        jnp.concatenate(dos, axis=1).astype(f32) * mix[here, 512:768].astype(f32),
        NT,
        2,
    )
    dqs[...] = jnp.zeros_like(dqs)

    def keys(block, _):
        start = pl.multiple_of(block * rows, rows)
        there = pl.ds(start, rows)
        away = attention_away(start, first, rows, own_seg, segcol)
        for pair in range(2):
            lanes = pair * 128
            q = proj[here, 1280 + lanes : 1408 + lanes] * jnp.asarray(0.125, bf16)
            k = proj[there, 1536 + lanes : 1664 + lanes]
            v = proj[there, 1792 + lanes : 1920 + lanes]
            ps, dss, qms, doms = [], [], [], []
            for half in range(2):
                h = 2 * pair + half
                mine = slice(h * 64, h * 64 + 64)
                qm, dom = keep(halves[half], q), keep(halves[half], dos[pair])
                p = jnp.exp(mm(k, qm, NT) + away - lse_in[h : h + 1, here])
                dp = mm(v, dom, NT)
                ds = (p * (dp - delta[h : h + 1, :])).astype(bf16)
                dqs[mine, :] = dqs[mine, :] + mm(k, ds, TN)[half * 64 : half * 64 + 64, :]
                ps.append(p.astype(bf16))
                dss.append(ds)
                qms.append(qm)
                doms.append(dom)
            kl, vl = slice(lanes, lanes + 128), slice(256 + lanes, 384 + lanes)
            dkv[there, kl] = dkv[there, kl] + mm(
                jnp.concatenate(dss, axis=1), jnp.concatenate(qms, axis=0)
            )
            dkv[there, vl] = dkv[there, vl] + mm(
                jnp.concatenate(ps, axis=1), jnp.concatenate(doms, axis=0)
            )
        return 0

    lax.fori_loop(0, index + 1, keys, 0)
    for pair in range(2):
        mine = slice(pair * 128, pair * 128 + 128)
        dproj[here, 1280 + pair * 128 : 1408 + pair * 128] = (dqs[mine, :] * 0.125).T.astype(bf16)
    dproj[here, 1536:2048] = dkv[here, :].astype(bf16)


def bwd_kernel(count, dp, proj, step, seg, t0, t1, t2, bias, rate, skip, gain, mix, ssd_in,
               states_in, lse_in, dmix, grads_in, dproj, dstep, dtaps, dheads, dgain, dskip,
               grads_out, segcol, uext, segx, slopes, dext, dstate, dkv, dqs, load, *scratch):
    rows = proj.shape[0] // count
    sums = Halving(*scratch)
    take = pltpu.make_async_copy(grads_in, sums.data, load)
    take.start()
    enter_pairs(dp)
    fill_segments(seg, segcol)
    for ref in (dtaps, dheads, dgain, dskip, dstate, dkv):
        ref[...] = jnp.zeros_like(ref)
    dext[0:8, :] = jnp.zeros((8, 768), f32)

    def chunk(turn, _):
        def begin():
            @pl.when(turn == 0)
            def _():
                take.wait()
                if sums.bits:
                    sums.start(0)

        mixer_bwd_chunk(count - 1 - turn, rows, proj, step, seg, segcol, (t0, t1, t2), bias,
                        rate, skip, gain, uext, segx, slopes, dext, dstate, dkv, dqs, mix, ssd_in,
                        states_in, lse_in, dmix, dproj, dstep, dtaps, dheads, dgain, dskip,
                        begin)
        for stage in range(sums.bits):

            @pl.when(turn == -(-stage * (count - 1) // max(sums.bits - 1, 1)))
            def _(stage=stage):
                sums.finish(stage)
                if stage + 1 < sums.bits:
                    sums.start(stage + 1)

        return 0

    lax.fori_loop(0, count, chunk, 0)
    grads_out[...] = sums.data[sums.me]
    sums.leave()
    dskip8 = head_sum(jnp.broadcast_to(dskip[...], (8, 512)))
    dskip[0:1, 0:8] = dskip8[0:1, :]


def mixer_bwd(count, proj, step, seg, taps, bias, rate, skip, gain, mix, ssd, states, lse, dmix, grads):
    length = proj.shape[0]
    rows = length // count
    dp, block, columns = grads.shape
    return pl.pallas_call(
        functools.partial(bwd_kernel, count, dp),
        out_shape=(
            jax.ShapeDtypeStruct((length, 2048), bf16),
            jax.ShapeDtypeStruct((length, 8), bf16),
            jax.ShapeDtypeStruct((4, 768), f32),
            jax.ShapeDtypeStruct((2, 8), f32),
            jax.ShapeDtypeStruct((1, 512), f32),
            jax.ShapeDtypeStruct((1, 512), f32),
            jax.ShapeDtypeStruct((block, columns), bf16),
        ),
        in_specs=[pl.BlockSpec(memory_space=pltpu.VMEM)] * 15
        + [pl.BlockSpec(memory_space=pl.ANY)],
        scratch_shapes=[
            pltpu.VMEM((length + 16, 128), f32),
            pltpu.VMEM((rows + 8, 768), f32),
            pltpu.VMEM((rows + 16, 128), f32),
            pltpu.VMEM((rows, 768), f32),
            pltpu.VMEM((rows + 8, 768), f32),
            pltpu.VMEM((NST, 512), f32),
            pltpu.VMEM((length, 512), f32),
            pltpu.VMEM((256, rows), f32),
            pltpu.SemaphoreType.DMA,
        ]
        + Halving.scratch(dp, block, columns),
        compiler_params=pltpu.CompilerParams(
            collective_id=5, has_side_effects=True, vmem_limit_bytes=60 * 2**20
        ),
    )(proj, step, seg, *taps, bias, rate, skip, gain, mix, ssd, states, lse, dmix, grads)


MESH = pl.DeviceIdType.MESH


class Line:
    def __init__(self, scratch, size, hop=1):
        self.hop = hop
        (self.own, self.left, self.right, self.full, self.acc,
         self.ss, self.sr, self.gs, self.gr) = scratch
        self.size = size
        self.steps = self.own.shape[1]
        self.me = lax.axis_index("tp")
        self.last = size - 1

    @staticmethod
    def scratch(size, steps, sub, width):
        return [
            pltpu.VMEM((size, steps, sub, width), f32),
            pltpu.VMEM((size, steps, sub, width), bf16),
            pltpu.VMEM((size, steps, sub, width), bf16),
            pltpu.VMEM((size, steps, sub, width), bf16),
            pltpu.VMEM((sub, width), f32),
            pltpu.SemaphoreType.DMA((2, size, steps)),
            pltpu.SemaphoreType.DMA((2, size, steps)),
            pltpu.SemaphoreType.DMA((2, size, steps)),
            pltpu.SemaphoreType.DMA((2, size, steps)),
        ]

    def sum_copy(self, way, d, j):
        buf = self.left if way == 0 else self.right
        return pltpu.make_async_remote_copy(
            src_ref=buf.at[d, j],
            dst_ref=buf.at[d, j],
            send_sem=self.ss.at[way, d, j],
            recv_sem=self.sr.at[way, d, j],
            device_id={"tp": self.me + 1 if way == 0 else self.me - 1},
            device_id_type=MESH,
        )

    def row_copy(self, way, d, j):
        return pltpu.make_async_remote_copy(
            src_ref=self.full.at[d, j],
            dst_ref=self.full.at[d, j],
            send_sem=self.gs.at[way, d, j],
            recv_sem=self.gr.at[way, d, j],
            device_id={"tp": self.me + 1 if way == 0 else self.me - 1},
            device_id_type=MESH,
        )

    def enter(self):
        barrier = pltpu.get_barrier_semaphore()
        me, last = self.me, self.last

        @pl.when(me > 0)
        def _():
            pl.semaphore_signal(barrier, inc=1, device_id={"tp": me - 1}, device_id_type=MESH)

        @pl.when(me < last)
        def _():
            pl.semaphore_signal(barrier, inc=1, device_id={"tp": me + 1}, device_id_type=MESH)

        peers = jnp.where(me > 0, 1, 0) + jnp.where(me < last, 1, 0)
        pl.semaphore_wait(barrier, peers)

    def relay(self, way, j):
        me, last = self.me, self.last
        buf = self.left if way == 0 else self.right
        first_one = me == 0 if way == 0 else me == last

        def one(d, _):
            @pl.when(first_one)
            def _():
                buf[d, j] = self.own[d, j].astype(bf16)

            @pl.when(jnp.logical_not(first_one))
            def _():
                self.sum_copy(way, d, j).wait_recv()
                buf[d, j] = (buf[d, j].astype(f32) + self.own[d, j]).astype(bf16)

            self.sum_copy(way, d, j).start()
            return 0

        if way == 0:
            lax.fori_loop(me + 1, self.size, one, 0)
        else:
            lax.fori_loop(0, me, one, 0)

    def settle(self, j, finish):
        me, last = self.me, self.last
        self.acc[...] = self.own[me, j]

        @pl.when(me > 0)
        def _():
            self.sum_copy(0, me, j).wait_recv()
            self.acc[...] = self.acc[...] + self.left[me, j].astype(f32)

        @pl.when(me < last)
        def _():
            self.sum_copy(1, me, j).wait_recv()
            self.acc[...] = self.acc[...] + self.right[me, j].astype(f32)

        self.full[me, j] = finish(j, self.acc[...])

        @pl.when(me < last)
        def _():
            self.row_copy(0, me, j).start()

        @pl.when(me > 0)
        def _():
            self.row_copy(1, me, j).start()

    def inside(self, j):
        return jnp.logical_and(j >= 0, j < self.steps)

    def pass_on(self, i):
        me, last = self.me, self.last

        def from_left(d, _):
            j = i - self.hop * (jnp.maximum(d, last - d) + me - d)

            @pl.when(self.inside(j))
            def _():
                self.row_copy(0, d, j).wait_recv()

                @pl.when(me < last)
                def _():
                    self.row_copy(0, d, j).start()

            return 0

        def from_right(d, _):
            j = i - self.hop * (jnp.maximum(d, last - d) + d - me)

            @pl.when(self.inside(j))
            def _():
                self.row_copy(1, d, j).wait_recv()

                @pl.when(me > 0)
                def _():
                    self.row_copy(1, d, j).start()

            return 0

        lax.fori_loop(0, me, from_left, 0)
        lax.fori_loop(me + 1, self.size, from_right, 0)

    def move(self, i, finish):
        me, last = self.me, self.last
        right_step = i - self.hop * me
        left_step = i - self.hop * (last - me)
        final_step = i - self.hop * jnp.maximum(me, last - me)

        @pl.when(self.inside(right_step))
        def _():
            self.relay(0, right_step)

        @pl.when(self.inside(left_step))
        def _():
            self.relay(1, left_step)

        @pl.when(self.inside(final_step))
        def _():
            self.settle(final_step, finish)

        self.pass_on(i)

    def ready_step(self, i):
        return i - self.hop * (self.last + jnp.maximum(self.me, self.last - self.me))

    def lag(self):
        return 2 * self.hop * self.last

    def leave(self):
        me, last = self.me, self.last

        def step(j, _):
            def right_sums(d, _):
                self.sum_copy(0, d, j).wait_send()
                return 0

            def left_sums(d, _):
                self.sum_copy(1, d, j).wait_send()
                return 0

            def right_rows(d, _):
                self.row_copy(0, d, j).wait_send()
                return 0

            def left_rows(d, _):
                self.row_copy(1, d, j).wait_send()
                return 0

            lax.fori_loop(me + 1, self.size, right_sums, 0)
            lax.fori_loop(0, me, left_sums, 0)

            @pl.when(me < last)
            def _():
                lax.fori_loop(0, me + 1, right_rows, 0)

            @pl.when(me > 0)
            def _():
                lax.fori_loop(me, self.size, left_rows, 0)

            return 0

        lax.fori_loop(0, self.steps, step, 0)


HOOKS = 4


def fwd_kernel(count, proj, step, seg, t0, t1, t2, bias, rate, skip, gain, rows_in,
               mix_out, ssd_out, states_out, lse_out, rows_out, segcol, uext, segx, state, oacc, stats,
               gathered, ss, sr, load):
    rows = proj.shape[0] // count
    ring = Gather(gathered, ss, sr)
    mine = pltpu.make_async_copy(rows_in, gathered.at[ring.me], load.at[0])
    mine.start()
    ring.enter()
    mine.wait()
    ring.send_own()
    fill_segments(seg, segcol)
    lse_out[...] = jnp.zeros_like(lse_out)
    state[...] = jnp.zeros_like(state)

    hooks = count * (HOOKS + 1)
    assert hooks >= ring.turns

    def chunk(index, _):
        def hook(k):
            turn = index * (HOOKS + 1) + k - (hooks - ring.turns)

            @pl.when(turn >= 0)
            def _():
                ring.move(turn)

        mixer_fwd_chunk(index, rows, proj, step, seg, segcol, (t0, t1, t2), bias, rate, skip,
                        gain, uext, segx, state, oacc, stats, mix_out, ssd_out, states_out,
                        lse_out, hook)
        hook(HOOKS)
        return 0

    lax.fori_loop(0, count, chunk, 0)

    give = pltpu.make_async_copy(gathered, rows_out, load.at[1])
    give.start()
    ring.leave()
    give.wait()


def mixer_fwd(count, proj, step, seg, taps, bias, rate, skip, gain, own_rows):
    length = proj.shape[0]
    rows = length // count
    width = own_rows.shape[2]
    pieces = own_rows.shape[0]
    shape = (count, *own_rows.shape)
    return pl.pallas_call(
        functools.partial(fwd_kernel, count),
        out_shape=(
            jax.ShapeDtypeStruct((length, 768), bf16),
            jax.ShapeDtypeStruct((length, 512), bf16),
            jax.ShapeDtypeStruct((count, NST, 512), bf16),
            jax.ShapeDtypeStruct((8, length), f32),
            jax.ShapeDtypeStruct(shape, bf16),
        ),
        in_specs=[pl.BlockSpec(memory_space=pltpu.VMEM)] * 10
        + [pl.BlockSpec(memory_space=pl.ANY)],
        out_specs=(
            *[pl.BlockSpec(memory_space=pltpu.VMEM)] * 4,
            pl.BlockSpec(memory_space=pl.ANY),
        ),
        scratch_shapes=[
            pltpu.VMEM((length + 16, 128), f32),
            pltpu.VMEM((rows + 8, 768), f32),
            pltpu.VMEM((rows + 16, 128), f32),
            pltpu.VMEM((NST, 512), f32),
            pltpu.VMEM((256, rows), f32),
            pltpu.VMEM((8, rows), f32),
            pltpu.VMEM(shape, bf16),
            pltpu.SemaphoreType.DMA((2, count, pieces)),
            pltpu.SemaphoreType.DMA((2, count, pieces)),
            pltpu.SemaphoreType.DMA((2,)),
        ],
        compiler_params=pltpu.CompilerParams(
            collective_id=4, has_side_effects=True, vmem_limit_bytes=60 * 2**20
        ),
    )(proj, step, seg, *taps, bias, rate, skip, gain, own_rows)


def enter_pairs(dp):
    barrier = pltpu.get_barrier_semaphore()
    me = lax.axis_index("dp")
    bits = dp.bit_length() - 1
    for b in range(bits):
        flip = (1 - 2 * lax.rem(me // 2**b, 2)) * 2**b
        pl.semaphore_signal(barrier, inc=1, device_id={"dp": me + flip}, device_id_type=MESH)
    pl.semaphore_wait(barrier, bits)


def flat(v):
    return v.reshape(v.shape[0] * v.shape[1], v.shape[2])


def normed(v, gain):
    return v * lax.rsqrt(jnp.mean(v * v, axis=1, keepdims=True) + eps) * gain


def normed_back(grad, v, gain):
    r = lax.rsqrt(jnp.mean(v * v, axis=1, keepdims=True) + eps)
    a = grad * gain
    back = r * a - (r * r * r) * v * jnp.mean(a * v, axis=1, keepdims=True)
    return back, jnp.sum(grad * v * r, axis=0, keepdims=True)


class Gather:
    def __init__(self, full, ss, sr):
        self.full, self.ss, self.sr = full, ss, sr
        self.size, self.pieces = full.shape[0], full.shape[1]
        self.me = lax.axis_index("tp")
        self.last = self.size - 1
        self.turns = self.pieces + 2 * self.last

    enter = Line.enter

    def copy(self, way, d, j):
        return pltpu.make_async_remote_copy(
            src_ref=self.full.at[d, j],
            dst_ref=self.full.at[d, j],
            send_sem=self.ss.at[way, d, j],
            recv_sem=self.sr.at[way, d, j],
            device_id={"tp": self.me + 1 if way == 0 else self.me - 1},
            device_id_type=MESH,
        )

    def sends(self, way):
        return self.me < self.last if way == 0 else self.me > 0

    def send_own(self):
        def piece(j, _):
            for way in range(2):

                @pl.when(self.sends(way))
                def _(way=way):
                    self.copy(way, self.me, j).start()

            return 0

        lax.fori_loop(0, self.pieces, piece, 0)

    def arrived(self, way, d, j):
        @pl.when(jnp.logical_and(j >= 0, j < self.pieces))
        def _():
            self.copy(way, d, j).wait_recv()

            @pl.when(self.sends(way))
            def _():
                self.copy(way, d, j).start()

    def move(self, turn):
        def from_left(d, _):
            self.arrived(0, d, turn - 2 * (self.me - d) + 1)
            return 0

        def from_right(d, _):
            self.arrived(1, d, turn - 2 * (d - self.me) + 1)
            return 0

        lax.fori_loop(0, self.me, from_left, 0)
        lax.fori_loop(self.me + 1, self.size, from_right, 0)

    def leave(self):
        def piece(j, _):
            def right(d, _):
                self.copy(0, d, j).wait_send()
                return 0

            def left(d, _):
                self.copy(1, d, j).wait_send()
                return 0

            @pl.when(self.me < self.last)
            def _():
                lax.fori_loop(0, self.me + 1, right, 0)

            @pl.when(self.me > 0)
            def _():
                lax.fori_loop(self.me, self.size, left, 0)

            return 0

        lax.fori_loop(0, self.pieces, piece, 0)


class Fetch:
    def __init__(self, sources, places, sems, first=0):
        self.copies = [
            pltpu.make_async_copy(source, place, sems.at[first + n])
            for n, (source, place) in enumerate(zip(sources, places))
        ]

    def start(self):
        for copy in self.copies:
            copy.start()

    def wait(self):
        for copy in self.copies:
            copy.wait()


def embed_kernel(size, patches, embed, keep_rows, gain, *refs):
    weights_in, ws = refs[0:7], refs[7]
    resid_out, full_out, proj_out, step_out = refs[8:12]
    wz, wx, wb, wc, wq, wk, wv = weights = refs[12:19]
    fetch = Fetch(weights_in, weights, refs[19])
    line = Line(refs[20:], size)
    steps, sub = line.steps, line.own.shape[2]
    columns = []
    for ref in (wz, wx, wb, wc, wq, wk, wv):
        columns.append((ref, sum(c[0].shape[1] for c in columns)))

    def produce(j):
        line.own[:, j] = mm(flat(patches[:, j]), embed[...]).reshape(size, sub, line.own.shape[3])

    def finish(j, total):
        rows = total * keep_rows[j]
        resid_out[j] = rows
        return normed(rows, gain[...]).astype(bf16)

    def consume(j):
        x = line.full[:, j]
        full_out[:, j] = x
        x = flat(x)
        for ref, start in columns:
            width = ref.shape[1]
            proj_out[:, j, :, start : start + width] = (
                mm(x, ref[...]).astype(bf16).reshape(size, sub, width)
            )
        step_out[:, j] = mm(x, ws[...], NT).reshape(size, sub, ws.shape[0])

    fetch.start()
    line.enter()
    produce(0)

    def iteration(i, _):
        line.move(i, finish)

        @pl.when(i + 1 < steps)
        def _():
            produce(i + 1)

        ready = line.ready_step(i)

        @pl.when(ready == 0)
        def _():
            fetch.wait()

        @pl.when(line.inside(ready))
        def _():
            consume(ready)

        return 0

    lax.fori_loop(0, steps + line.lag(), iteration, 0)
    line.leave()


def ffn_kernel(size, mix, wmo, wao, resid_one, gain, wg_in, wu_in, wd_in, og_in, og_mine,
               resid_grad, ffn_out, resid_out, dmix, grads_out, gain_grad, hidden_all, gg_all, ug_all,
               wg, wu, wd, og_full, grads, load, *scratch):
    fetch = Fetch((wg_in, wu_in, wd_in, og_in), (wg, wu, wd, og_full), load)
    half = len(scratch) // 2
    one, two = Line(scratch[:half], size), Line(scratch[half:], size)
    steps, sub, width = one.steps, one.own.shape[2], one.own.shape[3]
    length = size * steps * sub
    inner, mixed, units = wmo.shape[0], mix.shape[3], wg.shape[1]
    group = 256
    groups = width // group

    def shaped(v):
        return v.reshape(size, sub, v.shape[1])

    def all_rows(v):
        return v.reshape(length, v.shape[3])

    def produce(j):
        x = flat(mix[:, j])
        one.own[:, j] = shaped(mm(x[:, 0:inner], wmo[...]) + mm(x[:, inner:], wao[...]))

    def finish_one(j, total):
        rows = resid_one[j] + total
        resid_out[j] = rows
        return normed(rows, gain[...]).astype(bf16)

    def middle(j):
        x = flat(one.full[:, j])
        og = flat(og_full[:, j])
        gate, up = mm(x, wg[...]), mm(x, wu[...])
        hg = mm(og, wd[...], NT)
        sig = jax.nn.sigmoid(gate)
        act = gate * sig
        hidden = (act * up).astype(bf16)
        gg = (hg * up * (sig * (1.0 + gate * (1.0 - sig)))).astype(bf16)
        ug = (hg * act).astype(bf16)
        hidden_all[:, j] = shaped(hidden)
        gg_all[:, j] = shaped(gg)
        ug_all[:, j] = shaped(ug)
        two.own[:, j] = shaped(mm(gg, wg[...], NT) + mm(ug, wu[...], NT))
        ffn_out[:, j] = shaped(mm(hidden, wd[...]).astype(bf16))

    def finish_two(j, total):
        back, part = normed_back(total, resid_out[j], gain[...])
        rows = og_mine[j].astype(f32) + back
        resid_grad[j] = rows
        gain_grad[...] = gain_grad[...] + part
        return rows.astype(bf16)

    def consume(j):
        x = flat(two.full[:, j])
        dmix[:, j, :, 0:inner] = shaped(mm(x, wmo[...], NT).astype(bf16))
        dmix[:, j, :, inner:] = shaped(mm(x, wao[...], NT).astype(bf16))

    def columns(ref, g):
        return all_rows(ref[:, :, :, pl.ds(pl.multiple_of(g * group, group), group)])

    def ffn_grads(g):
        here = pl.ds(pl.multiple_of(g * group, group), group)
        x = columns(one.full, g)
        grads[here, 0:units] = mm(x, all_rows(gg_all[...]), TN).astype(bf16)
        grads[here, units : 2 * units] = mm(x, all_rows(ug_all[...]), TN).astype(bf16)
        total = mm(columns(og_full, g), all_rows(hidden_all[...]), TN)
        grads[here, 2 * units : 3 * units] = total.astype(bf16)
        give(g).start()

    def give(g):
        here = pl.ds(pl.multiple_of(g * group, group), group)
        return pltpu.make_async_copy(
            grads.at[here, 0 : 3 * units], grads_out.at[here, 0 : 3 * units], load.at[4 + g]
        )

    def given(g, _):
        give(g).wait()
        return 0

    def mix_grads(g, _):
        here = pl.ds(pl.multiple_of(g * group, group), group)
        grads[here, 3 * units :] = mm(
            columns(two.full, g), all_rows(mix[...]), TN
        ).astype(bf16)
        return 0

    fetch.start()
    one.enter()
    gain_grad[...] = jnp.zeros_like(gain_grad)
    produce(0)
    lag = one.lag() + 1

    def iteration(i, _):
        one.move(i, finish_one)
        two.move(i - lag, finish_two)

        @pl.when(i + 1 < steps)
        def _():
            produce(i + 1)

        ready_one = one.ready_step(i)

        @pl.when(ready_one == 0)
        def _():
            fetch.wait()

        @pl.when(one.inside(ready_one))
        def _():
            middle(ready_one)

        ready_two = two.ready_step(i - lag)

        @pl.when(two.inside(ready_two))
        def _():
            consume(ready_two)

        turn = i - (steps + lag)

        @pl.when(jnp.logical_and(turn >= 0, turn < groups))
        def _():
            ffn_grads(turn)

        return 0

    lax.fori_loop(0, steps + lag + two.lag(), iteration, 0)
    lax.fori_loop(0, groups, mix_grads, 0)
    last = pltpu.make_async_copy(
        grads.at[:, 3 * units :], grads_out.at[:, 3 * units :], load.at[4 + groups]
    )
    last.start()
    lax.fori_loop(0, groups, given, 0)
    last.wait()
    one.leave()
    two.leave()


def comm_call(body, out_shape, scratch, identity, *args, kept=(), given=()):
    return pl.pallas_call(
        body,
        out_shape=out_shape,
        in_specs=[
            pl.BlockSpec(memory_space=pl.ANY if place in kept else pltpu.VMEM)
            for place in range(len(args))
        ],
        out_specs=tuple(
            pl.BlockSpec(memory_space=pl.ANY if place in given else pltpu.VMEM)
            for place in range(len(out_shape))
        ),
        scratch_shapes=scratch,
        compiler_params=pltpu.CompilerParams(
            collective_id=identity, has_side_effects=True, vmem_limit_bytes=62 * 2**20
        ),
    )(*args)


def sds(shape, kind):
    return jax.ShapeDtypeStruct(shape, kind)


class Halving:
    def __init__(self, data, got, ss, sr):
        self.data, self.got, self.ss, self.sr = data, got, ss, sr
        self.count, self.rows = data.shape[0], data.shape[1]
        self.bits = self.count.bit_length() - 1
        self.me = lax.axis_index("dp")
        plain = list(range(self.bits))
        other = plain if self.bits < 3 else [0, 2, 1] + plain[3:]
        self.orders = (plain, other)

    @staticmethod
    def scratch(count, rows, columns):
        spare = max(count - 1, 1)
        return [
            pltpu.VMEM((count, rows, columns), bf16),
            pltpu.VMEM((spare, rows, columns), bf16),
            pltpu.SemaphoreType.DMA((2, spare)),
            pltpu.SemaphoreType.DMA((2, spare)),
        ]

    def bit(self, b):
        return lax.rem(self.me // 2**b, 2)

    def block(self, half, stage, e, theirs):
        order = self.orders[half]
        place = 0
        for b in order[:stage]:
            place = place + self.bit(b) * 2**b
        b = order[stage]
        place = place + (1 - self.bit(b) if theirs else self.bit(b)) * 2**b
        for t, b in enumerate(sorted(order[stage + 1 :])):
            place = place + lax.rem(e // 2**t, 2) * 2**b
        return place

    def open(self, stage):
        return 2 ** (self.bits - 1 - stage)

    def slot(self, stage, e):
        return sum(self.open(s) for s in range(stage)) + e

    def part(self, half):
        rows = self.rows // 2
        return pl.ds(half * rows, rows)

    def copy(self, half, stage, e):
        b = self.orders[half][stage]
        slot = self.slot(stage, e)
        return pltpu.make_async_remote_copy(
            src_ref=self.data.at[self.block(half, stage, e, True), self.part(half)],
            dst_ref=self.got.at[slot, self.part(half)],
            send_sem=self.ss.at[half, slot],
            recv_sem=self.sr.at[half, slot],
            device_id={"dp": self.me + (1 - 2 * self.bit(b)) * 2**b},
            device_id_type=MESH,
        )

    def start(self, stage, low=0, high=None):
        def one(e, _):
            self.copy(0, stage, e).start()
            self.copy(1, stage, e).start()
            return 0

        lax.fori_loop(low, self.open(stage) if high is None else high, one, 0)

    def take(self, half, stage, e):
        self.copy(half, stage, e).wait_recv()
        place, part = self.block(half, stage, e, False), self.part(half)
        got = self.got[self.slot(stage, e), part]
        self.data[place, part] = self.data[place, part] + got

    def finish(self, stage):
        def one(e, _):
            for half in range(2):
                self.copy(half, stage, e).wait_recv()
                place, part = self.block(half, stage, e, False), self.part(half)
                got = self.got[self.slot(stage, e), part]
                self.data[place, part] = self.data[place, part] + got
            return 0

        lax.fori_loop(0, self.open(stage), one, 0)

    def leave(self):
        for stage in range(self.bits):

            def one(e, _, stage=stage):
                self.copy(0, stage, e).wait_send()
                self.copy(1, stage, e).wait_send()
                return 0

            lax.fori_loop(0, self.open(stage), one, 0)


class Doubling:
    def __init__(self, parts, got, ss, sr, dp, tp):
        self.parts, self.got, self.ss, self.sr = parts, got, ss, sr
        self.hops = [("dp", b) for b in range(dp.bit_length() - 1)]
        self.hops += [("tp", b) for b in range(tp.bit_length() - 1)]

    @staticmethod
    def scratch(dp, tp, rows, columns):
        hops = dp.bit_length() + tp.bit_length() - 2
        return [
            pltpu.VMEM((hops + 1, rows, columns), f32),
            pltpu.VMEM((hops, rows, columns), f32),
            pltpu.SemaphoreType.DMA((hops,)),
            pltpu.SemaphoreType.DMA((hops,)),
        ]

    def copy(self, hop):
        axis, b = self.hops[hop]
        me = lax.axis_index(axis)
        flip = (1 - 2 * lax.rem(me // 2**b, 2)) * 2**b
        return pltpu.make_async_remote_copy(
            src_ref=self.parts.at[hop],
            dst_ref=self.got.at[hop],
            send_sem=self.ss.at[hop],
            recv_sem=self.sr.at[hop],
            device_id={axis: me + flip},
            device_id_type=MESH,
        )

    def start(self, hop):
        self.copy(hop).start()

    def finish(self, hop):
        self.copy(hop).wait_recv()
        self.parts[hop + 1] = self.parts[hop] + self.got[hop]

    def leave(self):
        for hop in range(len(self.hops)):
            self.copy(hop).wait_send()


def enter_both(dp, tp):
    barrier = pltpu.get_barrier_semaphore()
    me_t, me_d = lax.axis_index("tp"), lax.axis_index("dp")
    for away in range(1, tp):
        pl.semaphore_signal(
            barrier, inc=1, device_id={"tp": lax.rem(me_t + away, tp)}, device_id_type=MESH
        )
    bits = dp.bit_length() - 1
    for b in range(bits):
        flip = (1 - 2 * lax.rem(me_d // 2**b, 2)) * 2**b
        pl.semaphore_signal(barrier, inc=1, device_id={"dp": me_d + flip}, device_id_type=MESH)
    pl.semaphore_wait(barrier, tp - 1 + bits)


def entry_kernel(size, dp, dproj, dstep, wz, wx, wb, wc, wq, wk, wv, ws, resid_one, gain, resid_grad,
                 keep_rows, embed_in, full_in, patches_in, dtaps, dheads, dgain, dskip, two_gain_grad,
                 patch_out, embed_out, in_out, small_out, full_one, embed, patches, patch_grad, load,
                 *scratch):
    fetch = Fetch((full_in, embed_in, patches_in), (full_one, embed, patches), load)
    line = Line(scratch[0:9], size)
    ins = Halving(*scratch[9:13])
    emb = Halving(*scratch[13:17])
    small = Doubling(*scratch[17:21], dp, size)
    steps, sub, width = line.steps, line.own.shape[2], line.own.shape[3]
    length = size * steps * sub
    weights = (wz, wx, wb, wc, wq, wk, wv)
    columns = []
    for ref in weights:
        columns.append((ref, sum(c[0].shape[1] for c in columns)))
    group = 256
    groups = width // group
    in_group = group // ins.rows

    def all_rows(v):
        return v.reshape(length, v.shape[3])

    def produce(j):
        total = mm(flat(dstep[:, j]), ws[...])
        for ref, start in columns:
            total = total + mm(flat(dproj[:, j, :, start : start + ref.shape[1]]), ref[...], NT)
        line.own[:, j] = total.reshape(size, sub, width)

    def finish(j, total):
        back, part = normed_back(total, resid_one[j], gain[...])
        small.parts[0, 9:10] = small.parts[0, 9:10] + part
        return ((resid_grad[j] + back) * keep_rows[j]).astype(bf16)

    def consume(d, _):
        x = flat(line.full[d])
        patch_grad[d] = mm(x, embed[...], NT).astype(bf16).reshape(steps, sub, embed.shape[0])
        give(d).start()
        return 0

    def give(d):
        return pltpu.make_async_copy(patch_grad.at[d], patch_out.at[d], load.at[3 + d])

    def given(d, _):
        give(d).wait()
        return 0

    def weight_group(g):
        x = full_one[:, pl.ds(pl.multiple_of(g * group, group), group)]
        here = pl.ds(g * in_group, in_group)
        grad = mm(x, all_rows(dproj[...]), TN).astype(bf16)
        ins.data[here, :, 0:PROJ] = grad.reshape(in_group, ins.rows, PROJ)
        grad = mm(x, all_rows(dstep[...]), TN).astype(bf16)
        grad = jnp.concatenate([grad, jnp.zeros((group, 120), bf16)], axis=1)
        ins.data[here, :, PROJ:] = grad.reshape(in_group, ins.rows, 128)
        if ins.bits:
            ins.start(0, g * in_group // 2, (g + 1) * in_group // 2)

    def embed_group(g):
        x = all_rows(line.full[:, :, :, pl.ds(pl.multiple_of(g * group, group), group)])
        grad = mm(x, all_rows(patches[...]), TN).astype(bf16)
        emb.data[pl.ds(g * in_group, in_group)] = grad.reshape(
            in_group, emb.rows, grad.shape[1]
        )
        if emb.bits:
            emb.start(0, g * in_group // 2, (g + 1) * in_group // 2)

    fetch.start()
    enter_both(dp, size)
    first = jnp.zeros((16, width), f32)
    small.parts[0] = first
    small.parts[0, 0:4, 0:768] = dtaps[...]
    small.parts[0, 4:5, 0:512] = dgain[...]
    small.parts[0, 5:6, 0:512] = dskip[...]
    small.parts[0, 6:8, 0:8] = dheads[...]
    small.parts[0, 8:9] = two_gain_grad[...]
    produce(0)
    fetch.copies[0].wait()

    def iteration(i, _):
        line.move(i, finish)

        @pl.when(i + 1 < steps)
        def _():
            produce(i + 1)

        @pl.when(i < groups)
        def _():
            weight_group(i)

        for stage in range(ins.bits):

            @pl.when(i == groups + (8 * stage) // max(ins.bits - 1, 1))
            def _(stage=stage):
                ins.finish(stage)
                if stage + 1 < ins.bits:
                    ins.start(stage + 1)

        return 0

    lax.fori_loop(0, steps + line.lag(), iteration, 0)
    small.start(0)
    fetch.copies[1].wait()
    fetch.copies[2].wait()

    in_out[...] = ins.data[ins.me]
    hops = len(small.hops)

    def small_turn(turn):
        if turn < hops:
            small.finish(turn)
            if turn + 1 < hops:
                small.start(turn + 1)

    if emb.bits == 3:
        mid, top = emb.bit(1), emb.bit(2)
        far_mid, far_top = 1 - mid, 1 - top

        def each_turn(t, _):
            g_mid = mid + (1 - t // 2) * (far_mid - mid)
            g_top = top + (1 - lax.rem(t, 2)) * (far_top - top)
            embed_group(g_mid + 2 * g_top)

            @pl.when(t == 1)
            def _():
                for half in range(2):
                    emb.take(half, 0, far_mid + 2 * far_top)
                emb.copy(0, 1, far_top).start()
                emb.copy(1, 1, far_mid).start()

            @pl.when(t == 2)
            def _():
                for half in range(2):
                    emb.take(half, 0, far_mid + 2 * top)
                emb.copy(0, 1, top).start()

            @pl.when(t == 3)
            def _():
                for half in range(2):
                    emb.take(half, 0, mid + 2 * far_top)
                emb.copy(1, 1, mid).start()

            return 0

        lax.fori_loop(0, groups, each_turn, 0)
        small_turn(0)
        for half in range(2):
            emb.take(half, 0, mid + 2 * top)
        lax.fori_loop(0, size // 2, consume, 0)
        small_turn(1)
        emb.take(0, 1, far_top)
        emb.copy(0, 2, 0).start()
        emb.take(1, 1, far_mid)
        emb.copy(1, 2, 0).start()
        lax.fori_loop(size // 2, size, consume, 0)
        small_turn(2)
        emb.take(0, 1, top)
        emb.take(1, 1, mid)
        small_turn(3)
        emb.take(0, 2, 0)
        emb.take(1, 2, 0)
        for turn in range(4, hops):
            small_turn(turn)
    else:

        def each_group(g, _):
            embed_group(g)
            return 0

        lax.fori_loop(0, groups, each_group, 0)
        lax.fori_loop(0, size, consume, 0)
        for turn in range(max(hops, emb.bits)):
            small_turn(turn)
            if turn < emb.bits:
                emb.finish(turn)
                if turn + 1 < emb.bits:
                    emb.start(turn + 1)
    small_out[0:8] = small.parts[dp.bit_length() - 1, 0:8]
    small_out[8:16] = small.parts[hops, 8:16]
    embed_out[...] = emb.data[emb.me]
    lax.fori_loop(0, size, given, 0)
    line.leave()
    ins.leave()
    emb.leave()
    small.leave()


def last_kernel(patch_in, embed_in, ins, mids, small, resid, ffn, place, patch_out, result,
                embed_out, gz, gx, gb, gc, gq, gk, gv, gs, t0, t1, t2, hb, hr, hs, inner_gain,
                gmo, gao, ggate, gup, gdown, gain_one, gain_two, held, sem):
    rows = patch_in.shape[0] // 4
    pieces = [pl.ds(n * rows, rows) for n in range(4)]
    takes = [pltpu.make_async_copy(patch_in.at[p], held.at[p], sem.at[n]) for n, p in enumerate(pieces)]
    gives = [pltpu.make_async_copy(held.at[p], patch_out.at[p], sem.at[4 + n]) for n, p in enumerate(pieces)]
    for take in takes:
        take.start()
    result[...] = (resid[...] + ffn[...].astype(f32)).astype(bf16)
    start = 0
    for out in (gz, gx, gb, gc, gq, gk, gv):
        out[...] = ins[:, start : start + out.shape[1]].astype(f32)
        start = start + out.shape[1]
    steps_part = ins[:, start:].astype(f32)
    gs[...] = steps_part.T[0 : gs.shape[0], :] if gs.shape[1] % 128 == 0 else steps_part[:, 0 : gs.shape[1]]
    units, inner = ggate.shape[1], t0.shape[1]
    ggate[...] = mids[:, 0:units].astype(f32)
    gup[...] = mids[:, units : 2 * units].astype(f32)
    for take, give in zip(takes, gives):
        take.wait()
        give.start()
    flipped = mids[:, 2 * units :].astype(f32)
    outs = ((gdown, flipped[:, 0:units]), (gmo, flipped[:, units : units + inner]),
            (gao, flipped[:, units + inner :]), (embed_out, embed_in[...].astype(f32)))
    for out, value in outs:
        out[...] = value.T if out.shape != value.shape else value
    t0[...] = small[0:4, 0 : t0.shape[1]]
    t1[...] = small[0:4, t0.shape[1] : t0.shape[1] + t1.shape[1]]
    t2[...] = small[0:4, t0.shape[1] + t1.shape[1] : t0.shape[1] + 2 * t1.shape[1]]
    hb[...] = small[6:7, 0 : hb.shape[1]]
    hr[...] = small[7:8, 0 : hr.shape[1]]
    hs[...] = small[5:6, 0 : hs.shape[1]]
    inner_gain[...] = small[4:5, 0 : inner_gain.shape[1]]
    width, share = small.shape[1], gain_one.shape[1]
    chosen = (iota((width, share), 0) == iota((width, share), 1) + place[0] * share).astype(bf16)
    gains = sum(mm(term, chosen) for term in parts_of(small[8:16, :], 3))
    gain_two[...] = gains[0:1, :]
    gain_one[...] = gains[1:2, :]
    for give in gives:
        give.wait()


def shards(
    patches,
    keep_mask,
    segments,
    embed_weight,
    first_gain,
    mamba_gate,
    mamba_input,
    state_in,
    state_out,
    step_weight,
    conv_input,
    conv_statein,
    conv_stateout,
    step_bias,
    rate_log,
    skip_gain,
    inner_gain,
    mamba_output,
    query_weight,
    key_weight,
    value_weight,
    attn_output,
    second_gain,
    ffn_gate,
    ffn_up,
    ffn_down,
    out_grad,
):
    size = lax.axis_size("tp")
    segment = segments[0]
    length = patches.shape[0]
    mine = length // size
    sub = mine // STEPS
    shape = (size, STEPS, sub)
    width = embed_weight.shape[1]
    keep_rows = keep_mask.astype(f32).reshape(STEPS, sub, 1)
    seg_row = segment.astype(f32)[None]
    taps = (conv_input, conv_statein, conv_stateout)
    core_params = (step_bias[None], rate_log[None], skip_gain[None], inner_gain[None])
    in_list = (
        mamba_gate,
        mamba_input,
        state_in,
        state_out,
        query_weight,
        key_weight,
        value_weight,
        step_weight.T,
    )
    one_gain, two_gain = first_gain[None], second_gain[None]
    buffers = Line.scratch(size, STEPS, sub, width)
    resid_one, full_one, projected, step_raw = comm_call(
        functools.partial(embed_kernel, size),
        (
            sds((STEPS, sub, width), f32),
            sds((*shape, width), bf16),
            sds((*shape, PROJ), bf16),
            sds((*shape, step_weight.shape[1]), f32),
        ),
        [pltpu.VMEM(member.shape, bf16) for member in in_list[:7]]
        + [pltpu.SemaphoreType.DMA((7,))]
        + buffers,
        1,
        patches.reshape(*shape, patches.shape[1]),
        embed_weight,
        keep_rows,
        one_gain,
        *in_list,
        kept=(4, 5, 6, 7, 8, 9, 10),
    )
    projected = projected.reshape(length, PROJ)
    step_raw = step_raw.reshape(length, step_weight.shape[1])
    own_grad = out_grad.reshape(STEPS, sub, width)
    mix_in, ssd, states, lse, og_full = mixer_fwd(
        size, projected, step_raw, seg_row, taps, *core_params, own_grad
    )
    inner_width = mamba_output.shape[0]
    hidden_width = ffn_gate.shape[1]
    rows16 = sds((*shape, width), bf16)
    rows32 = sds((STEPS, sub, width), f32)
    mixed = mix_in.shape[1]
    resid_grad, ffn_part, resid_two, dmix, grads, second_gain_grad = comm_call(
        functools.partial(ffn_kernel, size),
        (
            rows32, rows16, rows32, sds((*shape, mixed), bf16),
            sds((width, 3 * hidden_width + mixed), bf16), sds((1, width), f32),
        ),
        [pltpu.VMEM((*shape, hidden_width), bf16)] * 3
        + [
            pltpu.VMEM(ffn_gate.shape, bf16),
            pltpu.VMEM(ffn_up.shape, bf16),
            pltpu.VMEM(ffn_down.shape, bf16),
            pltpu.VMEM((*shape, width), bf16),
            pltpu.VMEM((width, 3 * hidden_width + mixed), bf16),
            pltpu.SemaphoreType.DMA((5 + width // 256,)),
        ]
        + buffers
        + buffers,
        2,
        mix_in.reshape(*shape, mixed),
        mamba_output,
        attn_output,
        resid_one,
        two_gain,
        ffn_gate,
        ffn_up,
        ffn_down,
        og_full,
        own_grad,
        kept=(5, 6, 7, 8),
        given=(4,),
    )
    ffn_sum = lax.psum_scatter(
        ffn_part.reshape(length, width), "tp", scatter_dimension=0, tiled=True
    )
    blocks = lax.axis_size("dp")
    grads = grads.reshape(blocks, width // blocks, grads.shape[1])
    proj_grad, step_grad, dtaps, dheads, dgain, dskip, mid_sum = mixer_bwd(
        size, projected, step_raw, seg_row, taps, *core_params, mix_in, ssd, states, lse,
        dmix.reshape(length, mixed),
        grads,
    )
    dp = lax.axis_size("dp")
    block = width // dp
    features = patches.shape[1]
    patches_grad, embed_sum, in_sum, small = comm_call(
        functools.partial(entry_kernel, size, dp),
        (
            sds((*shape, features), bf16),
            sds((block, features), bf16),
            sds((block, PROJ + 128), bf16),
            sds((16, width), f32),
        ),
        [
            pltpu.VMEM((length, width), bf16),
            pltpu.VMEM(embed_weight.shape, bf16),
            pltpu.VMEM((*shape, features), bf16),
            pltpu.VMEM((*shape, features), bf16),
            pltpu.SemaphoreType.DMA((3 + size,)),
        ]
        + buffers
        + Halving.scratch(dp, block, PROJ + 128)
        + Halving.scratch(dp, block, features)
        + Doubling.scratch(dp, size, 16, width),
        3,
        proj_grad.reshape(*shape, PROJ),
        step_grad.reshape(*shape, step_grad.shape[1]),
        *in_list,
        resid_one,
        one_gain,
        resid_grad,
        keep_rows,
        embed_weight,
        full_one.reshape(length, width),
        patches.reshape(*shape, features),
        dtaps,
        dheads,
        dgain,
        dskip,
        second_gain_grad,
        kept=(14, 15, 16),
        given=(0,),
    )
    place = (lax.axis_index("dp") * size + lax.axis_index("tp"))[None]
    flip = block % 128 == 0

    def turned(rows):
        return sds((rows, block) if flip else (block, rows), f32)

    outs = pl.pallas_call(
        last_kernel,
        out_shape=(
            sds((length, features), bf16),
            sds((mine, width), bf16),
            turned(features),
            *[sds((block, member.shape[1]), f32) for member in in_list[:7]],
            turned(step_weight.shape[1]),
            *[sds(member.shape, f32) for member in taps],
            *[sds((1, step_bias.shape[0]), f32)] * 3,
            sds((1, inner_width), f32),
            turned(inner_width),
            turned(attn_output.shape[0]),
            sds((block, hidden_width), f32),
            sds((block, hidden_width), f32),
            turned(hidden_width),
            sds((1, block // size), f32),
            sds((1, block // size), f32),
        ),
        in_specs=[pl.BlockSpec(memory_space=pl.ANY)]
        + [pl.BlockSpec(memory_space=pltpu.VMEM)] * 6
        + [pl.BlockSpec(memory_space=pltpu.SMEM)],
        out_specs=(
            pl.BlockSpec(memory_space=pl.ANY),
            *[pl.BlockSpec(memory_space=pltpu.VMEM)] * 24,
        ),
        scratch_shapes=[pltpu.VMEM((length, features), bf16), pltpu.SemaphoreType.DMA((8,))],
        compiler_params=pltpu.CompilerParams(vmem_limit_bytes=60 * 2**20),
    )(
        patches_grad.reshape(length, features),
        embed_sum,
        in_sum,
        mid_sum,
        small,
        resid_two.reshape(mine, width),
        ffn_sum,
        place,
    )
    (
        patches_grad, result, embed_cols, gz, gx, gb, gc, gq, gk, gv, gs, t0, t1, t2, hb, hr, hs,
        inner_grad, gmo, gao, ggate, gup, gdown, gain_one, gain_two,
    ) = outs
    if flip:
        gs = gs.T
    else:
        embed_cols, gmo, gao, gdown = embed_cols.T, gmo.T, gao.T, gdown.T
    return (
        result,
        patches_grad,
        embed_cols,
        gain_one[0],
        gz,
        gx,
        gb,
        gc,
        gs,
        t0,
        t1,
        t2,
        hb[0],
        hr[0],
        hs[0],
        inner_grad[0],
        gmo,
        gq,
        gk,
        gv,
        gao,
        gain_two[0],
        ggate,
        gup,
        gdown,
    )


def solution(mesh):
    return jax.shard_map(
        shards,
        mesh=mesh,
        in_specs=(
            P("dp", "tp"),
            P(("dp", "tp")),
            P("dp", None),
            P("tp", None),
            P(),
            P(None, "tp"),
            P(None, "tp"),
            P(None, "tp"),
            P(None, "tp"),
            P(None, "tp"),
            P(None, "tp"),
            P(None, "tp"),
            P(None, "tp"),
            P("tp"),
            P("tp"),
            P("tp"),
            P("tp"),
            P("tp", None),
            P(None, "tp"),
            P(None, "tp"),
            P(None, "tp"),
            P("tp", None),
            P(),
            P(None, "tp"),
            P(None, "tp"),
            P("tp", None),
            P(("dp", "tp"), None),
        ),
        out_specs=(
            P(("dp", "tp"), None),
            P("dp", "tp"),
            P("tp", "dp"),
            P(("dp", "tp")),
            P("dp", "tp"),
            P("dp", "tp"),
            P("dp", "tp"),
            P("dp", "tp"),
            P("dp", "tp"),
            P(None, "tp"),
            P(None, "tp"),
            P(None, "tp"),
            P("tp"),
            P("tp"),
            P("tp"),
            P("tp"),
            P("tp", "dp"),
            P("dp", "tp"),
            P("dp", "tp"),
            P("dp", "tp"),
            P("tp", "dp"),
            P(("dp", "tp")),
            P("dp", "tp"),
            P("dp", "tp"),
            P("tp", "dp"),
        ),
        check_vma=False,
    )
```
